32 devices in a mesh: img: 8 (over y, x, core), ch: 4 (over z).
Axes of the slice: x: 2, y: 2, z: 4, core: 2. Of those that a mesh axis runs over, the one named last changes fastest.
Arguments:
- images: bfloat16 [64, 14, 14, 320], P('img', None, None, 'ch'), may hold values from -16 to 16
- conv_kernel: bfloat16 [2, 3, 3, 320], P(None, None, None, 'ch'), may hold values from -2 to 2
- bn_gain: bfloat16 [2, 320], P(None, 'ch'), may hold values from 0.5 to 1.5
- bn_bias: bfloat16 [2, 320], P(None, 'ch'), may hold values from -3 to 3
- mix_rows: bfloat16 [2, 14, 14], replicated, may hold values from -1.5 to 1.5
- mix_rows_bias: bfloat16 [2, 14], replicated, may hold values from -3 to 3
- mix_cols: bfloat16 [2, 14, 14], replicated, may hold values from -1.5 to 1.5
- mix_cols_bias: bfloat16 [2, 14], replicated, may hold values from -3 to 3
- join_weight: bfloat16 [2, 3, 320, 320], P(None, None, 'ch'), may hold values from -0.1875 to 0.1875
- join_bias: bfloat16 [2, 320], P(None, 'ch'), may hold values from -3 to 3
- norm_gain: bfloat16 [2, 320], P(None, 'ch'), may hold values from 0.5 to 1.5
- norm_bias: bfloat16 [2, 320], P(None, 'ch'), may hold values from -3 to 3
- weight_in: bfloat16 [2, 320, 1280], P(None, None, 'ch'), may hold values from -0.3125 to 0.3125
- bias_in: bfloat16 [2, 1280], P(None, 'ch'), may hold values from -3 to 3
- weight_out: bfloat16 [2, 1280, 320], P(None, 'ch'), may hold values from -0.15625 to 0.15625
- bias_out: bfloat16 [2, 320], P(None, 'ch'), may hold values from -3 to 3
- running_mean: float32 [2, 320], P(None, 'ch'), may hold values from -1 to 1
- running_var: float32 [2, 320], P(None, 'ch'), may hold values from 0.5 to 2
- cotangent: float32 [64, 14, 14, 320], P('img', None, None, 'ch'), may hold values from -6 to 6
Outputs:
- output: bfloat16 [64, 14, 14, 320], P('img', None, None, 'ch')
- images_grad: float32 [64, 14, 14, 320], P('img', None, None, 'ch')
- conv_kernel_grad: float32 [2, 3, 3, 320], P(None, None, None, 'ch')
- bn_gain_grad: float32 [2, 320], P(None, 'ch')
- bn_bias_grad: float32 [2, 320], P(None, 'ch')
- mix_rows_grad: float32 [2, 14, 14], replicated
- mix_rows_bias_grad: float32 [2, 14], replicated
- mix_cols_grad: float32 [2, 14, 14], replicated
- mix_cols_bias_grad: float32 [2, 14], replicated
- join_weight_grad: float32 [2, 3, 320, 320], P(None, None, 'ch')
- join_bias_grad: float32 [2, 320], P(None, 'ch')
- norm_gain_grad: float32 [2, 320], P(None, 'ch')
- norm_bias_grad: float32 [2, 320], P(None, 'ch')
- weight_in_grad: float32 [2, 320, 1280], P(None, None, 'ch')
- bias_in_grad: float32 [2, 1280], P(None, 'ch')
- weight_out_grad: float32 [2, 1280, 320], P(None, 'ch')
- bias_out_grad: float32 [2, 320], P(None, 'ch')
- running_mean_out: float32 [2, 320], P(None, 'ch')
- running_var_out: float32 [2, 320], P(None, 'ch')
The draws below stay inside these ranges and needn't reach their ends.
All inputs are finite; a program needn't handle non-finite values.
Results may differ from the reference program's by a relative error of at most 0.024.
Values may be sent and summed in bfloat16 or wider, within the bound.
A program may use at most 128 MiB of HBM per device.

```python
import jax
import jax.numpy as jnp
from jax import lax

C = 320
FF = 1280
HW = 14
LAYERS = 2
BATCH = 64


def draw_images(key, part):
    key = jax.random.fold_in(key, 11)
    key_noise, key_rough = jax.random.split(key, 2)
    ramp = jnp.exp(jnp.log(3.0) * jnp.arange(BATCH, dtype=jnp.float32) / max(BATCH - 1, 1))
    rough = jax.random.uniform(key_rough, (BATCH,), minval=0.7, maxval=1.4)
    scale = (ramp * rough)[:, None, None, None]
    noise = jnp.clip(jax.random.normal(key_noise, (BATCH, HW, HW, C)), -4.0, 4.0)
    return (noise * scale / 1.5).astype(jnp.bfloat16)


def levels(key, shape, pieces, least, top_value):
    def one(dim, shards_of):
        steps = jax.random.uniform(jax.random.fold_in(jax.random.fold_in(key, 6), dim), (shards_of,), jnp.float32, least / len(pieces), top_value / len(pieces))
        return jnp.repeat(jnp.exp(steps), shape[dim] // shards_of).reshape((-1,) + (1,) * (len(shape) - dim - 1))

    factor_of = one(*pieces[0])
    for cut in pieces[1:]:
        factor_of = factor_of * one(*cut)
    return factor_of


def scatter_about(own_key, shape, width, most, cuts=(), kind=jnp.bfloat16):
    drawn = width * jax.random.normal(own_key, shape, jnp.float32)
    if cuts:
        drawn = drawn * levels(own_key, shape, cuts, -0.22, 0.18)
    return jnp.clip(drawn, -most, most).astype(kind)


def setup_inputs(seed: int = 0) -> dict:
    key_list = jax.random.split(jax.random.key(seed), 20)
    images = draw_images(jax.random.fold_in(key_list[19], 71), 0)
    conv_kernel = scatter_about(key_list[1], (LAYERS, 3, 3, C), 9 ** -0.5, 2.0, ((3, 4),))
    bn_gain = jnp.clip(1.0 + 0.1 * jax.random.normal(key_list[2], (LAYERS, C), jnp.float32), 0.5, 1.5).astype(jnp.bfloat16)
    bn_bias = scatter_about(key_list[3], (LAYERS, C), 0.5, 3.0, ((1, 4),))
    mix_rows = scatter_about(key_list[4], (LAYERS, HW, HW), HW ** -0.5, 1.5)
    mix_rows_bias = scatter_about(key_list[5], (LAYERS, HW), 0.5, 3.0)
    mix_cols = scatter_about(key_list[6], (LAYERS, HW, HW), HW ** -0.5, 1.5)
    mix_cols_bias = scatter_about(key_list[7], (LAYERS, HW), 0.5, 3.0)
    join_weight = scatter_about(key_list[8], (LAYERS, 3, C, C), (3 * C) ** -0.5, 0.1875, ((2, 4),))
    join_bias = scatter_about(key_list[9], (LAYERS, C), 0.5, 3.0, ((1, 4),))
    norm_gain = jnp.clip(1.0 + 0.1 * jax.random.normal(key_list[10], (LAYERS, C), jnp.float32), 0.5, 1.5).astype(jnp.bfloat16)
    norm_bias = scatter_about(key_list[11], (LAYERS, C), 0.5, 3.0, ((1, 4),))
    weight_in = scatter_about(key_list[12], (LAYERS, C, FF), C ** -0.5, 0.3125, ((2, 4),))
    bias_in = scatter_about(key_list[13], (LAYERS, FF), 0.5, 3.0, ((1, 4),))
    weight_out = scatter_about(key_list[14], (LAYERS, FF, C), FF ** -0.5, 0.15625, ((1, 4),))
    bias_out = scatter_about(key_list[15], (LAYERS, C), 0.5, 3.0, ((1, 4),))
    running_mean = jnp.clip(jax.random.uniform(key_list[16], (LAYERS, C), jnp.float32, -1.0, 1.0) * levels(key_list[16], (LAYERS, C), ((1, 4),), -0.4, 0.0), -1.0, 1.0)
    running_var = jnp.clip(0.5 + 1.5 * jax.random.uniform(key_list[17], (LAYERS, C), jnp.float32) ** levels(key_list[17], (LAYERS, C), ((1, 4),), -0.2, 0.2), 0.5, 2.0)
    cotangent = scatter_about(key_list[18], (BATCH, HW, HW, C), 1.0, 6.0, ((0, 8), (3, 4)), jnp.float32)
    return {"images": images, "conv_kernel": conv_kernel, "bn_gain": bn_gain, "bn_bias": bn_bias, "mix_rows": mix_rows, "mix_rows_bias": mix_rows_bias, "mix_cols": mix_cols, "mix_cols_bias": mix_cols_bias, "join_weight": join_weight, "join_bias": join_bias, "norm_gain": norm_gain, "norm_bias": norm_bias, "weight_in": weight_in, "bias_in": bias_in, "weight_out": weight_out, "bias_out": bias_out, "running_mean": running_mean, "running_var": running_var, "cotangent": cotangent}


@jax.custom_vjp
def low(v):
    return lax.optimization_barrier(v.astype(jnp.bfloat16)).astype(jnp.float32)

@jax.custom_vjp
def low_back(v):
    return v

def low_keep(v):
    return (low(v), None)

def low_pass(kept, grad):
    return (grad,)

def back_keep(v):
    return (v, None)

def back_low(kept, grad):
    return (low(grad),)
low.defvjp(low_keep, low_pass)
low_back.defvjp(back_keep, back_low)
highest = lax.Precision.HIGHEST
epsilon = 1e-05

def depthwise(source, kernel):
    extent = source.shape[1]
    padded = jnp.pad(source, ((0, 0), (1, 1), (1, 1), (0, 0)))
    summed = jnp.zeros_like(source)
    for offset_row in range(3):
        for offset_col in range(3):
            summed = summed + padded[:, offset_row:offset_row + extent, offset_col:offset_col + extent, :] * kernel[offset_row, offset_col]
    return summed

def layer_forward(current, weights):
    kernel, bn_gain, bn_bias, mix_rows, rows_bias, mix_cols, cols_bias, join_weight, join_bias, norm_gain, norm_bias, weight_in, bias_in, weight_out, bias_out = weights
    conv_out = depthwise(current, kernel)
    chan_mean = lax.optimization_barrier(jnp.mean(conv_out, axis=(0, 1, 2)))
    chan_var = lax.optimization_barrier(jnp.mean((conv_out - chan_mean) ** 2, axis=(0, 1, 2)))
    normed = (conv_out - chan_mean) * lax.rsqrt(chan_var + epsilon) * bn_gain + bn_bias
    after_conv = current + jax.nn.gelu(normed)
    along_rows = jnp.einsum('ij,bjwc->biwc', mix_rows, after_conv, precision=highest) + rows_bias[None, :, None, None]
    along_cols = jnp.einsum('ij,bhjc->bhic', mix_cols, after_conv, precision=highest) + cols_bias[None, None, :, None]
    tokens_all = after_conv.shape[0] * HW * HW
    joined_out = jnp.dot(low(after_conv).reshape(tokens_all, C), join_weight[0], precision=highest)
    joined_out = joined_out + jnp.dot(low(along_rows).reshape(tokens_all, C), join_weight[1], precision=highest)
    joined_out = joined_out + jnp.dot(low(along_cols).reshape(tokens_all, C), join_weight[2], precision=highest)
    joined_out = low_back(joined_out)
    after_join = after_conv.reshape(tokens_all, C) + joined_out + join_bias
    row_mean = lax.optimization_barrier(jnp.mean(after_join, axis=1, keepdims=True))
    row_var = lax.optimization_barrier(jnp.mean((after_join - row_mean) ** 2, axis=1, keepdims=True))
    normal = (after_join - row_mean) * lax.rsqrt(row_var + epsilon) * norm_gain + norm_bias
    hidden = low_back(jnp.dot(low(normal), weight_in, precision=highest) + bias_in)
    mlp_out = low_back(jnp.dot(low(jax.nn.gelu(hidden)), weight_out, precision=highest))
    after_mlp = after_join + mlp_out + bias_out
    return (after_mlp.reshape(after_conv.shape), (chan_mean, chan_var))

def reference(images, conv_kernel, bn_gain, bn_bias, mix_rows, mix_rows_bias, mix_cols, mix_cols_bias, join_weight, join_bias, norm_gain, norm_bias, weight_in, bias_in, weight_out, bias_out, running_mean, running_var, cotangent):
    params = tuple((item.astype(jnp.float32) for item in (conv_kernel, bn_gain, bn_bias, mix_rows, mix_rows_bias, mix_cols, mix_cols_bias, join_weight, join_bias, norm_gain, norm_bias, weight_in, bias_in, weight_out, bias_out)))

    def forward(start, weights):
        current = start
        means = []
        variances = []
        for layer_index in range(LAYERS):
            current, stats = layer_forward(current, tuple((item[layer_index] for item in weights)))
            means.append(stats[0])
            variances.append(stats[1])
        return (current, (jnp.stack(means), jnp.stack(variances)))
    result, pullback, stats = jax.vjp(forward, images.astype(jnp.float32), params, has_aux=True)
    grad_images, grad_params = pullback(cotangent)
    cell_count = BATCH * HW * HW
    new_mean = 0.9 * running_mean + 0.1 * stats[0]
    new_var = 0.9 * running_var + 0.1 * stats[1] * (cell_count / (cell_count - 1.0))
    return (result.astype(jnp.bfloat16), grad_images, grad_params[0], grad_params[1], grad_params[2], grad_params[3], grad_params[4], grad_params[5], grad_params[6], grad_params[7], grad_params[8], grad_params[9], grad_params[10], grad_params[11], grad_params[12], grad_params[13], grad_params[14], new_mean, new_var)
```

```python
import functools
from types import SimpleNamespace

import jax
import jax.numpy as jnp
from jax import lax
from jax.experimental import pallas as pl
from jax.experimental.pallas import tpu as pltpu
from jax.sharding import PartitionSpec as P

f32 = jnp.float32
bf16 = jnp.bfloat16
MESH = pl.DeviceIdType.MESH
epsilon = 1e-05
LANES = 128
ROOT = 0.7978845608028654
CUBE = 0.044715


def up(number, step):
    return -(-number // step) * step


def dot_nn(left, right):
    return lax.dot_general(left, right, (((1,), (0,)), ((), ())), preferred_element_type=f32)


def dot_nt(left, right):
    return lax.dot_general(left, right, (((1,), (1,)), ((), ())), preferred_element_type=f32)


def dot_tn(left, right):
    return lax.dot_general(left, right, (((0,), (0,)), ((), ())), preferred_element_type=f32)


def gelu_both(value):
    square = value * value
    bend = jnp.tanh(value * (ROOT + (ROOT * CUBE) * square))
    half = 0.5 + 0.5 * bend
    slope = half + (0.5 * value) * (1.0 - bend * bend) * (ROOT + (3.0 * ROOT * CUBE) * square)
    return value * half, slope


def lane_index(shape):
    return lax.broadcasted_iota(jnp.int32, shape, len(shape) - 1)


def assemble(pieces, tiles):
    placed = [None] * tiles
    axis = pieces[0][0].ndim - 1
    lane = lane_index(pieces[0][0].shape)

    def add(place, value):
        placed[place] = value if placed[place] is None else placed[place] + value

    for tile, offset, width in pieces:
        first, shift = divmod(offset, LANES)
        if shift == 0:
            add(first, tile)
            continue
        turned = pltpu.roll(tile, shift, axis)
        if shift + width <= LANES:
            add(first, turned)
        else:
            add(first, jnp.where(lane >= shift, turned, 0.0))
            add(first + 1, jnp.where(lane < shift, turned, 0.0))
    return [jnp.zeros(pieces[0][0].shape, f32) if tile is None else tile for tile in placed]


def cut(tiles, offset, width):
    axis = tiles[0].ndim - 1
    lane = lane_index(tiles[0].shape)
    first, shift = divmod(offset, LANES)
    if shift == 0:
        value = tiles[first]
    else:
        value = pltpu.roll(tiles[first], LANES - shift, axis)
        if shift + width > LANES:
            value = jnp.where(lane < LANES - shift, value, pltpu.roll(tiles[first + 1], LANES - shift, axis))
    return value if width == LANES else jnp.where(lane < width, value, 0.0)


class Sizes:
    def __init__(self, ni, nk, images, conv_kernel, weight_in):
        self.ni, self.nk, self.nd = ni, nk, ni * nk
        self.chips = ni // 2
        self.group, self.high, self.wide, self.cl = images.shape
        self.layers = conv_kernel.shape[0]
        self.own = self.group // nk
        self.channels = weight_in.shape[1]
        self.fl = weight_in.shape[2]
        self.tj = up(self.wide, 16)
        self.cp = up(self.channels, LANES)
        self.ct = self.cp // LANES
        self.bh = self.own * self.high
        self.rows = self.bh * self.tj
        self.rb = self.high * self.tj
        self.cells = ni * self.group * self.high * self.wide
        self.clp = up(self.cl, 16)
        def part_rows(rows):
            return up(-(-rows // ni), 16)

        join_rows, mlp_rows = 3 * self.clp, 2 * self.fl
        apart, together = part_rows(join_rows) + part_rows(mlp_rows), part_rows(join_rows + mlp_rows)
        if 4 * apart <= 5 * together:
            self.parts = {"m": part_rows(mlp_rows), "j": part_rows(join_rows)}
            self.join_kind, self.join_row = "j", 0
        else:
            self.parts = {"m": together}
            self.join_kind, self.join_row = "m", mlp_rows
        self.kg = next((n for n in range(1, nk + 1) if nk % n == 0 and n * self.fl % LANES == 0), nk)
        self.nkg = nk // self.kg
        self.ft = self.kg * self.fl
        self.ftiles = -(-self.fl // LANES)
        self.step = next(n for n in (4, 2, 1) if self.bh % n == 0)
        self.lines = next(n for n in (7, 4, 2, 1) if self.high % n == 0)
        self.stat = up(2 * self.ct, 8)


PARAM_ROWS = 16
SMALL_ROWS = 40


def scratch_list(z):
    tile = (z.own, z.high, z.tj, LANES)
    layer, rows, cp = z.layers, z.rows, z.cp
    shapes = dict(
        xl=((z.group, z.high + 2, z.tj, LANES), f32),
        al=((z.group, z.high, z.tj, LANES), f32),
        stage=((4, z.nk) + tile, bf16),
        land=((4, z.nk) + tile, bf16),
        par=((layer, PARAM_ROWS + 8, LANES), f32),
        pars=((z.nk, layer, PARAM_ROWS + 8, LANES), f32),
        pf=((layer, PARAM_ROWS, cp), f32),
        bi=((layer, z.nkg, 8, z.ft), f32),
        msg=((2 * layer, z.stat, LANES), f32),
        stats=((2 * layer, z.nd, z.stat, LANES), f32),
        jf=((layer, 3, cp, cp), bf16),
        mix=((layer, 4, z.rb, z.rb), bf16),
        mixb=((layer, 2, z.rb, 8), f32),
        mixs=((4, 16, 16), f32),
        x=((layer, z.own, z.high + 2, z.tj, cp), f32),
        a=((layer, z.bh, z.tj, cp), f32),
        sz=((layer, z.bh, z.tj, cp), f32),
        mv=((layer, 8, cp), f32),
        u=((z.bh, z.tj, cp), f32),
        cat=((layer, 3, z.own, z.rb, cp), bf16),
        w=((z.bh, z.tj, cp), f32),
        what=((layer, z.bh, z.tj, cp), f32),
        inv=((layer, z.bh, z.tj, LANES), f32),
        yb=((layer, z.bh, z.tj, cp), bf16),
        hs=((layer, z.nkg, z.own, z.rb, z.ft), f32),
        gb=((layer, z.nkg, z.own, z.rb, z.ft), bf16),
        gh=((z.own, z.rb, z.ft), bf16),
        o=((z.bh, z.tj, cp), f32),
        gx=((z.bh, z.tj, cp), f32),
        gob=((z.bh, z.tj, cp), bf16),
        gw=((z.bh, z.tj, cp), f32),
        gsb=((z.bh, z.tj, cp), bf16),
        gpq=((2, z.own, z.rb, cp), bf16),
        gu=((z.bh, z.tj, cp), f32),
        gz=((z.bh, z.tj, cp), f32),
        ga=((z.own, z.high + 2, z.tj, cp), f32),
        sg=((PARAM_ROWS, cp), f32),
        bg=((8, z.nkg * z.ft), f32),
        mg=((16, LANES), f32),
        sgm=((layer, z.nk, 32, LANES), f32),
        sgk=((layer, z.nk, 32, LANES), f32),
        sgz=((layer, 32, LANES), f32),
        sgi=((layer, z.ni, 32, LANES), f32),
    )
    groups = []
    for part in z.parts.values():
        whole_rows = z.ni * part
        groups.append(
            dict(
                wt=((layer, z.nk, whole_rows, cp), bf16),
                gr=((layer, z.nk, whole_rows, cp), bf16),
                r1=((layer, z.chips, z.nk, part, cp), bf16),
                r2=((layer, z.chips - 1, z.nk, part, cp), bf16),
                r3=((layer, z.nk - 1, part, cp), bf16),
                fin=((layer, whole_rows, cp), bf16),
            )
        )
    return shapes, groups


def whole(z, *refs):
    inputs, refs = refs[:17], refs[17:]
    outputs, refs = refs[: 3 + len(z.parts)], refs[3 + len(z.parts) :]
    shapes, groups = scratch_list(z)
    r = SimpleNamespace(**dict(zip(shapes, refs[: len(shapes)], strict=True)))
    (r.images, r.conv_kernel, r.bn_gain, r.bn_bias, r.mix_rows, r.mix_rows_bias, r.mix_cols, r.mix_cols_bias) = inputs[:8]
    (r.join_weight, r.join_bias, r.norm_gain, r.norm_bias, r.weight_in, r.bias_in, r.weight_out, r.bias_out) = inputs[8:16]
    r.cotangent = inputs[16]
    r.out_y, r.out_g, r.out_s = outputs[:3]
    r.outs = dict(zip(z.parts, outputs[3:], strict=True))
    refs = refs[len(shapes) :]
    table = SimpleNamespace(**{name: {} for name in groups[0]})
    for kind, group in zip(z.parts, groups, strict=True):
        for name, ref in zip(group, refs[: len(group)], strict=True):
            getattr(table, name)[kind] = ref
        refs = refs[len(group) :]
    r.wt, r.gr, r.r1, r.r2, r.r3, r.fin = table.wt, table.gr, table.r1, table.r2, table.r3, table.fin
    ssem, rsem = refs
    ni, nk, nd, layers = z.ni, z.nk, z.nd, z.layers
    i = lax.axis_index("img")
    k = lax.axis_index("ch")
    core = lax.rem(i, 2)
    chip = lax.div(i, 2)
    partner = i + 1 - 2 * core
    events = {}
    sends = []

    def at(image_index, channel_index):
        return {"img": image_index, "ch": channel_index}

    def event(name):
        return events.setdefault(name, len(events))

    def send(name, src, dst, device):
        number = event(name)
        pltpu.make_async_remote_copy(
            src_ref=src,
            dst_ref=dst,
            send_sem=ssem.at[number],
            recv_sem=rsem.at[number],
            device_id=device,
            device_id_type=MESH,
        ).start()

    def arrived(name, ref):
        number = event(name)
        sends.append((number, ref))
        pltpu.make_async_remote_copy(
            src_ref=ref,
            dst_ref=ref,
            send_sem=ssem.at[number],
            recv_sem=rsem.at[number],
            device_id=at(partner, k),
            device_id_type=MESH,
        ).wait_recv()

    def loop(count, body, start=0):
        def run(index, carry):
            body(index)
            return carry

        lax.fori_loop(start, count, run, 0)

    barrier = pltpu.get_barrier_semaphore()

    def greet(j):
        pl.semaphore_signal(
            barrier,
            inc=1,
            device_id=at(lax.rem(i + lax.div(j, nk), ni), lax.rem(k + lax.rem(j, nk), nk)),
            device_id_type=MESH,
        )

    loop(nd, greet, 1)

    def exchange_start(slot):
        stats, msg = r.stats, r.msg
        mine = i * nk + k
        stats[slot, mine] = msg[slot]

        def one(j):
            send(
                ("st", slot),
                msg.at[slot],
                stats.at[slot, mine],
                at(lax.rem(i + lax.div(j, nk), ni), lax.rem(k + lax.rem(j, nk), nk)),
            )

        loop(nd, one, 1)

    def exchange_wait(slot):
        arrived(("st", slot), r.stats.at[slot, pl.ds(0, nd - 1)])

    def swap_start(slot):
        for step in range(1, nk):
            other = lax.rem(k + step, nk)
            send(("sw", slot), r.stage.at[slot, other], r.land.at[slot, k], at(i, other))

    def swap_wait(slot):
        arrived(("sw", slot), r.land.at[slot, pl.ds(0, nk - 1)])

    def own_tile(slot):
        r.land[slot, k] = r.stage[slot, k]

    def rps(kind):
        return z.parts[kind]

    def piece(number, size):
        return pl.ds(pl.multiple_of(number * size, 16), size)

    done = set()

    def once(work):
        def run(layer, kind):
            if kind in z.parts and (work, layer, kind) not in done:
                done.add((work, layer, kind))
                work(layer, kind)

        return run

    @once
    def weights_along(layer, kind):
        buffer = r.wt[kind]
        place = piece(i, rps(kind))
        for step in range(1, nk):
            ref = buffer.at[layer, k, place]
            send(("w1", layer, kind), ref, ref, at(i, lax.rem(k + step, nk)))

    @once
    def weights_across(layer, kind):
        buffer = r.wt[kind]
        size = rps(kind)
        arrived(("w1", layer, kind), buffer.at[layer, pl.ds(0, nk - 1), pl.ds(0, size)])
        for step in range(1, nk):
            ref = buffer.at[layer, lax.rem(k + step, nk), piece(i, size)]
            for turn in range(1, z.chips):
                send(("w2", layer, kind), ref, ref, at(2 * lax.rem(chip + turn, z.chips) + core, k))

    @once
    def weights_pair(layer, kind):
        buffer = r.wt[kind]
        size = rps(kind)
        arrived(("w2", layer, kind), buffer.at[layer, pl.ds(0, nk - 1), pl.ds(0, (z.chips - 1) * size)])
        for step in range(1, nk):
            for other in range(z.chips):
                ref = buffer.at[layer, lax.rem(k + step, nk), piece(2 * other + core, size)]
                send(("w3", layer, kind), ref, ref, at(partner, k))

    @once
    def weights_ready(layer, kind):
        size = rps(kind)
        arrived(("w3", layer, kind), r.wt[kind].at[layer, pl.ds(0, nk - 1), pl.ds(0, z.chips * size)])
        if kind == z.join_kind:
            for branch in range(3):
                row = z.join_row + branch * z.clp
                parts = [
                    r.wt[kind][layer, part, row : row + z.cl, :].astype(f32)
                    for part in range(nk)
                ]
                if z.cp > z.channels:
                    parts.append(jnp.zeros((z.cp - z.channels, z.cp), f32))
                r.jf[layer, branch] = jnp.concatenate(parts, axis=0).astype(bf16)

    @once
    def reduce_pair(layer, kind):
        size = rps(kind)
        for other in range(z.chips):
            send(
                ("r1", layer, kind),
                r.gr[kind].at[layer, :, piece(2 * other + 1 - core, size)],
                r.r1[kind].at[layer, other],
                at(partner, k),
            )

    @once
    def reduce_across(layer, kind):
        size = rps(kind)
        arrived(("r1", layer, kind), r.r1[kind].at[layer])
        for other in range(z.chips):
            place = piece(2 * other + core, size)

            def add(part, other=other, place=place):
                r.gr[kind][layer, part, place] = (
                    r.gr[kind][layer, part, place].astype(f32) + r.r1[kind][layer, other, part].astype(f32)
                ).astype(bf16)

            loop(nk, add)
        for turn in range(1, z.chips):
            other = lax.rem(chip + turn, z.chips)
            send(
                ("r2", layer, kind),
                r.gr[kind].at[layer, :, piece(2 * other + core, size)],
                r.r2[kind].at[layer, turn - 1],
                at(2 * other + core, k),
            )

    @once
    def reduce_along(layer, kind):
        arrived(("r2", layer, kind), r.r2[kind].at[layer])
        place = piece(i, rps(kind))

        def add(part):
            total = r.gr[kind][layer, part, place].astype(f32)
            for turn in range(z.chips - 1):
                total = total + r.r2[kind][layer, turn, part].astype(f32)
            r.gr[kind][layer, part, place] = total.astype(bf16)

        loop(nk, add)
        for step in range(1, nk):
            other = lax.rem(k + step, nk)
            send(
                ("r3", layer, kind),
                r.gr[kind].at[layer, other, place],
                r.r3[kind].at[layer, step - 1],
                at(i, other),
            )

    @once
    def spread_across(layer, kind):
        size = rps(kind)
        arrived(("r3", layer, kind), r.r3[kind].at[layer])
        place = piece(i, size)
        total = r.gr[kind][layer, k, place].astype(f32)
        for step in range(nk - 1):
            total = total + r.r3[kind][layer, step].astype(f32)
        r.fin[kind][layer, place] = total.astype(bf16)
        ref = r.fin[kind].at[layer, place]
        for turn in range(1, z.chips):
            send(("r4", layer, kind), ref, ref, at(2 * lax.rem(chip + turn, z.chips) + core, k))

    @once
    def spread_pair(layer, kind):
        size = rps(kind)
        arrived(("r4", layer, kind), r.fin[kind].at[layer, pl.ds(0, (z.chips - 1) * size)])
        for other in range(z.chips):
            ref = r.fin[kind].at[layer, piece(2 * other + core, size)]
            send(("r5", layer, kind), ref, ref, at(partner, k))

    @once
    def spread_ready(layer, kind):
        arrived(("r5", layer, kind), r.fin[kind].at[layer, pl.ds(0, z.chips * rps(kind))])
        r.outs[kind][layer] = r.fin[kind][layer]

    cleared = [r.xl, r.x, r.ga, r.par, r.pf, r.bi, r.mixs, r.mg, r.sg, r.bg, r.sgm]
    for ref in cleared + list(r.gr.values()):
        if len(ref.shape) > 3:

            def clear(index, ref=ref):
                ref[index] = jnp.zeros(ref.shape[1:], ref.dtype)

            loop(ref.shape[0], clear)
        else:
            ref[...] = jnp.zeros(ref.shape, ref.dtype)

    tile_row = lax.broadcasted_iota(jnp.int32, (z.tj, LANES), 0)
    inside = tile_row < z.wide

    def take_image(n):
        def line(h):
            r.xl[n, h + 1, 0 : z.wide, 0 : z.cl] = r.images[n, h].astype(f32)

        loop(z.high, line)
        r.stage[0, lax.div(n, z.own), lax.rem(n, z.own)] = r.xl[n, 1 : z.high + 1].astype(bf16)

    loop(z.group, take_image)

    small = [
        (9, r.bn_gain),
        (10, r.bn_bias),
        (11, r.join_bias),
        (12, r.norm_gain),
        (13, r.norm_bias),
        (14, r.bias_out),
    ]
    for row, ref in small:
        values = ref[...].astype(f32)
        for layer in range(layers):
            r.par[layer, row : row + 1, 0 : z.cl] = values[layer : layer + 1]
    values = r.bias_in[...].astype(f32)
    for layer in range(layers):
        for tap in range(3):
            r.par[layer, 3 * tap : 3 * tap + 3, 0 : z.cl] = r.conv_kernel[layer, tap].astype(f32)
        for tile in range(z.ftiles):
            stop = min(z.fl, LANES * (tile + 1))
            r.par[layer, PARAM_ROWS + tile : PARAM_ROWS + tile + 1, 0 : stop - LANES * tile] = values[
                layer : layer + 1, LANES * tile : stop
            ]

    def conv(lines, taps):
        count = lines.shape[0] - 2
        shifted = (pltpu.roll(lines, 1, 1), lines, pltpu.roll(lines, z.tj - 1, 1))
        total = None
        for down in range(3):
            for side in range(3):
                term = shifted[side][down : down + count] * taps[3 * down + side]
                total = term if total is None else total + term
        return total

    taps = [r.par[0, t : t + 1, :] for t in range(9)]

    def conv_local(n, carry):
        value = jnp.where(inside, conv(r.xl[n], taps), 0.0)
        r.al[n] = value
        return carry + jnp.sum(value, axis=0)

    local_cells = z.group * z.high * z.wide
    total = lax.fori_loop(0, z.group, conv_local, jnp.zeros((z.tj, LANES), f32))
    local_mean = jnp.sum(total, axis=0, keepdims=True) * (1.0 / local_cells)

    def square_local(n, carry):
        away = jnp.where(inside, r.al[n] - local_mean, 0.0)
        return carry + jnp.sum(away * away, axis=0)

    total = lax.fori_loop(0, z.group, square_local, jnp.zeros((z.tj, LANES), f32))
    local_var = jnp.sum(total, axis=0, keepdims=True) * (1.0 / local_cells)
    r.msg[0] = jnp.concatenate([local_mean, local_var, jnp.zeros((z.stat - 2, LANES), f32)], axis=0)

    pl.semaphore_wait(barrier, nd - 1)

    swap_start(0)
    exchange_start(0)
    r.pars[k] = r.par[...]
    for step in range(1, nk):
        send("par", r.par, r.pars.at[k], at(i, lax.rem(k + step, nk)))
    own_tile(0)

    blank = jnp.zeros((z.cl, z.cp - z.channels), f32)
    blank_hidden = jnp.zeros((z.fl, z.cp - z.channels), f32)
    for layer in range(layers):
        for kind in z.parts:
            r.wt[kind][layer, k] = jnp.zeros(r.wt[kind].shape[2:], bf16)
        for branch in range(3):
            value = r.join_weight[layer, branch].astype(f32)
            if z.cp > z.channels:
                value = jnp.concatenate([value, blank], axis=1)
            row = z.join_row + branch * z.clp
            r.wt[z.join_kind][layer, k, row : row + z.cl, :] = value.astype(bf16)
        for place, value in (
            (0, r.weight_in[layer].astype(f32).T),
            (z.fl, r.weight_out[layer].astype(f32)),
        ):
            if z.cp > z.channels:
                value = jnp.concatenate([value, blank_hidden], axis=1)
            r.wt["m"][layer, k, place : place + z.fl, :] = value.astype(bf16)
        if layer == 0:
            for kind in ("j", "m"):
                weights_along(0, kind)

    select_row = lax.broadcasted_iota(jnp.int32, (z.rb, 16), 0)
    select_col = lax.broadcasted_iota(jnp.int32, (z.rb, 16), 1)
    pick_high = (lax.div(select_row, z.tj) == select_col).astype(f32)
    pick_wide = (lax.rem(select_row, z.tj) == select_col).astype(f32)
    low_high, low_wide = pick_high.astype(bf16), pick_wide.astype(bf16)
    full_row = lax.broadcasted_iota(jnp.int32, (z.rb, z.rb), 0)
    full_col = lax.broadcasted_iota(jnp.int32, (z.rb, z.rb), 1)
    same_wide = (lax.rem(full_row, z.tj) == lax.rem(full_col, z.tj)) & (lax.rem(full_row, z.tj) < z.wide)
    same_high = lax.div(full_row, z.tj) == lax.div(full_col, z.tj)
    for layer in range(layers):
        for which, (maps, shifts, pick, same, extent) in enumerate(
            (
                (r.mix_rows, r.mix_rows_bias, low_high, same_wide, z.high),
                (r.mix_cols, r.mix_cols_bias, low_wide, same_high, z.wide),
            )
        ):
            r.mixs[which, 0:extent, 0:extent] = maps[layer].astype(f32)
            table = r.mixs[which].astype(bf16)
            for turned, half in ((0, dot_nn(pick, table)), (1, dot_nt(pick, table))):
                spread = dot_nt(half.astype(bf16), pick)
                r.mix[layer, 2 * which + turned] = jnp.where(same, spread, 0.0).astype(bf16)
            r.mixs[2 + which, 0:1, 0:extent] = shifts[layer : layer + 1, :].astype(f32)
            r.mixb[layer, which] = dot_nt(pick, r.mixs[2 + which, 0:8, :].astype(bf16))

    exchange_wait(0)
    arrived("par", r.pars.at[pl.ds(0, nk - 1)])
    for layer in range(layers):
        tiles = assemble(
            [(r.pars[part, layer, 0:PARAM_ROWS, :], part * z.cl, z.cl) for part in range(nk)], z.ct
        )
        for tile in range(z.ct):
            r.pf[layer, :, LANES * tile : LANES * (tile + 1)] = tiles[tile]
        for block in range(z.nkg):
            pieces = []
            for part in range(z.kg):
                for tile in range(z.ftiles):
                    row = PARAM_ROWS + tile
                    value = r.pars[block * z.kg + part, layer, row : row + 1, :]
                    width = min(LANES, z.fl - LANES * tile)
                    pieces.append((jnp.broadcast_to(value, (8, LANES)), part * z.fl + LANES * tile, width))
            tiles = assemble(pieces, -(-z.ft // LANES))
            for tile, value in enumerate(tiles):
                stop = min(z.ft, LANES * (tile + 1))
                r.bi[layer, block, :, LANES * tile : stop] = value[:, 0 : stop - LANES * tile]

    def param(layer, row):
        return r.pf[layer, row : row + 1, :]

    def wide_row(tiles):
        return jnp.concatenate(tiles, axis=1)

    def combine(means, variances):
        count = means.shape[0]
        mean = jnp.sum(means, axis=0, keepdims=True) * (1.0 / count)
        away = means - mean
        var = jnp.sum(variances + away * away, axis=0, keepdims=True) * (1.0 / count)
        return mean[0], var[0]

    lane_full = lane_index((z.step, z.tj, z.cp))
    column_full = lax.broadcasted_iota(jnp.int32, (z.step, z.tj, z.cp), 1)
    real_lane = lane_full < z.channels
    real_column = column_full < z.wide
    blocks = z.bh // z.step

    def place_of(t):
        return lax.div(t, z.high), lax.rem(t, z.high)

    def unpack(slot, store):
        def image(b):
            def lines(part):
                start = part * z.lines
                tiles = assemble(
                    [
                        (r.land[slot, source, b, pl.ds(start, z.lines)].astype(f32), source * z.cl, z.cl)
                        for source in range(nk)
                    ],
                    z.ct,
                )
                store(b, start, tiles)

            loop(z.high // z.lines, lines)

        loop(z.own, image)

    def store_x(b, start, tiles):
        for tile in range(z.ct):
            r.x[0, b, pl.ds(start + 1, z.lines), :, LANES * tile : LANES * (tile + 1)] = tiles[tile]

    def store_gx(b, start, tiles):
        for tile in range(z.ct):
            r.gx[pl.ds(b * z.high + start, z.lines), :, LANES * tile : LANES * (tile + 1)] = tiles[tile]

    def pack(slot, take):
        def image(b):
            def lines(part):
                start = part * z.lines
                tiles = [take(b, start, tile) for tile in range(z.ct)]
                for target in range(nk):
                    r.stage[slot, target, b, pl.ds(start, z.lines)] = cut(tiles, target * z.cl, z.cl).astype(bf16)

            loop(z.high // z.lines, lines)

        loop(z.own, image)

    swap_wait(0)
    unpack(0, store_x)

    own_cells = z.own * z.high * z.wide

    for layer in range(layers):

        def conv_part(t, carry, layer=layer):
            b, part = lax.div(t, z.high // z.lines), lax.rem(t, z.high // z.lines)
            start = part * z.lines
            sums = []
            for tile in range(z.ct):
                lanes = slice(LANES * tile, LANES * (tile + 1))
                taps = [r.pf[layer, row : row + 1, lanes] for row in range(9)]
                value = conv(r.x[layer, b, pl.ds(start, z.lines + 2), :, lanes], taps)
                value = jnp.where(inside, value, 0.0)
                r.a[layer, pl.ds(b * z.high + start, z.lines), :, lanes] = value
                sums.append(carry[tile] + jnp.sum(value, axis=0))
            return tuple(sums)

        sums = lax.fori_loop(
            0,
            z.own * (z.high // z.lines),
            conv_part,
            tuple(jnp.zeros((z.tj, LANES), f32) for _ in range(z.ct)),
        )
        if layer == 0:
            stats = r.stats[0].reshape(ni, nk, z.stat, LANES)
            whole_mean, whole_var = [], []
            for part in range(nk):
                mean, var = combine(stats[:, part, 0:1, :], stats[:, part, 1:2, :])
                whole_mean.append((jnp.broadcast_to(mean, (8, LANES)), part * z.cl, z.cl))
                whole_var.append((jnp.broadcast_to(var, (8, LANES)), part * z.cl, z.cl))
            mean = wide_row([tile[0:1] for tile in assemble(whole_mean, z.ct)])
            var = wide_row([tile[0:1] for tile in assemble(whole_var, z.ct)])
        else:
            own_mean = wide_row([jnp.sum(tile, axis=0, keepdims=True) for tile in sums]) * (1.0 / own_cells)

            def square_part(t, carry, layer=layer, own_mean=own_mean):
                value = r.a[layer, pl.ds(t * z.step, z.step)] - own_mean
                value = jnp.where(real_column, value, 0.0)
                return carry + jnp.sum(value * value, axis=0)

            squares = lax.fori_loop(0, blocks, square_part, jnp.zeros((z.tj, z.cp), f32))
            own_var = jnp.sum(squares, axis=0, keepdims=True) * (1.0 / own_cells)
            for tile in range(z.ct):
                lanes = slice(LANES * tile, LANES * (tile + 1))
                r.msg[layer, tile : tile + 1, :] = own_mean[:, lanes]
                r.msg[layer, z.ct + tile : z.ct + tile + 1, :] = own_var[:, lanes]
            exchange_start(layer)
            weights_across(layer, "j")
            weights_across(layer, "m")
            weights_pair(layer, z.join_kind)
            exchange_wait(layer)
            stats = r.stats[layer]
            mean, var = combine(stats[:, 0 : z.ct, :], stats[:, z.ct : 2 * z.ct, :])
            mean = wide_row([mean[t : t + 1] for t in range(z.ct)])
            var = wide_row([var[t : t + 1] for t in range(z.ct)])
        inv_std = lax.rsqrt(var + epsilon)
        r.mv[layer, 0:1, :] = mean
        r.mv[layer, 1:2, :] = var
        r.mv[layer, 2:3, :] = inv_std
        scale = inv_std * param(layer, 9)
        shift = param(layer, 10)

        def norm_part(t, layer=layer, mean=mean, scale=scale, shift=shift):
            lines = pl.ds(t * z.step, z.step)
            active, slope = gelu_both((r.a[layer, lines] - mean) * scale + shift)
            r.sz[layer, lines] = slope
            b, start = place_of(t * z.step)
            value = jnp.where(real_column, active, 0.0)
            r.u[lines] = value

        loop(blocks, norm_part)

        def add_part(b, layer=layer):
            value = r.u[pl.ds(b * z.high, z.high)] + r.x[layer, b, 1 : z.high + 1]
            r.u[pl.ds(b * z.high, z.high)] = value
            r.cat[layer, 0, b] = value.reshape(z.rb, z.cp).astype(bf16)

        loop(z.own, add_part)
        if layer == 0:
            weights_across(0, "j")
            weights_across(0, "m")
            if layers > 1:
                weights_along(1, "j")
                weights_along(1, "m")

        def mix_part(b, layer=layer):
            low = r.cat[layer, 0, b]
            for which in range(2):
                value = dot_nn(r.mix[layer, 2 * which], low) + r.mixb[layer, which, :, 0:1]
                r.cat[layer, 1 + which, b] = value.astype(bf16)

        loop(z.own, mix_part)
        weights_pair(layer, z.join_kind)
        weights_ready(layer, z.join_kind)
        weights_pair(layer, "m")
        if 0 < layer < layers - 1:
            weights_along(layer + 1, "j")
            weights_along(layer + 1, "m")

        def join_part(b, layer=layer):
            value = dot_nn(r.cat[layer, 0, b], r.jf[layer, 0])
            value = value + dot_nn(r.cat[layer, 1, b], r.jf[layer, 1])
            value = value + dot_nn(r.cat[layer, 2, b], r.jf[layer, 2])
            r.w[pl.ds(b * z.high, z.high)] = value.reshape(z.high, z.tj, z.cp)

        loop(z.own, join_part)

        def token_part(t, layer=layer):
            lines = pl.ds(t * z.step, z.step)
            value = r.w[lines] + r.u[lines] + param(layer, 11)
            r.w[lines] = value
            mean = jnp.sum(value, axis=2, keepdims=True) * (1.0 / z.channels)
            away = jnp.where(real_lane, value - mean, 0.0)
            var = jnp.sum(away * away, axis=2, keepdims=True) * (1.0 / z.channels)
            inv = lax.rsqrt(var + epsilon)
            what = away * inv
            r.what[layer, lines] = what
            r.inv[layer, lines] = jnp.broadcast_to(inv, (z.step, z.tj, LANES))
            r.yb[layer, lines] = (what * param(layer, 12) + param(layer, 13)).astype(bf16)

        loop(blocks, token_part)
        weights_ready(layer, "m")

        def mlp_part(b, layer=layer):
            lines = pl.ds(b * z.high, z.high)
            low = r.yb[layer, lines].reshape(z.rb, z.cp)
            total = None
            for block in range(z.nkg):
                parts = slice(block * z.kg, (block + 1) * z.kg)
                rising = r.wt["m"][layer, parts, 0 : z.fl, :].reshape(z.ft, z.cp)
                hidden = dot_nt(low, rising) + r.bi[layer, block, 0:1, :]
                active, slope = gelu_both(hidden)
                r.hs[layer, block, b] = slope
                active = active.astype(bf16)
                r.gb[layer, block, b] = active
                falling = r.wt["m"][layer, parts, z.fl : 2 * z.fl, :].reshape(z.ft, z.cp)
                term = dot_nn(active, falling)
                total = term if total is None else total + term
            value = total.reshape(z.high, z.tj, z.cp) + r.w[lines] + param(layer, 14)
            value = jnp.where(real_part, value, 0.0)
            if layer + 1 < layers:
                r.x[layer + 1, b, 1 : z.high + 1] = value
            else:
                r.o[lines] = value

        real_part = lax.broadcasted_iota(jnp.int32, (z.high, z.tj, z.cp), 1) < z.wide
        loop(z.own, mlp_part)

        if layer == 0:
            def take_cotangent(n):
                def line(h):
                    r.xl[n, h + 1, 0 : z.wide, 0 : z.cl] = r.cotangent[n, h]

                loop(z.high, line)
                r.stage[1, lax.div(n, z.own), lax.rem(n, z.own)] = r.xl[n, 1 : z.high + 1].astype(bf16)

            loop(z.group, take_cotangent)
            swap_start(1)
            own_tile(1)

    def take_o(b, start, tile):
        return r.o[pl.ds(b * z.high + start, z.lines), :, LANES * tile : LANES * (tile + 1)]

    pack(2, take_o)
    swap_start(2)
    own_tile(2)
    swap_wait(1)
    unpack(1, store_gx)

    for layer in reversed(range(layers)):
        above = layer + 1 if layer + 1 < layers else None

        def start_part(t, carry):
            lines = pl.ds(t * z.step, z.step)
            value = r.gx[lines]
            r.gob[lines] = value.astype(bf16)
            return carry + jnp.sum(value, axis=0)

        total = lax.fori_loop(0, blocks, start_part, jnp.zeros((z.tj, z.cp), f32))
        r.sg[12:13, :] = jnp.sum(total, axis=0, keepdims=True)
        low_out = r.gob[...].reshape(z.rows, z.cp)

        for block in range(z.nkg):
            parts = slice(block * z.kg, (block + 1) * z.kg)
            falling = r.wt["m"][layer, parts, z.fl : 2 * z.fl, :].reshape(z.ft, z.cp)
            rising = r.wt["m"][layer, parts, 0 : z.fl, :].reshape(z.ft, z.cp)

            def back_part(b, carry, layer=layer, block=block, falling=falling, rising=rising):
                lines = pl.ds(b * z.high, z.high)
                low = r.gob[lines].reshape(z.rb, z.cp)
                value = dot_nt(low, falling) * r.hs[layer, block, b]
                low = value.astype(bf16)
                r.gh[b] = low
                term = dot_nn(low, rising).reshape(z.high, z.tj, z.cp)
                r.o[lines] = term if block == 0 else r.o[lines] + term
                return carry + jnp.sum(value, axis=0, keepdims=True)

            total = lax.fori_loop(0, z.own, back_part, jnp.zeros((1, z.ft), f32))
            r.bg[0:1, block * z.ft : (block + 1) * z.ft] = total
            low_hidden = r.gh[...].reshape(z.rows, z.ft)
            low_in = r.yb[layer].reshape(z.rows, z.cp)
            value = dot_tn(low_hidden, low_in).astype(bf16).reshape(z.kg, z.fl, z.cp)
            r.gr["m"][layer, parts, 0 : z.fl, :] = value
            low_active = r.gb[layer, block].reshape(z.rows, z.ft)
            value = dot_tn(low_active, low_out).astype(bf16).reshape(z.kg, z.fl, z.cp)
            r.gr["m"][layer, parts, z.fl : 2 * z.fl, :] = value
        if z.join_kind != "m":
            reduce_pair(layer, "m")
        if above is not None:
            reduce_along(above, "m")
            reduce_along(above, "j")

        def token_back(t, carry, layer=layer):
            lines = pl.ds(t * z.step, z.step)
            gain_sum, bias_sum, join_sum = carry
            gy, what = r.o[lines], r.what[layer, lines]
            inv = r.inv[layer, lines][:, :, 0:1]
            scaled = gy * param(layer, 12)
            plain = jnp.sum(scaled, axis=2, keepdims=True) * (1.0 / z.channels)
            cross = jnp.sum(scaled * what, axis=2, keepdims=True) * (1.0 / z.channels)
            value = r.gx[lines] + inv * (jnp.where(real_lane, scaled - plain, 0.0) - what * cross)
            r.gw[lines] = value
            r.gsb[lines] = value.astype(bf16)
            return (
                gain_sum + jnp.sum(gy * what, axis=0),
                bias_sum + jnp.sum(gy, axis=0),
                join_sum + jnp.sum(value, axis=0),
            )

        zero = jnp.zeros((z.tj, z.cp), f32)
        gain_sum, bias_sum, join_sum = lax.fori_loop(0, blocks, token_back, (zero, zero, zero))
        r.sg[9:10, :] = jnp.sum(join_sum, axis=0, keepdims=True)
        r.sg[10:11, :] = jnp.sum(gain_sum, axis=0, keepdims=True)
        r.sg[11:12, :] = jnp.sum(bias_sum, axis=0, keepdims=True)

        low_join = r.gsb[...].reshape(z.rows, z.cp)
        for branch in range(3):
            value = dot_tn(r.cat[layer, branch].reshape(z.rows, z.cp), low_join)
            for part in range(nk):
                row = z.join_row + branch * z.clp
                r.gr[z.join_kind][layer, part, row : row + z.cl, :] = value[
                    part * z.cl : (part + 1) * z.cl
                ].astype(bf16)
        reduce_pair(layer, z.join_kind)

        def mix_back(b, carry, layer=layer):
            lines = pl.ds(b * z.high, z.high)
            low = r.gsb[lines].reshape(z.rb, z.cp)
            total = r.gw[lines].reshape(z.rb, z.cp) + dot_nt(low, r.jf[layer, 0])
            tables, sums = [], []
            for which in range(2):
                value = dot_nt(low, r.jf[layer, 1 + which])
                back = value.astype(bf16)
                total = total + dot_nn(r.mix[layer, 2 * which + 1], back)
                tables.append(carry[which] + dot_nt(back, r.cat[layer, 0, b]))
                sums.append(carry[2 + which] + jnp.sum(value, axis=1, keepdims=True))
            r.gu[lines] = total.reshape(z.high, z.tj, z.cp)
            return (*tables, *sums)

        square, column = jnp.zeros((z.rb, z.rb), f32), jnp.zeros((z.rb, 1), f32)
        rows_table, cols_table, rows_sum, cols_sum = lax.fori_loop(
            0, z.own, mix_back, (square, square, column, column)
        )

        inv_std = r.mv[layer, 2:3, :]
        mean = r.mv[layer, 0:1, :]

        def gate_back(t, carry, layer=layer, mean=mean, inv_std=inv_std):
            lines = pl.ds(t * z.step, z.step)
            value = r.gu[lines] * r.sz[layer, lines]
            r.gz[lines] = value
            centred = (r.a[layer, lines] - mean) * inv_std
            return carry[0] + jnp.sum(value, axis=0), carry[1] + jnp.sum(value * centred, axis=0)

        first, second = lax.fori_loop(0, blocks, gate_back, (zero, zero))
        first = jnp.sum(first, axis=0, keepdims=True)
        second = jnp.sum(second, axis=0, keepdims=True)
        slot = layers + layer
        for tile in range(z.ct):
            lanes = slice(LANES * tile, LANES * (tile + 1))
            r.msg[slot, tile : tile + 1, :] = first[:, lanes]
            r.msg[slot, z.ct + tile : z.ct + tile + 1, :] = second[:, lanes]
        exchange_start(slot)

        rows_table = jnp.where(same_wide, rows_table, 0.0).reshape(z.high, z.tj, z.rb)
        rows_table = jnp.sum(rows_table, axis=1)
        rows_table = lax.dot_general(
            rows_table, pick_high, (((1,), (0,)), ((), ())), preferred_element_type=f32, precision=lax.Precision.HIGHEST
        )
        cols_table = jnp.sum(jnp.where(same_high, cols_table, 0.0).reshape(z.high, z.tj, z.rb), axis=0)
        cols_table = lax.dot_general(
            cols_table, pick_wide, (((1,), (0,)), ((), ())), preferred_element_type=f32, precision=lax.Precision.HIGHEST
        )
        r.mg[0 : z.high, 0:16] = rows_table
        r.mg[:, 16:32] = cols_table
        r.mg[0 : z.high, 32:33] = jnp.sum(rows_sum.reshape(z.high, z.tj, 1), axis=1)
        r.mg[:, 33:34] = jnp.sum(cols_sum.reshape(z.high, z.tj, 1), axis=0)
        reduce_across(layer, "m")
        reduce_across(layer, "j")
        if above is not None:
            spread_across(above, "m")
            spread_across(above, "j")

        exchange_wait(slot)
        stats = jnp.sum(r.stats[slot], axis=0)
        bias_total = wide_row([stats[t : t + 1] for t in range(z.ct)])
        gain_total = wide_row([stats[z.ct + t : z.ct + t + 1] for t in range(z.ct)])
        r.mv[layer, 3:4, :] = gain_total
        r.mv[layer, 4:5, :] = bias_total
        factor = inv_std * param(layer, 9)
        plain = bias_total * (1.0 / z.cells)
        cross = gain_total * (1.0 / z.cells) * inv_std

        def conv_gate(b, layer=layer, mean=mean, factor=factor, plain=plain, cross=cross):
            lines = pl.ds(b * z.high, z.high)
            value = r.gz[lines] - plain - (r.a[layer, lines] - mean) * cross
            r.ga[b, 1 : z.high + 1] = jnp.where(real_part, value * factor, 0.0)

        loop(z.own, conv_gate)

        def conv_back(t, layer=layer):
            b, part = lax.div(t, z.high // z.lines), lax.rem(t, z.high // z.lines)
            start = part * z.lines
            lines = pl.ds(b * z.high + start, z.lines)
            for tile in range(z.ct):
                lanes = slice(LANES * tile, LANES * (tile + 1))
                taps = [r.pf[layer, 8 - row : 9 - row, lanes] for row in range(9)]
                value = conv(r.ga[b, pl.ds(start, z.lines + 2), :, lanes], taps)
                r.gx[lines, :, lanes] = jnp.where(inside, value + r.gu[lines, :, lanes], 0.0)

        loop(z.own * (z.high // z.lines), conv_back)

        if layer == 0:

            def take_gx(b, start, tile):
                return r.gx[pl.ds(b * z.high + start, z.lines), :, LANES * tile : LANES * (tile + 1)]

            pack(3, take_gx)
            swap_start(3)
            own_tile(3)

        for tile in range(z.ct):
            lanes = slice(LANES * tile, LANES * (tile + 1))

            def kernel_part(t, carry, layer=layer, lanes=lanes):
                b, part = lax.div(t, z.high // z.lines), lax.rem(t, z.high // z.lines)
                start = part * z.lines
                lines = r.x[layer, b, pl.ds(start, z.lines + 2), :, lanes]
                upstream = r.ga[b, pl.ds(start + 1, z.lines), :, lanes]
                shifted = (pltpu.roll(lines, 1, 1), lines, pltpu.roll(lines, z.tj - 1, 1))
                return tuple(
                    carry[3 * down + side]
                    + jnp.sum(jnp.sum(shifted[side][down : down + z.lines] * upstream, axis=0), axis=0, keepdims=True)
                    for down in range(3)
                    for side in range(3)
                )

            totals = lax.fori_loop(
                0,
                z.own * (z.high // z.lines),
                kernel_part,
                tuple(jnp.zeros((1, LANES), f32) for _ in range(9)),
            )
            for row in range(9):
                r.sg[row : row + 1, lanes] = totals[row]

        tiles = [r.sg[:, LANES * tile : LANES * (tile + 1)] for tile in range(z.ct)]
        for part in range(nk):
            r.sgm[layer, part, 0:16, :] = cut(tiles, part * z.cl, z.cl)
            for tile in range(z.ftiles):
                start = part * z.fl + LANES * tile
                width = min(LANES, z.fl - LANES * tile)
                hidden = [
                    r.bg[:, LANES * t : min(LANES * (t + 1), nk * z.fl)] for t in range(-(-nk * z.fl // LANES))
                ]
                r.sgm[layer, part, 13 + tile : 14 + tile, :] = cut(hidden, start, width)[0:1]
            r.sgm[layer, part, 16:32, :] = r.mg[...]
        r.sgk[layer, k] = r.sgm[layer, k]
        for step in range(1, nk):
            other = lax.rem(k + step, nk)
            send(("s1", layer), r.sgm.at[layer, other], r.sgk.at[layer, k], at(i, other))

    def small_across(layer):
        arrived(("s1", layer), r.sgk.at[layer, pl.ds(0, nk - 1)])
        r.sgz[layer] = jnp.sum(r.sgk[layer], axis=0)
        r.sgi[layer, i] = r.sgz[layer]

        def one(j):
            send(("s2", layer), r.sgz.at[layer], r.sgi.at[layer, i], at(lax.rem(i + j, ni), k))

        loop(ni, one, 1)

    def small_ready(layer):
        arrived(("s2", layer), r.sgi.at[layer, pl.ds(0, ni - 1)])
        r.out_s[layer, 0:32, :] = jnp.sum(r.sgi[layer], axis=0)
        tiles = [r.mv[layer, :, LANES * tile : LANES * (tile + 1)] for tile in range(z.ct)]
        mine = jnp.zeros((8, LANES), f32)
        for part in range(nk):
            mine = mine + jnp.where(k == part, cut(tiles, part * z.cl, z.cl), 0.0)
        r.out_s[layer, 32:40, :] = mine

    for layer in reversed(range(layers)):
        small_across(layer)
    reduce_along(0, "m")
    reduce_along(0, "j")
    for layer in range(1, layers):
        spread_pair(layer, "m")
        spread_pair(layer, "j")
    spread_across(0, "m")
    spread_across(0, "j")
    swap_wait(2)
    r.out_y[...] = r.land[2]
    for layer in range(1, layers):
        small_ready(layer)
        spread_ready(layer, "m")
        spread_ready(layer, "j")
    small_ready(0)
    swap_wait(3)
    r.out_g[...] = r.land[3]
    spread_pair(0, "m")
    spread_pair(0, "j")
    spread_ready(0, "m")
    spread_ready(0, "j")

    for number, ref in sends:
        pltpu.make_async_remote_copy(
            src_ref=ref,
            dst_ref=ref,
            send_sem=ssem.at[number],
            recv_sem=rsem.at[number],
            device_id=at(partner, k),
            device_id_type=MESH,
        ).wait_send()


EVENTS = 80


def on_device(ni, nk, *args):
    images, conv_kernel, weight_in = args[0], args[1], args[12]
    running_mean, running_var, cotangent = args[16:19]
    z = Sizes(ni, nk, images, conv_kernel, weight_in)
    inputs = (*args[:16], cotangent)
    out_shape = (
        jax.ShapeDtypeStruct((nk, z.own, z.high, z.tj, LANES), bf16),
        jax.ShapeDtypeStruct((nk, z.own, z.high, z.tj, LANES), bf16),
        jax.ShapeDtypeStruct((z.layers, SMALL_ROWS, LANES), f32),
        *(jax.ShapeDtypeStruct((z.layers, ni * part, z.cp), bf16) for part in z.parts.values()),
    )
    vmem = pl.BlockSpec(memory_space=pltpu.VMEM)
    shapes, groups = scratch_list(z)
    scratch = [pltpu.VMEM(shape, kind) for table in (shapes, *groups) for shape, kind in table.values()]
    scratch += [pltpu.SemaphoreType.DMA((EVENTS,)), pltpu.SemaphoreType.DMA((EVENTS,))]
    out_y, out_g, out_s, *grads = pl.pallas_call(
        functools.partial(whole, z),
        out_shape=out_shape,
        in_specs=[vmem] * len(inputs),
        out_specs=(vmem,) * len(out_shape),
        scratch_shapes=scratch,
        compiler_params=pltpu.CompilerParams(
            collective_id=0, has_side_effects=True, vmem_limit_bytes=62 * 2**20
        ),
    )(*inputs)
    grads = dict(zip(z.parts, grads, strict=True))
    out_m, out_j = grads["m"], grads[z.join_kind][:, z.join_row :]
    shape = (z.group, z.high, z.tj, LANES)
    output = out_y.reshape(shape)[:, :, : z.wide, : z.cl]
    images_grad = out_g.reshape(shape)[:, :, : z.wide, : z.cl].astype(f32)
    rising = out_m[:, : z.fl, : z.channels].astype(f32).transpose(0, 2, 1)
    falling = out_m[:, z.fl : 2 * z.fl, : z.channels].astype(f32)
    join = out_j[:, : 3 * z.clp].reshape(z.layers, 3, z.clp, z.cp)[:, :, : z.cl, : z.channels].astype(f32)
    kernel_grad = out_s[:, :9, : z.cl].reshape(z.layers, 3, 3, z.cl)
    hidden_bias = out_s[:, 13 : 13 + z.ftiles, :].reshape(z.layers, -1)[:, : z.fl]
    mean, var = out_s[:, 32, : z.cl], out_s[:, 33, : z.cl]
    return (
        output,
        images_grad,
        kernel_grad,
        out_s[:, 35, : z.cl],
        out_s[:, 36, : z.cl],
        out_s[:, 16 : 16 + z.high, : z.high],
        out_s[:, 16 : 16 + z.high, 32],
        out_s[:, 16 : 16 + z.wide, 16 : 16 + z.wide],
        out_s[:, 16 : 16 + z.wide, 33],
        join,
        out_s[:, 9, : z.cl],
        out_s[:, 10, : z.cl],
        out_s[:, 11, : z.cl],
        rising,
        hidden_bias,
        falling,
        out_s[:, 12, : z.cl],
        0.9 * running_mean + 0.1 * mean,
        0.9 * running_var + 0.1 * var * (z.cells / (z.cells - 1.0)),
    )


def solution(mesh):
    return jax.shard_map(
        functools.partial(on_device, mesh.shape["img"], mesh.shape["ch"]),
        mesh=mesh,
        in_specs=(
            P("img", None, None, "ch"),
            P(None, None, None, "ch"),
            P(None, "ch"),
            P(None, "ch"),
            P(),
            P(),
            P(),
            P(),
            P(None, None, "ch", None),
            P(None, "ch"),
            P(None, "ch"),
            P(None, "ch"),
            P(None, None, "ch"),
            P(None, "ch"),
            P(None, "ch", None),
            P(None, "ch"),
            P(None, "ch"),
            P(None, "ch"),
            P("img", None, None, "ch"),
        ),
        out_specs=(
            P("img", None, None, "ch"),
            P("img", None, None, "ch"),
            P(None, None, None, "ch"),
            P(None, "ch"),
            P(None, "ch"),
            P(),
            P(),
            P(),
            P(),
            P(None, None, "ch", None),
            P(None, "ch"),
            P(None, "ch"),
            P(None, "ch"),
            P(None, None, "ch"),
            P(None, "ch"),
            P(None, "ch", None),
            P(None, "ch"),
            P(None, "ch"),
            P(None, "ch"),
        ),
        check_vma=False,
    )
```

```python
import functools
from types import SimpleNamespace

import jax
import jax.numpy as jnp
from jax import lax
from jax.experimental import pallas as pl
from jax.experimental.pallas import tpu as pltpu
from jax.sharding import PartitionSpec as P

f32 = jnp.float32
bf16 = jnp.bfloat16
MESH = pl.DeviceIdType.MESH
epsilon = 1e-05
LANES = 128
ROOT = 0.7978845608028654
CUBE = 0.044715


def up(number, step):
    return -(-number // step) * step


def dot_nn(left, right):
    return lax.dot_general(left, right, (((1,), (0,)), ((), ())), preferred_element_type=f32)


def dot_nt(left, right):
    return lax.dot_general(left, right, (((1,), (1,)), ((), ())), preferred_element_type=f32)


def dot_tn(left, right):
    return lax.dot_general(left, right, (((0,), (0,)), ((), ())), preferred_element_type=f32)


def gelu_both(value):
    square = value * value
    bend = jnp.tanh(value * (ROOT + (ROOT * CUBE) * square))
    half = 0.5 + 0.5 * bend
    slope = half + (0.5 * value) * (1.0 - bend * bend) * (ROOT + (3.0 * ROOT * CUBE) * square)
    return value * half, slope


def lane_index(shape):
    return lax.broadcasted_iota(jnp.int32, shape, len(shape) - 1)


def assemble(pieces, tiles):
    placed = [None] * tiles
    axis = pieces[0][0].ndim - 1
    lane = lane_index(pieces[0][0].shape)

    def add(place, value):
        placed[place] = value if placed[place] is None else placed[place] + value

    for tile, offset, width in pieces:
        first, shift = divmod(offset, LANES)
        if shift == 0:
            add(first, tile)
            continue
        turned = pltpu.roll(tile, shift, axis)
        if shift + width <= LANES:
            add(first, turned)
        else:
            add(first, jnp.where(lane >= shift, turned, 0.0))
            add(first + 1, jnp.where(lane < shift, turned, 0.0))
    return [jnp.zeros(pieces[0][0].shape, f32) if tile is None else tile for tile in placed]


def cut(tiles, offset, width):
    axis = tiles[0].ndim - 1
    lane = lane_index(tiles[0].shape)
    first, shift = divmod(offset, LANES)
    if shift == 0:
        value = tiles[first]
    else:
        value = pltpu.roll(tiles[first], LANES - shift, axis)
        if shift + width > LANES:
            value = jnp.where(lane < LANES - shift, value, pltpu.roll(tiles[first + 1], LANES - shift, axis))
    return value if width == LANES else jnp.where(lane < width, value, 0.0)


def line_groups(z, body):
    def run(g, carry):
        body(g * z.gl, g * z.gt, z.gl, z.gt)
        return carry

    if z.full:
        lax.fori_loop(0, z.full, run, 0)
    if z.rest:
        body(z.full * z.gl, z.full * z.gt, z.rest, z.rest_t)


def pack(z, stage, target, line):
    def group(first, tile, lines, tiles):
        values = assemble([(line(first + j), j * z.cl, z.cl) for j in range(lines)], tiles)
        for t in range(tiles):
            stage[target, tile + t] = values[t].astype(bf16)

    line_groups(z, group)


def unpack(z, land, store):
    def group(first, tile, lines, tiles):
        sources = [[land[k, tile + t].astype(f32) for t in range(tiles)] for k in range(z.nk)]
        for j in range(lines):
            store(
                first + j,
                assemble([(cut(source, j * z.cl, z.cl), k * z.cl, z.cl) for k, source in enumerate(sources)], z.ct),
            )

    line_groups(z, group)


class Sizes:
    def __init__(self, ni, nk, images, conv_kernel, weight_in):
        self.ni, self.nk, self.nd = ni, nk, ni * nk
        self.chips = ni // 2
        self.high, self.wide, self.group, self.cl = images.shape
        self.layers = conv_kernel.shape[2]
        self.own = self.group // nk
        self.channels = weight_in.shape[1]
        self.fl = weight_in.shape[2]
        self.tj = up(self.wide, 16)
        self.cp = up(self.channels, LANES)
        self.ct = self.cp // LANES
        self.bh = self.own * self.high
        self.rows = self.bh * self.tj
        self.rb = self.high * self.tj
        self.cells = ni * self.group * self.high * self.wide
        self.clp = up(self.cl, 16)
        def part_rows(rows):
            return up(-(-rows // ni), 16)

        join_rows, mlp_rows = 3 * self.clp, 2 * self.fl
        apart, together = part_rows(join_rows) + part_rows(mlp_rows), part_rows(join_rows + mlp_rows)
        if 4 * apart <= 5 * together:
            self.parts = {"m": part_rows(mlp_rows), "j": part_rows(join_rows)}
            self.join_kind, self.join_row = "j", 0
        else:
            self.parts = {"m": together}
            self.join_kind, self.join_row = "m", mlp_rows
        self.kg = next((n for n in range(1, nk + 1) if nk % n == 0 and n * self.fl % LANES == 0), nk)
        self.nkg = nk // self.kg
        self.ft = self.kg * self.fl
        self.ftiles = -(-self.fl // LANES)
        self.step = next(n for n in (4, 2, 1) if self.bh % n == 0)
        self.lines = next(n for n in (7, 4, 2, 1) if self.high % n == 0)
        self.stat = up(2 * self.ct, 8)
        self.gl = next(n for n in range(1, LANES + 1) if n * self.cl % LANES == 0)
        self.gt = self.gl * self.cl // LANES
        self.full, self.rest = divmod(self.bh, self.gl)
        self.rest_t = -(-self.rest * self.cl // LANES)
        self.packed = self.full * self.gt + self.rest_t


PARAM_ROWS = 16
SMALL_ROWS = 40


def scratch_list(z):
    tile = (z.packed, z.tj, LANES)
    layer, rows, cp = z.layers, z.rows, z.cp
    shapes = dict(
        tmp=((z.high, z.wide * z.group, LANES), f32),
        xl=((z.group, z.high + 2, z.tj, LANES), f32),
        al=((z.group, z.high, z.tj, LANES), f32),
        stage=((4, z.nk) + tile, bf16),
        land=((4, z.nk) + tile, bf16),
        par=((layer, PARAM_ROWS + 8, LANES), f32),
        pars=((z.nk, layer, PARAM_ROWS + 8, LANES), f32),
        pf=((layer, PARAM_ROWS, cp), f32),
        bi=((layer, z.nkg, 8, z.ft), f32),
        msg=((2 * layer, z.stat, LANES), f32),
        stats=((2 * layer, z.nd, z.stat, LANES), f32),
        jf=((layer, 3, cp, cp), bf16),
        mix=((layer, 4, z.rb, z.rb), bf16),
        mixb=((layer, 2, z.rb, 8), f32),
        mixs=((4, 16, 16), f32),
        x=((layer, z.own, z.high + 2, z.tj, cp), f32),
        a=((layer, z.bh, z.tj, cp), f32),
        sz=((layer, z.bh, z.tj, cp), f32),
        mv=((layer, 8, cp), f32),
        u=((z.bh, z.tj, cp), f32),
        cat=((layer, 3, z.own, z.rb, cp), bf16),
        w=((z.bh, z.tj, cp), f32),
        what=((layer, z.bh, z.tj, cp), f32),
        inv=((layer, z.bh, z.tj, LANES), f32),
        yb=((layer, z.bh, z.tj, cp), bf16),
        hs=((layer, z.nkg, z.own, z.rb, z.ft), f32),
        gb=((layer, z.nkg, z.own, z.rb, z.ft), bf16),
        gh=((z.own, z.rb, z.ft), bf16),
        o=((z.bh, z.tj, cp), f32),
        gx=((z.bh, z.tj, cp), f32),
        gob=((z.bh, z.tj, cp), bf16),
        gw=((z.bh, z.tj, cp), f32),
        gsb=((z.bh, z.tj, cp), bf16),
        gpq=((2, z.own, z.rb, cp), bf16),
        gu=((z.bh, z.tj, cp), f32),
        gz=((z.bh, z.tj, cp), f32),
        ga=((z.own, z.high + 2, z.tj, cp), f32),
        sg=((PARAM_ROWS, cp), f32),
        bg=((8, z.nkg * z.ft), f32),
        mg=((16, LANES), f32),
        sgm=((layer, z.nk, 32, LANES), f32),
        sgk=((layer, z.nk, 32, LANES), f32),
        sgz=((layer, 32, LANES), f32),
        sgi=((layer, z.ni, 32, LANES), f32),
    )
    groups = []
    for part in z.parts.values():
        whole_rows = z.ni * part
        groups.append(
            dict(
                wt=((layer, z.nk, whole_rows, cp), bf16),
                gr=((layer, z.nk, whole_rows, cp), bf16),
                r1=((layer, z.chips, z.nk, part, cp), bf16),
                r2=((layer, z.chips - 1, z.nk, part, cp), bf16),
                r3=((layer, z.nk - 1, part, cp), bf16),
                fin=((layer, whole_rows, cp), bf16),
            )
        )
    return shapes, groups


def whole(z, *refs):
    inputs, refs = refs[:17], refs[17:]
    outputs, refs = refs[: 3 + len(z.parts)], refs[3 + len(z.parts) :]
    shapes, groups = scratch_list(z)
    r = SimpleNamespace(**dict(zip(shapes, refs[: len(shapes)], strict=True)))
    (r.images, r.conv_kernel, r.bn_gain, r.bn_bias, r.mix_rows, r.mix_rows_bias, r.mix_cols, r.mix_cols_bias) = inputs[:8]
    (r.join_weight, r.join_bias, r.norm_gain, r.norm_bias, r.weight_in, r.bias_in, r.weight_out, r.bias_out) = inputs[8:16]
    r.cotangent = inputs[16]
    r.out_y, r.out_g, r.out_s = outputs[:3]
    r.outs = dict(zip(z.parts, outputs[3:], strict=True))
    refs = refs[len(shapes) :]
    table = SimpleNamespace(**{name: {} for name in groups[0]})
    for kind, group in zip(z.parts, groups, strict=True):
        for name, ref in zip(group, refs[: len(group)], strict=True):
            getattr(table, name)[kind] = ref
        refs = refs[len(group) :]
    r.wt, r.gr, r.r1, r.r2, r.r3, r.fin = table.wt, table.gr, table.r1, table.r2, table.r3, table.fin
    ssem, rsem = refs
    ni, nk, nd, layers = z.ni, z.nk, z.nd, z.layers
    i = lax.axis_index("img")
    k = lax.axis_index("ch")
    core = lax.rem(i, 2)
    chip = lax.div(i, 2)
    partner = i + 1 - 2 * core
    events = {}
    sends = []

    def at(image_index, channel_index):
        return {"img": image_index, "ch": channel_index}

    def event(name):
        return events.setdefault(name, len(events))

    def send(name, src, dst, device):
        number = event(name)
        pltpu.make_async_remote_copy(
            src_ref=src,
            dst_ref=dst,
            send_sem=ssem.at[number],
            recv_sem=rsem.at[number],
            device_id=device,
            device_id_type=MESH,
        ).start()

    def arrived(name, ref):
        number = event(name)
        sends.append((number, ref))
        pltpu.make_async_remote_copy(
            src_ref=ref,
            dst_ref=ref,
            send_sem=ssem.at[number],
            recv_sem=rsem.at[number],
            device_id=at(partner, k),
            device_id_type=MESH,
        ).wait_recv()

    def loop(count, body, start=0):
        def run(index, carry):
            body(index)
            return carry

        lax.fori_loop(start, count, run, 0)

    barrier = pltpu.get_barrier_semaphore()

    def greet(j):
        pl.semaphore_signal(
            barrier,
            inc=1,
            device_id=at(lax.rem(i + lax.div(j, nk), ni), lax.rem(k + lax.rem(j, nk), nk)),
            device_id_type=MESH,
        )

    loop(nd, greet, 1)

    def exchange_start(slot):
        stats, msg = r.stats, r.msg
        mine = i * nk + k
        stats[slot, mine] = msg[slot]

        def one(j):
            send(
                ("st", slot),
                msg.at[slot],
                stats.at[slot, mine],
                at(lax.rem(i + lax.div(j, nk), ni), lax.rem(k + lax.rem(j, nk), nk)),
            )

        loop(nd, one, 1)

    def exchange_wait(slot):
        arrived(("st", slot), r.stats.at[slot, pl.ds(0, nd - 1)])

    def swap_start(slot):
        for step in range(1, nk):
            other = lax.rem(k + step, nk)
            send(("sw", slot), r.stage.at[slot, other], r.land.at[slot, k], at(i, other))

    def swap_wait(slot):
        arrived(("sw", slot), r.land.at[slot, pl.ds(0, nk - 1)])

    def own_tile(slot):
        r.land[slot, k] = r.stage[slot, k]

    def rps(kind):
        return z.parts[kind]

    def piece(number, size):
        return pl.ds(pl.multiple_of(number * size, 16), size)

    done = set()

    def once(work):
        def run(layer, kind):
            if kind in z.parts and (work, layer, kind) not in done:
                done.add((work, layer, kind))
                work(layer, kind)

        return run

    @once
    def weights_along(layer, kind):
        buffer = r.wt[kind]
        place = piece(i, rps(kind))
        for step in range(1, nk):
            ref = buffer.at[layer, k, place]
            send(("w1", layer, kind), ref, ref, at(i, lax.rem(k + step, nk)))

    @once
    def weights_across(layer, kind):
        buffer = r.wt[kind]
        size = rps(kind)
        arrived(("w1", layer, kind), buffer.at[layer, pl.ds(0, nk - 1), pl.ds(0, size)])
        for step in range(1, nk):
            ref = buffer.at[layer, lax.rem(k + step, nk), piece(i, size)]
            for turn in range(1, z.chips):
                send(("w2", layer, kind), ref, ref, at(2 * lax.rem(chip + turn, z.chips) + core, k))

    @once
    def weights_pair(layer, kind):
        buffer = r.wt[kind]
        size = rps(kind)
        arrived(("w2", layer, kind), buffer.at[layer, pl.ds(0, nk - 1), pl.ds(0, (z.chips - 1) * size)])
        for step in range(1, nk):
            for other in range(z.chips):
                ref = buffer.at[layer, lax.rem(k + step, nk), piece(2 * other + core, size)]
                send(("w3", layer, kind), ref, ref, at(partner, k))

    @once
    def weights_ready(layer, kind):
        size = rps(kind)
        arrived(("w3", layer, kind), r.wt[kind].at[layer, pl.ds(0, nk - 1), pl.ds(0, z.chips * size)])
        if kind == z.join_kind:
            for branch in range(3):
                row = z.join_row + branch * z.clp
                parts = [
                    r.wt[kind][layer, part, row : row + z.cl, :].astype(f32)
                    for part in range(nk)
                ]
                if z.cp > z.channels:
                    parts.append(jnp.zeros((z.cp - z.channels, z.cp), f32))
                r.jf[layer, branch] = jnp.concatenate(parts, axis=0).astype(bf16)

    @once
    def reduce_pair(layer, kind):
        size = rps(kind)
        for other in range(z.chips):
            send(
                ("r1", layer, kind),
                r.gr[kind].at[layer, :, piece(2 * other + 1 - core, size)],
                r.r1[kind].at[layer, other],
                at(partner, k),
            )

    @once
    def reduce_across(layer, kind):
        size = rps(kind)
        arrived(("r1", layer, kind), r.r1[kind].at[layer])
        for other in range(z.chips):
            place = piece(2 * other + core, size)

            def add(part, other=other, place=place):
                r.gr[kind][layer, part, place] = (
                    r.gr[kind][layer, part, place].astype(f32) + r.r1[kind][layer, other, part].astype(f32)
                ).astype(bf16)

            loop(nk, add)
        for turn in range(1, z.chips):
            other = lax.rem(chip + turn, z.chips)
            send(
                ("r2", layer, kind),
                r.gr[kind].at[layer, :, piece(2 * other + core, size)],
                r.r2[kind].at[layer, turn - 1],
                at(2 * other + core, k),
            )

    @once
    def reduce_along(layer, kind):
        arrived(("r2", layer, kind), r.r2[kind].at[layer])
        place = piece(i, rps(kind))

        def add(part):
            total = r.gr[kind][layer, part, place].astype(f32)
            for turn in range(z.chips - 1):
                total = total + r.r2[kind][layer, turn, part].astype(f32)
            r.gr[kind][layer, part, place] = total.astype(bf16)

        loop(nk, add)
        for step in range(1, nk):
            other = lax.rem(k + step, nk)
            send(
                ("r3", layer, kind),
                r.gr[kind].at[layer, other, place],
                r.r3[kind].at[layer, step - 1],
                at(i, other),
            )

    @once
    def spread_across(layer, kind):
        size = rps(kind)
        arrived(("r3", layer, kind), r.r3[kind].at[layer])
        place = piece(i, size)
        total = r.gr[kind][layer, k, place].astype(f32)
        for step in range(nk - 1):
            total = total + r.r3[kind][layer, step].astype(f32)
        r.fin[kind][layer, place] = total.astype(bf16)
        ref = r.fin[kind].at[layer, place]
        for turn in range(1, z.chips):
            send(("r4", layer, kind), ref, ref, at(2 * lax.rem(chip + turn, z.chips) + core, k))

    @once
    def spread_pair(layer, kind):
        size = rps(kind)
        arrived(("r4", layer, kind), r.fin[kind].at[layer, pl.ds(0, (z.chips - 1) * size)])
        for other in range(z.chips):
            ref = r.fin[kind].at[layer, piece(2 * other + core, size)]
            send(("r5", layer, kind), ref, ref, at(partner, k))

    @once
    def spread_ready(layer, kind):
        arrived(("r5", layer, kind), r.fin[kind].at[layer, pl.ds(0, z.chips * rps(kind))])
        r.outs[kind][layer] = r.fin[kind][layer]

    cleared = [r.tmp, r.xl, r.x, r.ga, r.par, r.pf, r.bi, r.mixs, r.mg, r.sg, r.bg, r.sgm]
    for ref in cleared + list(r.gr.values()):
        if len(ref.shape) > 3:

            def clear(index, ref=ref):
                ref[index] = jnp.zeros(ref.shape[1:], ref.dtype)

            loop(ref.shape[0], clear)
        else:
            ref[...] = jnp.zeros(ref.shape, ref.dtype)

    tile_row = lax.broadcasted_iota(jnp.int32, (z.tj, LANES), 0)
    inside = tile_row < z.wide

    def take(ref, slot):
        def line(h):
            r.tmp[h, :, 0 : z.cl] = ref[h].astype(f32).reshape(z.wide * z.group, z.cl)
            for n in range(z.group):
                r.xl[n, h + 1, 0 : z.wide, :] = r.tmp[h, pl.ds(n, z.wide, stride=z.group), :]

        loop(z.high, line)

        def target(d):
            pack(z, r.stage.at[slot], d, lambda m: r.xl[d * z.own + lax.div(m, z.high), lax.rem(m, z.high) + 1])

        loop(nk, target)

    take(r.images, 0)

    small = [
        (9, r.bn_gain),
        (10, r.bn_bias),
        (11, r.join_bias),
        (12, r.norm_gain),
        (13, r.norm_bias),
        (14, r.bias_out),
    ]
    for row, ref in small:
        values = ref[...].astype(f32)
        for layer in range(layers):
            r.par[layer, row : row + 1, 0 : z.cl] = values[layer : layer + 1]
    values = r.bias_in[...].astype(f32)
    for layer in range(layers):
        for tap in range(3):
            for side in range(3):
                row = 3 * tap + side
                r.par[layer, row : row + 1, 0 : z.cl] = r.conv_kernel[tap, side].astype(f32)[layer : layer + 1]
        for tile in range(z.ftiles):
            stop = min(z.fl, LANES * (tile + 1))
            r.par[layer, PARAM_ROWS + tile : PARAM_ROWS + tile + 1, 0 : stop - LANES * tile] = values[
                layer : layer + 1, LANES * tile : stop
            ]

    def conv(lines, taps):
        count = lines.shape[0] - 2
        shifted = (pltpu.roll(lines, 1, 1), lines, pltpu.roll(lines, z.tj - 1, 1))
        total = None
        for down in range(3):
            for side in range(3):
                term = shifted[side][down : down + count] * taps[3 * down + side]
                total = term if total is None else total + term
        return total

    taps = [r.par[0, t : t + 1, :] for t in range(9)]

    def conv_local(n, carry):
        value = jnp.where(inside, conv(r.xl[n], taps), 0.0)
        r.al[n] = value
        return carry + jnp.sum(value, axis=0)

    local_cells = z.group * z.high * z.wide
    total = lax.fori_loop(0, z.group, conv_local, jnp.zeros((z.tj, LANES), f32))
    local_mean = jnp.sum(total, axis=0, keepdims=True) * (1.0 / local_cells)

    def square_local(n, carry):
        away = jnp.where(inside, r.al[n] - local_mean, 0.0)
        return carry + jnp.sum(away * away, axis=0)

    total = lax.fori_loop(0, z.group, square_local, jnp.zeros((z.tj, LANES), f32))
    local_var = jnp.sum(total, axis=0, keepdims=True) * (1.0 / local_cells)
    r.msg[0] = jnp.concatenate([local_mean, local_var, jnp.zeros((z.stat - 2, LANES), f32)], axis=0)

    blank = jnp.zeros((z.cl, z.cp - z.channels), f32)
    blank_hidden = jnp.zeros((z.fl, z.cp - z.channels), f32)
    for layer in range(layers):
        for kind in z.parts:
            r.wt[kind][layer, k] = jnp.zeros(r.wt[kind].shape[2:], bf16)
        for branch in range(3):
            value = r.join_weight[layer, branch].astype(f32)
            if z.cp > z.channels:
                value = jnp.concatenate([value, blank], axis=1)
            row = z.join_row + branch * z.clp
            r.wt[z.join_kind][layer, k, row : row + z.cl, :] = value.astype(bf16)
        for place, value in (
            (0, r.weight_in[layer].astype(f32).T),
            (z.fl, r.weight_out[layer].astype(f32)),
        ):
            if z.cp > z.channels:
                value = jnp.concatenate([value, blank_hidden], axis=1)
            r.wt["m"][layer, k, place : place + z.fl, :] = value.astype(bf16)

    pl.semaphore_wait(barrier, nd - 1)

    exchange_start(0)
    r.pars[k] = r.par[...]
    for step in range(1, nk):
        send("par", r.par, r.pars.at[k], at(i, lax.rem(k + step, nk)))
    weights_along(0, "j")
    weights_along(0, "m")
    swap_start(0)
    own_tile(0)

    select_row = lax.broadcasted_iota(jnp.int32, (z.rb, 16), 0)
    select_col = lax.broadcasted_iota(jnp.int32, (z.rb, 16), 1)
    pick_high = (lax.div(select_row, z.tj) == select_col).astype(f32)
    pick_wide = (lax.rem(select_row, z.tj) == select_col).astype(f32)
    low_high, low_wide = pick_high.astype(bf16), pick_wide.astype(bf16)
    full_row = lax.broadcasted_iota(jnp.int32, (z.rb, z.rb), 0)
    full_col = lax.broadcasted_iota(jnp.int32, (z.rb, z.rb), 1)
    same_wide = (lax.rem(full_row, z.tj) == lax.rem(full_col, z.tj)) & (lax.rem(full_row, z.tj) < z.wide)
    same_high = lax.div(full_row, z.tj) == lax.div(full_col, z.tj)
    for layer in range(layers):
        for which, (maps, shifts, pick, same, extent) in enumerate(
            (
                (r.mix_rows, r.mix_rows_bias, low_high, same_wide, z.high),
                (r.mix_cols, r.mix_cols_bias, low_wide, same_high, z.wide),
            )
        ):
            r.mixs[which, 0:extent, 0:extent] = maps[:, layer, :].astype(f32)
            table = r.mixs[which].astype(bf16)
            for turned, half in ((0, dot_nn(pick, table)), (1, dot_nt(pick, table))):
                spread = dot_nt(half.astype(bf16), pick)
                r.mix[layer, 2 * which + turned] = jnp.where(same, spread, 0.0).astype(bf16)
            r.mixs[2 + which, 0:1, 0:extent] = shifts[layer : layer + 1, :].astype(f32)
            r.mixb[layer, which] = dot_nt(pick, r.mixs[2 + which, 0:8, :].astype(bf16))

    weights_across(0, "j")
    weights_across(0, "m")

    exchange_wait(0)
    arrived("par", r.pars.at[pl.ds(0, nk - 1)])
    for layer in range(layers):
        tiles = assemble(
            [(r.pars[part, layer, 0:PARAM_ROWS, :], part * z.cl, z.cl) for part in range(nk)], z.ct
        )
        for tile in range(z.ct):
            r.pf[layer, :, LANES * tile : LANES * (tile + 1)] = tiles[tile]
        for block in range(z.nkg):
            pieces = []
            for part in range(z.kg):
                for tile in range(z.ftiles):
                    row = PARAM_ROWS + tile
                    value = r.pars[block * z.kg + part, layer, row : row + 1, :]
                    width = min(LANES, z.fl - LANES * tile)
                    pieces.append((jnp.broadcast_to(value, (8, LANES)), part * z.fl + LANES * tile, width))
            tiles = assemble(pieces, -(-z.ft // LANES))
            for tile, value in enumerate(tiles):
                stop = min(z.ft, LANES * (tile + 1))
                r.bi[layer, block, :, LANES * tile : stop] = value[:, 0 : stop - LANES * tile]

    def param(layer, row):
        return r.pf[layer, row : row + 1, :]

    def wide_row(tiles):
        return jnp.concatenate(tiles, axis=1)

    def combine(means, variances):
        count = means.shape[0]
        mean = jnp.sum(means, axis=0, keepdims=True) * (1.0 / count)
        away = means - mean
        var = jnp.sum(variances + away * away, axis=0, keepdims=True) * (1.0 / count)
        return mean[0], var[0]

    lane_full = lane_index((z.step, z.tj, z.cp))
    column_full = lax.broadcasted_iota(jnp.int32, (z.step, z.tj, z.cp), 1)
    real_lane = lane_full < z.channels
    real_column = column_full < z.wide
    blocks = z.bh // z.step

    def place_of(t):
        return lax.div(t, z.high), lax.rem(t, z.high)

    def store_x(m, tiles):
        for tile in range(z.ct):
            r.x[0, lax.div(m, z.high), lax.rem(m, z.high) + 1, :, LANES * tile : LANES * (tile + 1)] = tiles[tile]

    def store_gx(m, tiles):
        for tile in range(z.ct):
            r.gx[m, :, LANES * tile : LANES * (tile + 1)] = tiles[tile]

    def slices_of(ref, slot):
        for d in range(nk):

            def line(m, d=d):
                return cut([ref[m, :, LANES * t : LANES * (t + 1)] for t in range(z.ct)], d * z.cl, z.cl)

            pack(z, r.stage.at[slot], d, line)

    if layers > 1:
        weights_along(1, "j")
        weights_along(1, "m")
    swap_wait(0)
    unpack(z, r.land.at[0], store_x)

    own_cells = z.own * z.high * z.wide

    for layer in range(layers):

        def conv_part(t, carry, layer=layer):
            b, part = lax.div(t, z.high // z.lines), lax.rem(t, z.high // z.lines)
            start = part * z.lines
            sums = []
            for tile in range(z.ct):
                lanes = slice(LANES * tile, LANES * (tile + 1))
                taps = [r.pf[layer, row : row + 1, lanes] for row in range(9)]
                value = conv(r.x[layer, b, pl.ds(start, z.lines + 2), :, lanes], taps)
                value = jnp.where(inside, value, 0.0)
                r.a[layer, pl.ds(b * z.high + start, z.lines), :, lanes] = value
                sums.append(carry[tile] + jnp.sum(value, axis=0))
            return tuple(sums)

        sums = lax.fori_loop(
            0,
            z.own * (z.high // z.lines),
            conv_part,
            tuple(jnp.zeros((z.tj, LANES), f32) for _ in range(z.ct)),
        )
        if layer == 0:
            stats = r.stats[0].reshape(ni, nk, z.stat, LANES)
            whole_mean, whole_var = [], []
            for part in range(nk):
                mean, var = combine(stats[:, part, 0:1, :], stats[:, part, 1:2, :])
                whole_mean.append((jnp.broadcast_to(mean, (8, LANES)), part * z.cl, z.cl))
                whole_var.append((jnp.broadcast_to(var, (8, LANES)), part * z.cl, z.cl))
            mean = wide_row([tile[0:1] for tile in assemble(whole_mean, z.ct)])
            var = wide_row([tile[0:1] for tile in assemble(whole_var, z.ct)])
        else:
            own_mean = wide_row([jnp.sum(tile, axis=0, keepdims=True) for tile in sums]) * (1.0 / own_cells)

            def square_part(t, carry, layer=layer, own_mean=own_mean):
                value = r.a[layer, pl.ds(t * z.step, z.step)] - own_mean
                value = jnp.where(real_column, value, 0.0)
                return carry + jnp.sum(value * value, axis=0)

            squares = lax.fori_loop(0, blocks, square_part, jnp.zeros((z.tj, z.cp), f32))
            own_var = jnp.sum(squares, axis=0, keepdims=True) * (1.0 / own_cells)
            for tile in range(z.ct):
                lanes = slice(LANES * tile, LANES * (tile + 1))
                r.msg[layer, tile : tile + 1, :] = own_mean[:, lanes]
                r.msg[layer, z.ct + tile : z.ct + tile + 1, :] = own_var[:, lanes]
            exchange_start(layer)
            weights_across(layer, "j")
            weights_across(layer, "m")
            if layer == 1:
                take(r.cotangent, 1)
                swap_start(1)
                own_tile(1)
            exchange_wait(layer)
            stats = r.stats[layer]
            mean, var = combine(stats[:, 0 : z.ct, :], stats[:, z.ct : 2 * z.ct, :])
            mean = wide_row([mean[t : t + 1] for t in range(z.ct)])
            var = wide_row([var[t : t + 1] for t in range(z.ct)])
        inv_std = lax.rsqrt(var + epsilon)
        r.mv[layer, 0:1, :] = mean
        r.mv[layer, 1:2, :] = var
        r.mv[layer, 2:3, :] = inv_std
        scale = inv_std * param(layer, 9)
        shift = param(layer, 10)

        def norm_part(t, layer=layer, mean=mean, scale=scale, shift=shift):
            lines = pl.ds(t * z.step, z.step)
            active, slope = gelu_both((r.a[layer, lines] - mean) * scale + shift)
            r.sz[layer, lines] = slope
            b, start = place_of(t * z.step)
            value = jnp.where(real_column, active, 0.0)
            r.u[lines] = value

        loop(blocks, norm_part)

        def add_part(b, layer=layer):
            value = r.u[pl.ds(b * z.high, z.high)] + r.x[layer, b, 1 : z.high + 1]
            r.u[pl.ds(b * z.high, z.high)] = value
            r.cat[layer, 0, b] = value.reshape(z.rb, z.cp).astype(bf16)

        loop(z.own, add_part)
        weights_pair(layer, z.join_kind)

        def mix_part(b, layer=layer):
            low = r.cat[layer, 0, b]
            for which in range(2):
                value = dot_nn(r.mix[layer, 2 * which], low) + r.mixb[layer, which, :, 0:1]
                r.cat[layer, 1 + which, b] = value.astype(bf16)

        loop(z.own, mix_part)
        weights_ready(layer, z.join_kind)
        weights_pair(layer, "m")
        if 0 < layer < layers - 1:
            weights_along(layer + 1, "j")
            weights_along(layer + 1, "m")

        def join_part(b, layer=layer):
            value = dot_nn(r.cat[layer, 0, b], r.jf[layer, 0])
            value = value + dot_nn(r.cat[layer, 1, b], r.jf[layer, 1])
            value = value + dot_nn(r.cat[layer, 2, b], r.jf[layer, 2])
            r.w[pl.ds(b * z.high, z.high)] = value.reshape(z.high, z.tj, z.cp)

        loop(z.own, join_part)

        def token_part(t, layer=layer):
            lines = pl.ds(t * z.step, z.step)
            value = r.w[lines] + r.u[lines] + param(layer, 11)
            r.w[lines] = value
            mean = jnp.sum(value, axis=2, keepdims=True) * (1.0 / z.channels)
            away = jnp.where(real_lane, value - mean, 0.0)
            var = jnp.sum(away * away, axis=2, keepdims=True) * (1.0 / z.channels)
            inv = lax.rsqrt(var + epsilon)
            what = away * inv
            r.what[layer, lines] = what
            r.inv[layer, lines] = jnp.broadcast_to(inv, (z.step, z.tj, LANES))
            r.yb[layer, lines] = (what * param(layer, 12) + param(layer, 13)).astype(bf16)

        loop(blocks, token_part)
        weights_ready(layer, "m")
        if layer + 1 < layers:
            weights_across(layer + 1, "j")

        def mlp_part(b, layer=layer):
            lines = pl.ds(b * z.high, z.high)
            low = r.yb[layer, lines].reshape(z.rb, z.cp)
            total = None
            for block in range(z.nkg):
                parts = slice(block * z.kg, (block + 1) * z.kg)
                rising = r.wt["m"][layer, parts, 0 : z.fl, :].reshape(z.ft, z.cp)
                hidden = dot_nt(low, rising) + r.bi[layer, block, 0:1, :]
                active, slope = gelu_both(hidden)
                r.hs[layer, block, b] = slope
                active = active.astype(bf16)
                r.gb[layer, block, b] = active
                falling = r.wt["m"][layer, parts, z.fl : 2 * z.fl, :].reshape(z.ft, z.cp)
                term = dot_nn(active, falling)
                total = term if total is None else total + term
            value = total.reshape(z.high, z.tj, z.cp) + r.w[lines] + param(layer, 14)
            value = jnp.where(real_part, value, 0.0)
            if layer + 1 < layers:
                r.x[layer + 1, b, 1 : z.high + 1] = value
            else:
                r.o[lines] = value

        real_part = lax.broadcasted_iota(jnp.int32, (z.high, z.tj, z.cp), 1) < z.wide
        loop(z.own, mlp_part)

    if layers == 1:
        take(r.cotangent, 1)
        swap_start(1)
        own_tile(1)
    slices_of(r.o, 2)
    own_tile(2)
    swap_wait(1)
    unpack(z, r.land.at[1], store_gx)

    def small_across(layer):
        arrived(("s1", layer), r.sgk.at[layer, pl.ds(0, nk - 1)])
        r.sgz[layer] = jnp.sum(r.sgk[layer], axis=0)
        r.sgi[layer, i] = r.sgz[layer]

        def one(j):
            send(("s2", layer), r.sgz.at[layer], r.sgi.at[layer, i], at(lax.rem(i + j, ni), k))

        loop(ni, one, 1)

    def small_ready(layer):
        arrived(("s2", layer), r.sgi.at[layer, pl.ds(0, ni - 1)])
        r.out_s[layer, 0:32, :] = jnp.sum(r.sgi[layer], axis=0)
        tiles = [r.mv[layer, :, LANES * tile : LANES * (tile + 1)] for tile in range(z.ct)]
        mine = jnp.zeros((8, LANES), f32)
        for part in range(nk):
            mine = mine + jnp.where(k == part, cut(tiles, part * z.cl, z.cl), 0.0)
        r.out_s[layer, 32:40, :] = mine

    for layer in reversed(range(layers)):
        above = layer + 1 if layer + 1 < layers else None

        def start_part(t, carry):
            lines = pl.ds(t * z.step, z.step)
            value = r.gx[lines]
            r.gob[lines] = value.astype(bf16)
            return carry + jnp.sum(value, axis=0)

        total = lax.fori_loop(0, blocks, start_part, jnp.zeros((z.tj, z.cp), f32))
        r.sg[12:13, :] = jnp.sum(total, axis=0, keepdims=True)
        low_out = r.gob[...].reshape(z.rows, z.cp)

        for block in range(z.nkg):
            parts = slice(block * z.kg, (block + 1) * z.kg)
            falling = r.wt["m"][layer, parts, z.fl : 2 * z.fl, :].reshape(z.ft, z.cp)
            rising = r.wt["m"][layer, parts, 0 : z.fl, :].reshape(z.ft, z.cp)

            def back_part(b, carry, layer=layer, block=block, falling=falling, rising=rising):
                lines = pl.ds(b * z.high, z.high)
                low = r.gob[lines].reshape(z.rb, z.cp)
                value = dot_nt(low, falling) * r.hs[layer, block, b]
                low = value.astype(bf16)
                r.gh[b] = low
                term = dot_nn(low, rising).reshape(z.high, z.tj, z.cp)
                r.o[lines] = term if block == 0 else r.o[lines] + term
                return carry + jnp.sum(value, axis=0, keepdims=True)

            total = lax.fori_loop(0, z.own, back_part, jnp.zeros((1, z.ft), f32))
            r.bg[0:1, block * z.ft : (block + 1) * z.ft] = total
            low_hidden = r.gh[...].reshape(z.rows, z.ft)
            low_in = r.yb[layer].reshape(z.rows, z.cp)
            value = dot_tn(low_hidden, low_in).astype(bf16).reshape(z.kg, z.fl, z.cp)
            r.gr["m"][layer, parts, 0 : z.fl, :] = value
            low_active = r.gb[layer, block].reshape(z.rows, z.ft)
            value = dot_tn(low_active, low_out).astype(bf16).reshape(z.kg, z.fl, z.cp)
            r.gr["m"][layer, parts, z.fl : 2 * z.fl, :] = value
        if z.join_kind != "m":
            reduce_pair(layer, "m")

        def token_back(t, carry, layer=layer):
            lines = pl.ds(t * z.step, z.step)
            gain_sum, bias_sum, join_sum = carry
            gy, what = r.o[lines], r.what[layer, lines]
            inv = r.inv[layer, lines][:, :, 0:1]
            scaled = gy * param(layer, 12)
            plain = jnp.sum(scaled, axis=2, keepdims=True) * (1.0 / z.channels)
            cross = jnp.sum(scaled * what, axis=2, keepdims=True) * (1.0 / z.channels)
            value = r.gx[lines] + inv * (jnp.where(real_lane, scaled - plain, 0.0) - what * cross)
            r.gw[lines] = value
            r.gsb[lines] = value.astype(bf16)
            return (
                gain_sum + jnp.sum(gy * what, axis=0),
                bias_sum + jnp.sum(gy, axis=0),
                join_sum + jnp.sum(value, axis=0),
            )

        zero = jnp.zeros((z.tj, z.cp), f32)
        gain_sum, bias_sum, join_sum = lax.fori_loop(0, blocks, token_back, (zero, zero, zero))
        r.sg[9:10, :] = jnp.sum(join_sum, axis=0, keepdims=True)
        r.sg[10:11, :] = jnp.sum(gain_sum, axis=0, keepdims=True)
        r.sg[11:12, :] = jnp.sum(bias_sum, axis=0, keepdims=True)

        low_join = r.gsb[...].reshape(z.rows, z.cp)
        for branch in range(3):
            value = dot_tn(r.cat[layer, branch].reshape(z.rows, z.cp), low_join)
            for part in range(nk):
                row = z.join_row + branch * z.clp
                r.gr[z.join_kind][layer, part, row : row + z.cl, :] = value[
                    part * z.cl : (part + 1) * z.cl
                ].astype(bf16)
        reduce_pair(layer, z.join_kind)

        def mix_back(b, carry, layer=layer):
            lines = pl.ds(b * z.high, z.high)
            low = r.gsb[lines].reshape(z.rb, z.cp)
            total = r.gw[lines].reshape(z.rb, z.cp) + dot_nt(low, r.jf[layer, 0])
            tables, sums = [], []
            for which in range(2):
                value = dot_nt(low, r.jf[layer, 1 + which])
                back = value.astype(bf16)
                total = total + dot_nn(r.mix[layer, 2 * which + 1], back)
                tables.append(carry[which] + dot_nt(back, r.cat[layer, 0, b]))
                sums.append(carry[2 + which] + jnp.sum(value, axis=1, keepdims=True))
            r.gu[lines] = total.reshape(z.high, z.tj, z.cp)
            return (*tables, *sums)

        square, column = jnp.zeros((z.rb, z.rb), f32), jnp.zeros((z.rb, 1), f32)
        rows_table, cols_table, rows_sum, cols_sum = lax.fori_loop(
            0, z.own, mix_back, (square, square, column, column)
        )

        inv_std = r.mv[layer, 2:3, :]
        mean = r.mv[layer, 0:1, :]

        def gate_back(t, carry, layer=layer, mean=mean, inv_std=inv_std):
            lines = pl.ds(t * z.step, z.step)
            value = r.gu[lines] * r.sz[layer, lines]
            r.gz[lines] = value
            centred = (r.a[layer, lines] - mean) * inv_std
            return carry[0] + jnp.sum(value, axis=0), carry[1] + jnp.sum(value * centred, axis=0)

        first, second = lax.fori_loop(0, blocks, gate_back, (zero, zero))
        first = jnp.sum(first, axis=0, keepdims=True)
        second = jnp.sum(second, axis=0, keepdims=True)
        slot = layers + layer
        for tile in range(z.ct):
            lanes = slice(LANES * tile, LANES * (tile + 1))
            r.msg[slot, tile : tile + 1, :] = first[:, lanes]
            r.msg[slot, z.ct + tile : z.ct + tile + 1, :] = second[:, lanes]
        exchange_start(slot)
        if above is None:
            swap_start(2)
        else:
            reduce_along(above, "m")
            reduce_along(above, "j")
        reduce_across(layer, "m")
        reduce_across(layer, "j")
        if above is not None:
            small_across(above)

        rows_table = jnp.where(same_wide, rows_table, 0.0).reshape(z.high, z.tj, z.rb)
        rows_table = jnp.sum(rows_table, axis=1)
        rows_table = lax.dot_general(
            rows_table, pick_high, (((1,), (0,)), ((), ())), preferred_element_type=f32, precision=lax.Precision.HIGHEST
        )
        cols_table = jnp.sum(jnp.where(same_high, cols_table, 0.0).reshape(z.high, z.tj, z.rb), axis=0)
        cols_table = lax.dot_general(
            cols_table, pick_wide, (((1,), (0,)), ((), ())), preferred_element_type=f32, precision=lax.Precision.HIGHEST
        )
        r.mg[0 : z.high, 0:16] = rows_table
        r.mg[:, 16:32] = cols_table
        r.mg[0 : z.high, 32:33] = jnp.sum(rows_sum.reshape(z.high, z.tj, 1), axis=1)
        r.mg[:, 33:34] = jnp.sum(cols_sum.reshape(z.high, z.tj, 1), axis=0)

        exchange_wait(slot)
        stats = jnp.sum(r.stats[slot], axis=0)
        bias_total = wide_row([stats[t : t + 1] for t in range(z.ct)])
        gain_total = wide_row([stats[z.ct + t : z.ct + t + 1] for t in range(z.ct)])
        r.mv[layer, 3:4, :] = gain_total
        r.mv[layer, 4:5, :] = bias_total
        factor = inv_std * param(layer, 9)
        plain = bias_total * (1.0 / z.cells)
        cross = gain_total * (1.0 / z.cells) * inv_std

        def conv_gate(b, layer=layer, mean=mean, factor=factor, plain=plain, cross=cross):
            lines = pl.ds(b * z.high, z.high)
            value = r.gz[lines] - plain - (r.a[layer, lines] - mean) * cross
            r.ga[b, 1 : z.high + 1] = jnp.where(real_part, value * factor, 0.0)

        loop(z.own, conv_gate)

        def conv_back(t, layer=layer):
            b, part = lax.div(t, z.high // z.lines), lax.rem(t, z.high // z.lines)
            start = part * z.lines
            lines = pl.ds(b * z.high + start, z.lines)
            for tile in range(z.ct):
                lanes = slice(LANES * tile, LANES * (tile + 1))
                taps = [r.pf[layer, 8 - row : 9 - row, lanes] for row in range(9)]
                value = conv(r.ga[b, pl.ds(start, z.lines + 2), :, lanes], taps)
                r.gx[lines, :, lanes] = jnp.where(inside, value + r.gu[lines, :, lanes], 0.0)

        loop(z.own * (z.high // z.lines), conv_back)

        if layer == 0:
            slices_of(r.gx, 3)
            swap_start(3)
            own_tile(3)
        if above is not None:
            spread_across(above, "m")
            spread_across(above, "j")

        for tile in range(z.ct):
            lanes = slice(LANES * tile, LANES * (tile + 1))

            def kernel_part(t, carry, layer=layer, lanes=lanes):
                b, part = lax.div(t, z.high // z.lines), lax.rem(t, z.high // z.lines)
                start = part * z.lines
                lines = r.x[layer, b, pl.ds(start, z.lines + 2), :, lanes]
                upstream = r.ga[b, pl.ds(start + 1, z.lines), :, lanes]
                shifted = (pltpu.roll(lines, 1, 1), lines, pltpu.roll(lines, z.tj - 1, 1))
                return tuple(
                    carry[3 * down + side]
                    + jnp.sum(jnp.sum(shifted[side][down : down + z.lines] * upstream, axis=0), axis=0, keepdims=True)
                    for down in range(3)
                    for side in range(3)
                )

            totals = lax.fori_loop(
                0,
                z.own * (z.high // z.lines),
                kernel_part,
                tuple(jnp.zeros((1, LANES), f32) for _ in range(9)),
            )
            for row in range(9):
                r.sg[row : row + 1, lanes] = totals[row]

        tiles = [r.sg[:, LANES * tile : LANES * (tile + 1)] for tile in range(z.ct)]
        for part in range(nk):
            r.sgm[layer, part, 0:16, :] = cut(tiles, part * z.cl, z.cl)
            for tile in range(z.ftiles):
                start = part * z.fl + LANES * tile
                width = min(LANES, z.fl - LANES * tile)
                hidden = [
                    r.bg[:, LANES * t : min(LANES * (t + 1), nk * z.fl)] for t in range(-(-nk * z.fl // LANES))
                ]
                r.sgm[layer, part, 13 + tile : 14 + tile, :] = cut(hidden, start, width)[0:1]
            r.sgm[layer, part, 16:32, :] = r.mg[...]
        r.sgk[layer, k] = r.sgm[layer, k]
        for step in range(1, nk):
            other = lax.rem(k + step, nk)
            send(("s1", layer), r.sgm.at[layer, other], r.sgk.at[layer, k], at(i, other))

    small_across(0)
    reduce_along(0, "m")
    reduce_along(0, "j")
    for layer in range(1, layers):
        spread_pair(layer, "m")
        spread_pair(layer, "j")
    spread_across(0, "m")
    spread_across(0, "j")
    swap_wait(2)
    r.out_y[...] = r.land[2]
    for layer in range(1, layers):
        small_ready(layer)
        spread_ready(layer, "m")
        spread_ready(layer, "j")
    small_ready(0)
    swap_wait(3)
    r.out_g[...] = r.land[3]
    spread_pair(0, "m")
    spread_pair(0, "j")
    spread_ready(0, "m")
    spread_ready(0, "j")

    for number, ref in sends:
        pltpu.make_async_remote_copy(
            src_ref=ref,
            dst_ref=ref,
            send_sem=ssem.at[number],
            recv_sem=rsem.at[number],
            device_id=at(partner, k),
            device_id_type=MESH,
        ).wait_send()


EVENTS = 80


def finish(z, *refs):
    count = 3 + len(z.parts)
    sources, refs = refs[:count], refs[count:]
    sem, copies, refs = refs[-1], refs[-1 - count : -1], refs[: -1 - count]
    loads = [pltpu.make_async_copy(src, dst, sem.at[n]) for n, (src, dst) in enumerate(zip(sources, copies, strict=True))]
    for load in loads:
        load.start()
    land_y, land_g, small = copies[:3]
    fins = dict(zip(z.parts, copies[3:], strict=True))
    mean_in, var_in = refs[:2]
    (output, images_grad, conv_grad, bn_gain, bn_bias, rows_grad, rows_bias, cols_grad, cols_bias, join) = refs[2:12]
    (join_bias, norm_gain, norm_bias, rising, bias_in, falling, bias_out, mean_out, var_out, tmp) = refs[12:]
    for number, land, out in ((0, land_y, output), (1, land_g, images_grad)):
        loads[number].wait()
        for k in range(z.nk):

            def group(first, tile, lines, tiles, land=land, k=k):
                source = [land[k, tile + t].astype(f32) for t in range(tiles)]
                for j in range(lines):
                    m = first + j
                    n = k * z.own + lax.div(m, z.high)
                    tmp[lax.rem(m, z.high), pl.ds(n, z.wide, stride=z.group), :] = cut(source, j * z.cl, z.cl)[: z.wide]

            line_groups(z, group)

        def line(h, carry, out=out):
            out[h] = tmp[h, :, 0 : z.cl].reshape(z.wide, z.group, z.cl).astype(out.dtype)
            return carry

        lax.fori_loop(0, z.high, line, 0)
    for load in loads[2:]:
        load.wait()
    for layer in range(z.layers):
        here = slice(layer, layer + 1)

        def row(number, layer=layer):
            return small[layer, number : number + 1, 0 : z.cl]

        for tap in range(9):
            conv_grad[tap // 3, tap % 3, here, :] = row(tap)
        join_bias[here, :] = row(9)
        norm_gain[here, :] = row(10)
        norm_bias[here, :] = row(11)
        bias_out[here, :] = row(12)
        for tile in range(z.ftiles):
            stop = min(z.fl, LANES * (tile + 1))
            bias_in[here, LANES * tile : stop] = small[layer, 13 + tile : 14 + tile, 0 : stop - LANES * tile]
        rows_grad[:, layer, :] = small[layer, 16 : 16 + z.high, 0 : z.high]
        cols_grad[:, layer, :] = small[layer, 16 : 16 + z.wide, 16 : 16 + z.wide]
        turned = small[layer, 16:32, :].T
        rows_bias[here, :] = turned[32:33, 0 : z.high]
        cols_bias[here, :] = turned[33:34, 0 : z.wide]
        mean_out[here, :] = 0.9 * mean_in[here, :] + 0.1 * row(32)
        var_out[here, :] = 0.9 * var_in[here, :] + (0.1 * z.cells / (z.cells - 1.0)) * row(33)
        bn_gain[here, :] = row(35)
        bn_bias[here, :] = row(36)
        fin = fins["m"]
        rising[layer] = fin[layer, 0 : z.fl, 0 : z.channels].astype(f32).T
        falling[layer] = fin[layer, z.fl : 2 * z.fl, 0 : z.channels].astype(f32)
        fin = fins[z.join_kind]
        for branch in range(3):
            start = z.join_row + branch * z.clp
            join[layer, branch] = fin[layer, start : start + z.cl, 0 : z.channels].astype(f32)


EVENTS = 80


def on_device(ni, nk, *args):
    first, second = (1, 2, 0, 3), (1, 0, 2)
    args = list(args)
    for number, order in ((0, first), (1, first), (18, first), (4, second), (6, second)):
        args[number] = args[number].transpose(order)
    images, conv_kernel, weight_in = args[0], args[1], args[12]
    running_mean, running_var, cotangent = args[16:19]
    z = Sizes(ni, nk, images, conv_kernel, weight_in)
    inputs = (*args[:16], cotangent)
    land = jax.ShapeDtypeStruct((nk, z.packed, z.tj, LANES), bf16)
    out_shape = (
        land,
        land,
        jax.ShapeDtypeStruct((z.layers, SMALL_ROWS, LANES), f32),
        *(jax.ShapeDtypeStruct((z.layers, ni * part, z.cp), bf16) for part in z.parts.values()),
    )
    vmem = pl.BlockSpec(memory_space=pltpu.VMEM)
    shapes, groups = scratch_list(z)
    scratch = [pltpu.VMEM(shape, kind) for table in (shapes, *groups) for shape, kind in table.values()]
    scratch += [pltpu.SemaphoreType.DMA((EVENTS,)), pltpu.SemaphoreType.DMA((EVENTS,))]
    moved = pl.pallas_call(
        functools.partial(whole, z),
        out_shape=out_shape,
        in_specs=[vmem] * len(inputs),
        out_specs=(vmem,) * len(out_shape),
        scratch_shapes=scratch,
        compiler_params=pltpu.CompilerParams(
            collective_id=0, has_side_effects=True, vmem_limit_bytes=62 * 2**20
        ),
    )(*inputs)
    lead = z.layers
    tokens = (z.high, z.wide, z.group, z.cl)
    sizes = [
        (tokens, bf16),
        (tokens, f32),
        ((3, 3, lead, z.cl), f32),
        ((lead, z.cl), f32),
        ((lead, z.cl), f32),
        ((z.high, lead, z.high), f32),
        ((lead, z.high), f32),
        ((z.wide, lead, z.wide), f32),
        ((lead, z.wide), f32),
        ((lead, 3, z.cl, z.channels), f32),
        ((lead, z.cl), f32),
        ((lead, z.cl), f32),
        ((lead, z.cl), f32),
        ((lead, z.channels, z.fl), f32),
        ((lead, z.fl), f32),
        ((lead, z.fl, z.channels), f32),
        ((lead, z.cl), f32),
        ((lead, z.cl), f32),
        ((lead, z.cl), f32),
    ]
    results = pl.pallas_call(
        functools.partial(finish, z),
        out_shape=tuple(jax.ShapeDtypeStruct(*size) for size in sizes),
        in_specs=[pl.BlockSpec(memory_space=pl.ANY)] * len(moved) + [vmem] * 2,
        out_specs=(vmem,) * len(sizes),
        scratch_shapes=[
            pltpu.VMEM((z.high, z.wide * z.group, LANES), f32),
            *(pltpu.VMEM(item.shape, item.dtype) for item in moved),
            pltpu.SemaphoreType.DMA((len(moved),)),
        ],
        compiler_params=pltpu.CompilerParams(vmem_limit_bytes=62 * 2**20),
    )(*moved, running_mean, running_var)
    results = list(results)
    for number, order in ((0, (2, 0, 1, 3)), (1, (2, 0, 1, 3)), (2, (2, 0, 1, 3)), (5, second), (7, second)):
        results[number] = results[number].transpose(order)
    return tuple(results)


def solution(mesh):
    return jax.shard_map(
        functools.partial(on_device, mesh.shape["img"], mesh.shape["ch"]),
        mesh=mesh,
        in_specs=(
            P("img", None, None, "ch"),
            P(None, None, None, "ch"),
            P(None, "ch"),
            P(None, "ch"),
            P(),
            P(),
            P(),
            P(),
            P(None, None, "ch", None),
            P(None, "ch"),
            P(None, "ch"),
            P(None, "ch"),
            P(None, None, "ch"),
            P(None, "ch"),
            P(None, "ch", None),
            P(None, "ch"),
            P(None, "ch"),
            P(None, "ch"),
            P("img", None, None, "ch"),
        ),
        out_specs=(
            P("img", None, None, "ch"),
            P("img", None, None, "ch"),
            P(None, None, None, "ch"),
            P(None, "ch"),
            P(None, "ch"),
            P(),
            P(),
            P(),
            P(),
            P(None, None, "ch", None),
            P(None, "ch"),
            P(None, "ch"),
            P(None, "ch"),
            P(None, None, "ch"),
            P(None, "ch"),
            P(None, "ch", None),
            P(None, "ch"),
            P(None, "ch"),
            P(None, "ch"),
        ),
        check_vma=False,
    )
```

```python
import functools
from types import SimpleNamespace

import jax
import jax.numpy as jnp
from jax import lax
from jax.experimental import pallas as pl
from jax.experimental.pallas import tpu as pltpu
from jax.sharding import PartitionSpec as P

f32 = jnp.float32
bf16 = jnp.bfloat16
MESH = pl.DeviceIdType.MESH
epsilon = 1e-05
LANES = 128
ROOT = 0.7978845608028654
CUBE = 0.044715


def up(number, step):
    return -(-number // step) * step


def dot_nn(left, right):
    return lax.dot_general(left, right, (((1,), (0,)), ((), ())), preferred_element_type=f32)


def dot_nt(left, right):
    return lax.dot_general(left, right, (((1,), (1,)), ((), ())), preferred_element_type=f32)


def dot_tn(left, right):
    return lax.dot_general(left, right, (((0,), (0,)), ((), ())), preferred_element_type=f32)


def gelu_both(value):
    square = value * value
    bend = jnp.tanh(value * (ROOT + (ROOT * CUBE) * square))
    half = 0.5 + 0.5 * bend
    slope = half + (0.5 * value) * (1.0 - bend * bend) * (ROOT + (3.0 * ROOT * CUBE) * square)
    return value * half, slope


def lane_index(shape):
    return lax.broadcasted_iota(jnp.int32, shape, len(shape) - 1)


def assemble(pieces, tiles):
    placed = [None] * tiles
    axis = pieces[0][0].ndim - 1
    lane = lane_index(pieces[0][0].shape)

    def add(place, value):
        placed[place] = value if placed[place] is None else placed[place] + value

    for tile, offset, width in pieces:
        first, shift = divmod(offset, LANES)
        if shift == 0:
            add(first, tile)
            continue
        turned = pltpu.roll(tile, shift, axis)
        if shift + width <= LANES:
            add(first, turned)
        else:
            add(first, jnp.where(lane >= shift, turned, 0.0))
            add(first + 1, jnp.where(lane < shift, turned, 0.0))
    return [jnp.zeros(pieces[0][0].shape, f32) if tile is None else tile for tile in placed]


def cut(tiles, offset, width):
    axis = tiles[0].ndim - 1
    lane = lane_index(tiles[0].shape)
    first, shift = divmod(offset, LANES)
    if shift == 0:
        value = tiles[first]
    else:
        value = pltpu.roll(tiles[first], LANES - shift, axis)
        if shift + width > LANES:
            value = jnp.where(lane < LANES - shift, value, pltpu.roll(tiles[first + 1], LANES - shift, axis))
    return value if width == LANES else jnp.where(lane < width, value, 0.0)


def line_groups(z, body):
    def run(g, carry):
        body(g * z.gl, g * z.gt, z.gl, z.gt)
        return carry

    if z.full:
        lax.fori_loop(0, z.full, run, 0)
    if z.rest:
        body(z.full * z.gl, z.full * z.gt, z.rest, z.rest_t)


def pack(z, stage, target, line):
    def group(first, tile, lines, tiles):
        values = assemble([(line(first + j), j * z.cl, z.cl) for j in range(lines)], tiles)
        for t in range(tiles):
            stage[target, tile + t] = values[t].astype(bf16)

    line_groups(z, group)


def unpack(z, land, store):
    def group(first, tile, lines, tiles):
        sources = [[land[k, tile + t].astype(f32) for t in range(tiles)] for k in range(z.nk)]
        for j in range(lines):
            store(
                first + j,
                assemble([(cut(source, j * z.cl, z.cl), k * z.cl, z.cl) for k, source in enumerate(sources)], z.ct),
            )

    line_groups(z, group)


class Sizes:
    def __init__(self, ni, nk, images, conv_kernel, weight_in):
        self.ni, self.nk, self.nd = ni, nk, ni * nk
        self.chips = ni // 2
        self.high, self.wide, self.group, self.cl = images.shape
        self.layers = conv_kernel.shape[2]
        self.own = self.group // nk
        self.channels = weight_in.shape[1]
        self.fl = weight_in.shape[2]
        self.tj = up(self.wide, 16)
        self.cp = up(self.channels, LANES)
        self.ct = self.cp // LANES
        self.bh = self.own * self.high
        self.rows = self.bh * self.tj
        self.rb = self.high * self.tj
        self.cells = ni * self.group * self.high * self.wide
        self.clp = up(self.cl, 16)
        def part_rows(rows):
            return up(-(-rows // ni), 16)

        join_rows, mlp_rows = 3 * self.clp, 2 * self.fl
        apart, together = part_rows(join_rows) + part_rows(mlp_rows), part_rows(join_rows + mlp_rows)
        if 4 * apart <= 5 * together:
            self.parts = {"m": part_rows(mlp_rows), "j": part_rows(join_rows)}
            self.join_kind, self.join_row = "j", 0
        else:
            self.parts = {"m": together}
            self.join_kind, self.join_row = "m", mlp_rows
        self.kg = next((n for n in range(1, nk + 1) if nk % n == 0 and n * self.fl % LANES == 0), nk)
        self.nkg = nk // self.kg
        self.ft = self.kg * self.fl
        self.ftiles = -(-self.fl // LANES)
        self.step = next(n for n in (4, 2, 1) if self.bh % n == 0)
        self.lines = next(n for n in (7, 4, 2, 1) if self.high % n == 0)
        self.stat = up(2 * self.ct, 8)
        self.gl = next(n for n in range(1, LANES + 1) if n * self.cl % LANES == 0)
        self.gt = self.gl * self.cl // LANES
        self.full, self.rest = divmod(self.bh, self.gl)
        self.rest_t = -(-self.rest * self.cl // LANES)
        self.packed = self.full * self.gt + self.rest_t


PARAM_ROWS = 16
SMALL_ROWS = 40


def scratch_list(z):
    tile = (z.packed, z.tj, LANES)
    layer, rows, cp = z.layers, z.rows, z.cp
    shapes = dict(
        tmp=((z.high, z.wide * z.group, LANES), f32),
        xl=((z.group, z.high + 2, z.tj, LANES), f32),
        al=((z.group, z.high, z.tj, LANES), f32),
        stage=((4, z.nk) + tile, bf16),
        land=((4, z.nk) + tile, bf16),
        par=((layer, PARAM_ROWS + 8, LANES), f32),
        pars=((z.nk, layer, PARAM_ROWS + 8, LANES), f32),
        pf=((layer, PARAM_ROWS, cp), f32),
        bi=((layer, z.nkg, 8, z.ft), f32),
        msg=((2 * layer, z.stat, LANES), f32),
        stats=((2 * layer, z.nd, z.stat, LANES), f32),
        jf=((layer, 3, cp, cp), bf16),
        mix=((layer, 4, z.rb, z.rb), bf16),
        mixb=((layer, 2, z.rb, 8), f32),
        mixs=((4, 16, 16), f32),
        x=((layer, z.own, z.high + 2, z.tj, cp), f32),
        a=((layer, z.bh, z.tj, cp), f32),
        sz=((layer, z.bh, z.tj, cp), f32),
        mv=((layer, 8, cp), f32),
        u=((z.bh, z.tj, cp), f32),
        cat=((layer, 3, z.own, z.rb, cp), bf16),
        w=((z.bh, z.tj, cp), f32),
        what=((layer, z.bh, z.tj, cp), f32),
        inv=((layer, z.bh, z.tj, LANES), f32),
        yb=((layer, z.bh, z.tj, cp), bf16),
        hs=((layer, z.nkg, z.own, z.rb, z.ft), f32),
        gb=((layer, z.nkg, z.own, z.rb, z.ft), bf16),
        gh=((z.own, z.rb, z.ft), bf16),
        o=((z.bh, z.tj, cp), f32),
        y=((z.bh, z.tj, cp), f32),
        gx=((z.bh, z.tj, cp), f32),
        gob=((z.bh, z.tj, cp), bf16),
        gw=((z.bh, z.tj, cp), f32),
        gsb=((z.bh, z.tj, cp), bf16),
        gpq=((2, z.own, z.rb, cp), bf16),
        gu=((z.bh, z.tj, cp), f32),
        gz=((z.bh, z.tj, cp), f32),
        ga=((z.own, z.high + 2, z.tj, cp), f32),
        sg=((PARAM_ROWS, cp), f32),
        bg=((8, z.nkg * z.ft), f32),
        mg=((16, LANES), f32),
        sgm=((layer, z.nk, 32, LANES), f32),
        sgk=((layer, z.nk, 32, LANES), f32),
        sgz=((layer, 32, LANES), f32),
        sgi=((layer, z.ni, 32, LANES), f32),
    )
    groups = []
    for part in z.parts.values():
        whole_rows = z.ni * part
        groups.append(
            dict(
                wt=((layer, z.nk, whole_rows, cp), bf16),
                gr=((layer, z.nk, whole_rows, cp), bf16),
                r1=((layer, z.chips, z.nk, part, cp), bf16),
                r2=((layer, z.chips - 1, z.nk, part, cp), bf16),
                r3=((layer, z.nk - 1, part, cp), bf16),
                fin=((layer, whole_rows, cp), bf16),
            )
        )
    return shapes, groups


def whole(z, *refs):
    inputs, refs = refs[:17], refs[17:]
    outputs, refs = refs[: 3 + len(z.parts)], refs[3 + len(z.parts) :]
    shapes, groups = scratch_list(z)
    r = SimpleNamespace(**dict(zip(shapes, refs[: len(shapes)], strict=True)))
    (r.images, r.conv_kernel, r.bn_gain, r.bn_bias, r.mix_rows, r.mix_rows_bias, r.mix_cols, r.mix_cols_bias) = inputs[:8]
    (r.join_weight, r.join_bias, r.norm_gain, r.norm_bias, r.weight_in, r.bias_in, r.weight_out, r.bias_out) = inputs[8:16]
    r.cotangent = inputs[16]
    r.out_y, r.out_g, r.out_s = outputs[:3]
    r.outs = dict(zip(z.parts, outputs[3:], strict=True))
    refs = refs[len(shapes) :]
    table = SimpleNamespace(**{name: {} for name in groups[0]})
    for kind, group in zip(z.parts, groups, strict=True):
        for name, ref in zip(group, refs[: len(group)], strict=True):
            getattr(table, name)[kind] = ref
        refs = refs[len(group) :]
    r.wt, r.gr, r.r1, r.r2, r.r3, r.fin = table.wt, table.gr, table.r1, table.r2, table.r3, table.fin
    ssem, rsem = refs
    ni, nk, nd, layers = z.ni, z.nk, z.nd, z.layers
    i = lax.axis_index("img")
    k = lax.axis_index("ch")
    core = lax.rem(i, 2)
    chip = lax.div(i, 2)
    partner = i + 1 - 2 * core
    events = {}
    sends = []

    def at(image_index, channel_index):
        return {"img": image_index, "ch": channel_index}

    def event(name):
        return events.setdefault(name, len(events))

    def send(name, src, dst, device):
        number = event(name)
        pltpu.make_async_remote_copy(
            src_ref=src,
            dst_ref=dst,
            send_sem=ssem.at[number],
            recv_sem=rsem.at[number],
            device_id=device,
            device_id_type=MESH,
        ).start()

    def arrived(name, ref):
        number = event(name)
        sends.append((number, ref))
        pltpu.make_async_remote_copy(
            src_ref=ref,
            dst_ref=ref,
            send_sem=ssem.at[number],
            recv_sem=rsem.at[number],
            device_id=at(partner, k),
            device_id_type=MESH,
        ).wait_recv()

    def loop(count, body, start=0):
        def run(index, carry):
            body(index)
            return carry

        lax.fori_loop(start, count, run, 0)

    barrier = pltpu.get_barrier_semaphore()

    def greet(j):
        pl.semaphore_signal(
            barrier,
            inc=1,
            device_id=at(lax.rem(i + lax.div(j, nk), ni), lax.rem(k + lax.rem(j, nk), nk)),
            device_id_type=MESH,
        )

    loop(nd, greet, 1)

    def exchange_start(slot):
        stats, msg = r.stats, r.msg
        mine = i * nk + k
        stats[slot, mine] = msg[slot]

        def one(j):
            send(
                ("st", slot),
                msg.at[slot],
                stats.at[slot, mine],
                at(lax.rem(i + lax.div(j, nk), ni), lax.rem(k + lax.rem(j, nk), nk)),
            )

        loop(nd, one, 1)

    def exchange_wait(slot):
        arrived(("st", slot), r.stats.at[slot, pl.ds(0, nd - 1)])

    def swap_start(slot):
        for step in range(1, nk):
            other = lax.rem(k + step, nk)
            send(("sw", slot), r.stage.at[slot, other], r.land.at[slot, k], at(i, other))

    def swap_wait(slot):
        arrived(("sw", slot), r.land.at[slot, pl.ds(0, nk - 1)])

    def own_tile(slot):
        r.land[slot, k] = r.stage[slot, k]

    def rps(kind):
        return z.parts[kind]

    def piece(number, size):
        return pl.ds(pl.multiple_of(number * size, 16), size)

    done = set()

    def once(work):
        def run(layer, kind):
            if kind in z.parts and (work, layer, kind) not in done:
                done.add((work, layer, kind))
                work(layer, kind)

        return run

    @once
    def weights_along(layer, kind):
        buffer = r.wt[kind]
        place = piece(i, rps(kind))
        for step in range(1, nk):
            ref = buffer.at[layer, k, place]
            send(("w1", layer, kind), ref, ref, at(i, lax.rem(k + step, nk)))

    @once
    def weights_across(layer, kind):
        buffer = r.wt[kind]
        size = rps(kind)
        arrived(("w1", layer, kind), buffer.at[layer, pl.ds(0, nk - 1), pl.ds(0, size)])
        for step in range(1, nk):
            ref = buffer.at[layer, lax.rem(k + step, nk), piece(i, size)]
            for turn in range(1, z.chips):
                send(("w2", layer, kind), ref, ref, at(2 * lax.rem(chip + turn, z.chips) + core, k))

    @once
    def weights_pair(layer, kind):
        buffer = r.wt[kind]
        size = rps(kind)
        arrived(("w2", layer, kind), buffer.at[layer, pl.ds(0, nk - 1), pl.ds(0, (z.chips - 1) * size)])
        for step in range(1, nk):
            for other in range(z.chips):
                ref = buffer.at[layer, lax.rem(k + step, nk), piece(2 * other + core, size)]
                send(("w3", layer, kind), ref, ref, at(partner, k))

    @once
    def weights_ready(layer, kind):
        size = rps(kind)
        arrived(("w3", layer, kind), r.wt[kind].at[layer, pl.ds(0, nk - 1), pl.ds(0, z.chips * size)])
        if kind == z.join_kind:
            for branch in range(3):
                row = z.join_row + branch * z.clp
                parts = [
                    r.wt[kind][layer, part, row : row + z.cl, :].astype(f32)
                    for part in range(nk)
                ]
                if z.cp > z.channels:
                    parts.append(jnp.zeros((z.cp - z.channels, z.cp), f32))
                r.jf[layer, branch] = jnp.concatenate(parts, axis=0).astype(bf16)

    @once
    def reduce_pair(layer, kind):
        size = rps(kind)
        for other in range(z.chips):
            send(
                ("r1", layer, kind),
                r.gr[kind].at[layer, :, piece(2 * other + 1 - core, size)],
                r.r1[kind].at[layer, other],
                at(partner, k),
            )

    @once
    def reduce_across(layer, kind):
        size = rps(kind)
        arrived(("r1", layer, kind), r.r1[kind].at[layer])
        for other in range(z.chips):
            place = piece(2 * other + core, size)

            def add(part, other=other, place=place):
                r.gr[kind][layer, part, place] = (
                    r.gr[kind][layer, part, place].astype(f32) + r.r1[kind][layer, other, part].astype(f32)
                ).astype(bf16)

            loop(nk, add)
        for turn in range(1, z.chips):
            other = lax.rem(chip + turn, z.chips)
            send(
                ("r2", layer, kind),
                r.gr[kind].at[layer, :, piece(2 * other + core, size)],
                r.r2[kind].at[layer, turn - 1],
                at(2 * other + core, k),
            )

    @once
    def reduce_along(layer, kind):
        arrived(("r2", layer, kind), r.r2[kind].at[layer])
        place = piece(i, rps(kind))

        def add(part):
            total = r.gr[kind][layer, part, place].astype(f32)
            for turn in range(z.chips - 1):
                total = total + r.r2[kind][layer, turn, part].astype(f32)
            r.gr[kind][layer, part, place] = total.astype(bf16)

        loop(nk, add)
        for step in range(1, nk):
            other = lax.rem(k + step, nk)
            send(
                ("r3", layer, kind),
                r.gr[kind].at[layer, other, place],
                r.r3[kind].at[layer, step - 1],
                at(i, other),
            )

    @once
    def spread_across(layer, kind):
        size = rps(kind)
        arrived(("r3", layer, kind), r.r3[kind].at[layer])
        place = piece(i, size)
        total = r.gr[kind][layer, k, place].astype(f32)
        for step in range(nk - 1):
            total = total + r.r3[kind][layer, step].astype(f32)
        r.fin[kind][layer, place] = total.astype(bf16)
        ref = r.fin[kind].at[layer, place]
        for turn in range(1, z.chips):
            send(("r4", layer, kind), ref, ref, at(2 * lax.rem(chip + turn, z.chips) + core, k))

    @once
    def spread_pair(layer, kind):
        size = rps(kind)
        arrived(("r4", layer, kind), r.fin[kind].at[layer, pl.ds(0, (z.chips - 1) * size)])
        for other in range(z.chips):
            ref = r.fin[kind].at[layer, piece(2 * other + core, size)]
            send(("r5", layer, kind), ref, ref, at(partner, k))

    @once
    def spread_ready(layer, kind):
        arrived(("r5", layer, kind), r.fin[kind].at[layer, pl.ds(0, z.chips * rps(kind))])
        r.outs[kind][layer] = r.fin[kind][layer]

    def clear(refs):
        for ref in refs:
            if len(ref.shape) > 3:

                def clear_one(index, ref=ref):
                    ref[index] = jnp.zeros(ref.shape[1:], ref.dtype)

                loop(ref.shape[0], clear_one)
            else:
                ref[...] = jnp.zeros(ref.shape, ref.dtype)

    clear([r.tmp, r.xl, r.par])

    tile_row = lax.broadcasted_iota(jnp.int32, (z.tj, LANES), 0)
    inside = tile_row < z.wide

    def take(ref, slot):
        def line(h):
            r.tmp[h, :, 0 : z.cl] = ref[h].astype(f32).reshape(z.wide * z.group, z.cl)
            for n in range(z.group):
                r.xl[n, h + 1, 0 : z.wide, :] = r.tmp[h, pl.ds(n, z.wide, stride=z.group), :]

        loop(z.high, line)

        def target(d):
            pack(z, r.stage.at[slot], d, lambda m: r.xl[d * z.own + lax.div(m, z.high), lax.rem(m, z.high) + 1])

        loop(nk, target)

    take(r.images, 0)

    small = [
        (9, r.bn_gain),
        (10, r.bn_bias),
        (11, r.join_bias),
        (12, r.norm_gain),
        (13, r.norm_bias),
        (14, r.bias_out),
    ]
    for row, ref in small:
        values = ref[...].astype(f32)
        for layer in range(layers):
            r.par[layer, row : row + 1, 0 : z.cl] = values[layer : layer + 1]
    values = r.bias_in[...].astype(f32)
    for layer in range(layers):
        for tap in range(3):
            for side in range(3):
                row = 3 * tap + side
                r.par[layer, row : row + 1, 0 : z.cl] = r.conv_kernel[tap, side].astype(f32)[layer : layer + 1]
        for tile in range(z.ftiles):
            stop = min(z.fl, LANES * (tile + 1))
            r.par[layer, PARAM_ROWS + tile : PARAM_ROWS + tile + 1, 0 : stop - LANES * tile] = values[
                layer : layer + 1, LANES * tile : stop
            ]

    def conv(lines, taps):
        count = lines.shape[0] - 2
        shifted = (pltpu.roll(lines, 1, 1), lines, pltpu.roll(lines, z.tj - 1, 1))
        total = None
        for down in range(3):
            for side in range(3):
                term = shifted[side][down : down + count] * taps[3 * down + side]
                total = term if total is None else total + term
        return total

    taps = [r.par[0, t : t + 1, :] for t in range(9)]

    def conv_local(n, carry):
        value = jnp.where(inside, conv(r.xl[n], taps), 0.0)
        r.al[n] = value
        return carry + jnp.sum(value, axis=0)

    local_cells = z.group * z.high * z.wide
    total = lax.fori_loop(0, z.group, conv_local, jnp.zeros((z.tj, LANES), f32))
    local_mean = jnp.sum(total, axis=0, keepdims=True) * (1.0 / local_cells)

    def square_local(n, carry):
        away = jnp.where(inside, r.al[n] - local_mean, 0.0)
        return carry + jnp.sum(away * away, axis=0)

    total = lax.fori_loop(0, z.group, square_local, jnp.zeros((z.tj, LANES), f32))
    local_var = jnp.sum(total, axis=0, keepdims=True) * (1.0 / local_cells)
    r.msg[0] = jnp.concatenate([local_mean, local_var, jnp.zeros((z.stat - 2, LANES), f32)], axis=0)

    blank = jnp.zeros((z.cl, z.cp - z.channels), f32)
    blank_hidden = jnp.zeros((z.fl, z.cp - z.channels), f32)
    for layer in range(layers):
        for kind in z.parts:
            r.wt[kind][layer, k] = jnp.zeros(r.wt[kind].shape[2:], bf16)
        for branch in range(3):
            value = r.join_weight[layer, branch].astype(f32)
            if z.cp > z.channels:
                value = jnp.concatenate([value, blank], axis=1)
            row = z.join_row + branch * z.clp
            r.wt[z.join_kind][layer, k, row : row + z.cl, :] = value.astype(bf16)
        for place, value in (
            (0, r.weight_in[layer].astype(f32).T),
            (z.fl, r.weight_out[layer].astype(f32)),
        ):
            if z.cp > z.channels:
                value = jnp.concatenate([value, blank_hidden], axis=1)
            r.wt["m"][layer, k, place : place + z.fl, :] = value.astype(bf16)

    pl.semaphore_wait(barrier, nd - 1)

    exchange_start(0)
    r.pars[k] = r.par[...]
    for step in range(1, nk):
        send("par", r.par, r.pars.at[k], at(i, lax.rem(k + step, nk)))
    weights_along(0, "j")
    weights_along(0, "m")
    swap_start(0)
    own_tile(0)

    clear([r.x, r.ga, r.pf, r.bi, r.mixs, r.mg, r.sg, r.bg, r.sgm, *r.gr.values()])

    select_row = lax.broadcasted_iota(jnp.int32, (z.rb, 16), 0)
    select_col = lax.broadcasted_iota(jnp.int32, (z.rb, 16), 1)
    pick_high = (lax.div(select_row, z.tj) == select_col).astype(f32)
    pick_wide = (lax.rem(select_row, z.tj) == select_col).astype(f32)
    low_high, low_wide = pick_high.astype(bf16), pick_wide.astype(bf16)
    full_row = lax.broadcasted_iota(jnp.int32, (z.rb, z.rb), 0)
    full_col = lax.broadcasted_iota(jnp.int32, (z.rb, z.rb), 1)
    same_wide = (lax.rem(full_row, z.tj) == lax.rem(full_col, z.tj)) & (lax.rem(full_row, z.tj) < z.wide)
    same_high = lax.div(full_row, z.tj) == lax.div(full_col, z.tj)
    for layer in range(layers):
        for which, (maps, shifts, pick, same, extent) in enumerate(
            (
                (r.mix_rows, r.mix_rows_bias, low_high, same_wide, z.high),
                (r.mix_cols, r.mix_cols_bias, low_wide, same_high, z.wide),
            )
        ):
            r.mixs[which, 0:extent, 0:extent] = maps[:, layer, :].astype(f32)
            table = r.mixs[which].astype(bf16)
            for turned, half in ((0, dot_nn(pick, table)), (1, dot_nt(pick, table))):
                spread = dot_nt(half.astype(bf16), pick)
                r.mix[layer, 2 * which + turned] = jnp.where(same, spread, 0.0).astype(bf16)
            r.mixs[2 + which, 0:1, 0:extent] = shifts[layer : layer + 1, :].astype(f32)
            r.mixb[layer, which] = dot_nt(pick, r.mixs[2 + which, 0:8, :].astype(bf16))

    weights_across(0, "j")
    weights_across(0, "m")

    exchange_wait(0)
    arrived("par", r.pars.at[pl.ds(0, nk - 1)])
    for layer in range(layers):
        tiles = assemble(
            [(r.pars[part, layer, 0:PARAM_ROWS, :], part * z.cl, z.cl) for part in range(nk)], z.ct
        )
        for tile in range(z.ct):
            r.pf[layer, :, LANES * tile : LANES * (tile + 1)] = tiles[tile]
        for block in range(z.nkg):
            pieces = []
            for part in range(z.kg):
                for tile in range(z.ftiles):
                    row = PARAM_ROWS + tile
                    value = r.pars[block * z.kg + part, layer, row : row + 1, :]
                    width = min(LANES, z.fl - LANES * tile)
                    pieces.append((jnp.broadcast_to(value, (8, LANES)), part * z.fl + LANES * tile, width))
            tiles = assemble(pieces, -(-z.ft // LANES))
            for tile, value in enumerate(tiles):
                stop = min(z.ft, LANES * (tile + 1))
                r.bi[layer, block, :, LANES * tile : stop] = value[:, 0 : stop - LANES * tile]

    def param(layer, row):
        return r.pf[layer, row : row + 1, :]

    def wide_row(tiles):
        return jnp.concatenate(tiles, axis=1)

    def combine(means, variances):
        count = means.shape[0]
        mean = jnp.sum(means, axis=0, keepdims=True) * (1.0 / count)
        away = means - mean
        var = jnp.sum(variances + away * away, axis=0, keepdims=True) * (1.0 / count)
        return mean[0], var[0]

    lane_full = lane_index((z.step, z.tj, z.cp))
    column_full = lax.broadcasted_iota(jnp.int32, (z.step, z.tj, z.cp), 1)
    real_lane = lane_full < z.channels
    real_column = column_full < z.wide
    blocks = z.bh // z.step

    def place_of(t):
        return lax.div(t, z.high), lax.rem(t, z.high)

    def store_x(m, tiles):
        for tile in range(z.ct):
            r.x[0, lax.div(m, z.high), lax.rem(m, z.high) + 1, :, LANES * tile : LANES * (tile + 1)] = tiles[tile]

    def store_gx(m, tiles):
        for tile in range(z.ct):
            r.gx[m, :, LANES * tile : LANES * (tile + 1)] = tiles[tile]

    def slices_of(ref, slot):
        for d in range(nk):

            def line(m, d=d):
                return cut([ref[m, :, LANES * t : LANES * (t + 1)] for t in range(z.ct)], d * z.cl, z.cl)

            pack(z, r.stage.at[slot], d, line)

    if layers > 1:
        weights_along(1, "j")
        weights_along(1, "m")
    swap_wait(0)
    unpack(z, r.land.at[0], store_x)

    own_cells = z.own * z.high * z.wide

    for layer in range(layers):

        def conv_part(t, carry, layer=layer):
            b, part = lax.div(t, z.high // z.lines), lax.rem(t, z.high // z.lines)
            start = part * z.lines
            sums = []
            for tile in range(z.ct):
                lanes = slice(LANES * tile, LANES * (tile + 1))
                taps = [r.pf[layer, row : row + 1, lanes] for row in range(9)]
                value = conv(r.x[layer, b, pl.ds(start, z.lines + 2), :, lanes], taps)
                value = jnp.where(inside, value, 0.0)
                r.a[layer, pl.ds(b * z.high + start, z.lines), :, lanes] = value
                sums.append(carry[tile] + jnp.sum(value, axis=0))
            return tuple(sums)

        sums = lax.fori_loop(
            0,
            z.own * (z.high // z.lines),
            conv_part,
            tuple(jnp.zeros((z.tj, LANES), f32) for _ in range(z.ct)),
        )
        if layer == 0:
            stats = r.stats[0].reshape(ni, nk, z.stat, LANES)
            whole_mean, whole_var = [], []
            for part in range(nk):
                mean, var = combine(stats[:, part, 0:1, :], stats[:, part, 1:2, :])
                whole_mean.append((jnp.broadcast_to(mean, (8, LANES)), part * z.cl, z.cl))
                whole_var.append((jnp.broadcast_to(var, (8, LANES)), part * z.cl, z.cl))
            mean = wide_row([tile[0:1] for tile in assemble(whole_mean, z.ct)])
            var = wide_row([tile[0:1] for tile in assemble(whole_var, z.ct)])
        else:
            own_mean = wide_row([jnp.sum(tile, axis=0, keepdims=True) for tile in sums]) * (1.0 / own_cells)

            def square_part(t, carry, layer=layer, own_mean=own_mean):
                value = r.a[layer, pl.ds(t * z.step, z.step)] - own_mean
                value = jnp.where(real_column, value, 0.0)
                return carry + jnp.sum(value * value, axis=0)

            squares = lax.fori_loop(0, blocks, square_part, jnp.zeros((z.tj, z.cp), f32))
            own_var = jnp.sum(squares, axis=0, keepdims=True) * (1.0 / own_cells)
            for tile in range(z.ct):
                lanes = slice(LANES * tile, LANES * (tile + 1))
                r.msg[layer, tile : tile + 1, :] = own_mean[:, lanes]
                r.msg[layer, z.ct + tile : z.ct + tile + 1, :] = own_var[:, lanes]
            exchange_start(layer)
            weights_across(layer, "j")
            weights_across(layer, "m")
            if layer == 1:
                take(r.cotangent, 1)
                swap_start(1)
                own_tile(1)
            exchange_wait(layer)
            stats = r.stats[layer]
            mean, var = combine(stats[:, 0 : z.ct, :], stats[:, z.ct : 2 * z.ct, :])
            mean = wide_row([mean[t : t + 1] for t in range(z.ct)])
            var = wide_row([var[t : t + 1] for t in range(z.ct)])
        inv_std = lax.rsqrt(var + epsilon)
        r.mv[layer, 0:1, :] = mean
        r.mv[layer, 1:2, :] = var
        r.mv[layer, 2:3, :] = inv_std
        scale = inv_std * param(layer, 9)
        shift = param(layer, 10)

        def norm_part(t, layer=layer, mean=mean, scale=scale, shift=shift):
            lines = pl.ds(t * z.step, z.step)
            active, slope = gelu_both((r.a[layer, lines] - mean) * scale + shift)
            r.sz[layer, lines] = slope
            b, start = place_of(t * z.step)
            value = jnp.where(real_column, active, 0.0)
            r.u[lines] = value

        loop(blocks, norm_part)

        def add_part(b, layer=layer):
            value = r.u[pl.ds(b * z.high, z.high)] + r.x[layer, b, 1 : z.high + 1]
            r.u[pl.ds(b * z.high, z.high)] = value
            r.cat[layer, 0, b] = value.reshape(z.rb, z.cp).astype(bf16)

        loop(z.own, add_part)
        weights_pair(layer, z.join_kind)

        def mix_part(b, layer=layer):
            low = r.cat[layer, 0, b]
            for which in range(2):
                value = dot_nn(r.mix[layer, 2 * which], low) + r.mixb[layer, which, :, 0:1]
                r.cat[layer, 1 + which, b] = value.astype(bf16)

        loop(z.own, mix_part)
        weights_ready(layer, z.join_kind)
        weights_pair(layer, "m")
        if 0 < layer < layers - 1:
            weights_along(layer + 1, "j")
            weights_along(layer + 1, "m")

        def join_part(b, layer=layer):
            value = dot_nn(r.cat[layer, 0, b], r.jf[layer, 0])
            value = value + dot_nn(r.cat[layer, 1, b], r.jf[layer, 1])
            value = value + dot_nn(r.cat[layer, 2, b], r.jf[layer, 2])
            r.w[pl.ds(b * z.high, z.high)] = value.reshape(z.high, z.tj, z.cp)

        loop(z.own, join_part)

        def token_part(t, layer=layer):
            lines = pl.ds(t * z.step, z.step)
            value = r.w[lines] + r.u[lines] + param(layer, 11)
            r.w[lines] = value
            mean = jnp.sum(value, axis=2, keepdims=True) * (1.0 / z.channels)
            away = jnp.where(real_lane, value - mean, 0.0)
            var = jnp.sum(away * away, axis=2, keepdims=True) * (1.0 / z.channels)
            inv = lax.rsqrt(var + epsilon)
            what = away * inv
            r.what[layer, lines] = what
            r.inv[layer, lines] = jnp.broadcast_to(inv, (z.step, z.tj, LANES))
            r.yb[layer, lines] = (what * param(layer, 12) + param(layer, 13)).astype(bf16)

        loop(blocks, token_part)
        weights_ready(layer, "m")
        if layer + 1 < layers:
            weights_across(layer + 1, "j")

        def mlp_part(b, layer=layer):
            lines = pl.ds(b * z.high, z.high)
            low = r.yb[layer, lines].reshape(z.rb, z.cp)
            total = None
            for block in range(z.nkg):
                parts = slice(block * z.kg, (block + 1) * z.kg)
                rising = r.wt["m"][layer, parts, 0 : z.fl, :].reshape(z.ft, z.cp)
                hidden = dot_nt(low, rising) + r.bi[layer, block, 0:1, :]
                active, slope = gelu_both(hidden)
                r.hs[layer, block, b] = slope
                active = active.astype(bf16)
                r.gb[layer, block, b] = active
                falling = r.wt["m"][layer, parts, z.fl : 2 * z.fl, :].reshape(z.ft, z.cp)
                term = dot_nn(active, falling)
                total = term if total is None else total + term
            value = total.reshape(z.high, z.tj, z.cp) + r.w[lines] + param(layer, 14)
            value = jnp.where(real_part, value, 0.0)
            if layer + 1 < layers:
                r.x[layer + 1, b, 1 : z.high + 1] = value
            else:
                r.y[lines] = value

        real_part = lax.broadcasted_iota(jnp.int32, (z.high, z.tj, z.cp), 1) < z.wide
        loop(z.own, mlp_part)

    if layers == 1:
        take(r.cotangent, 1)
        swap_start(1)
        own_tile(1)
    swap_wait(1)
    unpack(z, r.land.at[1], store_gx)

    def small_across(layer):
        arrived(("s1", layer), r.sgk.at[layer, pl.ds(0, nk - 1)])
        r.sgz[layer] = jnp.sum(r.sgk[layer], axis=0)
        r.sgi[layer, i] = r.sgz[layer]

        def one(j):
            send(("s2", layer), r.sgz.at[layer], r.sgi.at[layer, i], at(lax.rem(i + j, ni), k))

        loop(ni, one, 1)

    def small_ready(layer):
        arrived(("s2", layer), r.sgi.at[layer, pl.ds(0, ni - 1)])
        r.out_s[layer, 0:32, :] = jnp.sum(r.sgi[layer], axis=0)
        tiles = [r.mv[layer, :, LANES * tile : LANES * (tile + 1)] for tile in range(z.ct)]
        mine = jnp.zeros((8, LANES), f32)
        for part in range(nk):
            mine = mine + jnp.where(k == part, cut(tiles, part * z.cl, z.cl), 0.0)
        r.out_s[layer, 32:40, :] = mine

    for layer in reversed(range(layers)):
        above = layer + 1 if layer + 1 < layers else None

        def start_part(t, carry):
            lines = pl.ds(t * z.step, z.step)
            value = r.gx[lines]
            r.gob[lines] = value.astype(bf16)
            return carry + jnp.sum(value, axis=0)

        total = lax.fori_loop(0, blocks, start_part, jnp.zeros((z.tj, z.cp), f32))
        r.sg[12:13, :] = jnp.sum(total, axis=0, keepdims=True)
        low_out = r.gob[...].reshape(z.rows, z.cp)

        for block in range(z.nkg):
            parts = slice(block * z.kg, (block + 1) * z.kg)
            falling = r.wt["m"][layer, parts, z.fl : 2 * z.fl, :].reshape(z.ft, z.cp)
            rising = r.wt["m"][layer, parts, 0 : z.fl, :].reshape(z.ft, z.cp)

            def back_part(b, carry, layer=layer, block=block, falling=falling, rising=rising):
                lines = pl.ds(b * z.high, z.high)
                low = r.gob[lines].reshape(z.rb, z.cp)
                value = dot_nt(low, falling) * r.hs[layer, block, b]
                low = value.astype(bf16)
                r.gh[b] = low
                term = dot_nn(low, rising).reshape(z.high, z.tj, z.cp)
                r.o[lines] = term if block == 0 else r.o[lines] + term
                return carry + jnp.sum(value, axis=0, keepdims=True)

            total = lax.fori_loop(0, z.own, back_part, jnp.zeros((1, z.ft), f32))
            r.bg[0:1, block * z.ft : (block + 1) * z.ft] = total
            low_hidden = r.gh[...].reshape(z.rows, z.ft)
            low_in = r.yb[layer].reshape(z.rows, z.cp)
            value = dot_tn(low_hidden, low_in).astype(bf16).reshape(z.kg, z.fl, z.cp)
            r.gr["m"][layer, parts, 0 : z.fl, :] = value
            low_active = r.gb[layer, block].reshape(z.rows, z.ft)
            value = dot_tn(low_active, low_out).astype(bf16).reshape(z.kg, z.fl, z.cp)
            r.gr["m"][layer, parts, z.fl : 2 * z.fl, :] = value
        if z.join_kind != "m":
            reduce_pair(layer, "m")

        def token_back(t, carry, layer=layer):
            lines = pl.ds(t * z.step, z.step)
            gain_sum, bias_sum, join_sum = carry
            gy, what = r.o[lines], r.what[layer, lines]
            inv = r.inv[layer, lines][:, :, 0:1]
            scaled = gy * param(layer, 12)
            plain = jnp.sum(scaled, axis=2, keepdims=True) * (1.0 / z.channels)
            cross = jnp.sum(scaled * what, axis=2, keepdims=True) * (1.0 / z.channels)
            value = r.gx[lines] + inv * (jnp.where(real_lane, scaled - plain, 0.0) - what * cross)
            r.gw[lines] = value
            r.gsb[lines] = value.astype(bf16)
            return (
                gain_sum + jnp.sum(gy * what, axis=0),
                bias_sum + jnp.sum(gy, axis=0),
                join_sum + jnp.sum(value, axis=0),
            )

        zero = jnp.zeros((z.tj, z.cp), f32)
        gain_sum, bias_sum, join_sum = lax.fori_loop(0, blocks, token_back, (zero, zero, zero))
        r.sg[9:10, :] = jnp.sum(join_sum, axis=0, keepdims=True)
        r.sg[10:11, :] = jnp.sum(gain_sum, axis=0, keepdims=True)
        r.sg[11:12, :] = jnp.sum(bias_sum, axis=0, keepdims=True)

        def mix_back(b, layer=layer):
            lines = pl.ds(b * z.high, z.high)
            low = r.gsb[lines].reshape(z.rb, z.cp)
            total = r.gw[lines].reshape(z.rb, z.cp) + dot_nt(low, r.jf[layer, 0])
            for which in range(2):
                back = dot_nt(low, r.jf[layer, 1 + which]).astype(bf16)
                r.gpq[which, b] = back
                total = total + dot_nn(r.mix[layer, 2 * which + 1], back)
            r.gu[lines] = total.reshape(z.high, z.tj, z.cp)

        loop(z.own, mix_back)

        inv_std = r.mv[layer, 2:3, :]
        mean = r.mv[layer, 0:1, :]

        def gate_back(t, carry, layer=layer, mean=mean, inv_std=inv_std):
            lines = pl.ds(t * z.step, z.step)
            value = r.gu[lines] * r.sz[layer, lines]
            r.gz[lines] = value
            centred = (r.a[layer, lines] - mean) * inv_std
            return carry[0] + jnp.sum(value, axis=0), carry[1] + jnp.sum(value * centred, axis=0)

        first, second = lax.fori_loop(0, blocks, gate_back, (zero, zero))
        first = jnp.sum(first, axis=0, keepdims=True)
        second = jnp.sum(second, axis=0, keepdims=True)
        slot = layers + layer
        for tile in range(z.ct):
            lanes = slice(LANES * tile, LANES * (tile + 1))
            r.msg[slot, tile : tile + 1, :] = first[:, lanes]
            r.msg[slot, z.ct + tile : z.ct + tile + 1, :] = second[:, lanes]
        exchange_start(slot)
        if above is not None:
            reduce_along(above, "m")
            reduce_along(above, "j")
        if z.join_kind != "m":
            reduce_across(layer, "m")
        low_join = r.gsb[...].reshape(z.rows, z.cp)
        for branch in range(3):
            value = dot_tn(r.cat[layer, branch].reshape(z.rows, z.cp), low_join)
            for part in range(nk):
                row = z.join_row + branch * z.clp
                r.gr[z.join_kind][layer, part, row : row + z.cl, :] = value[
                    part * z.cl : (part + 1) * z.cl
                ].astype(bf16)
        reduce_pair(layer, z.join_kind)
        if above is None:
            slices_of(r.y, 2)
            swap_start(2)
            own_tile(2)

        def tables_part(b, carry, layer=layer):
            low = r.cat[layer, 0, b]
            backs = [r.gpq[which, b] for which in range(2)]
            return (
                *(carry[which] + dot_nt(backs[which], low) for which in range(2)),
                *(
                    carry[2 + which] + jnp.sum(backs[which].astype(f32), axis=1, keepdims=True)
                    for which in range(2)
                ),
            )

        square, column = jnp.zeros((z.rb, z.rb), f32), jnp.zeros((z.rb, 1), f32)
        rows_table, cols_table, rows_sum, cols_sum = lax.fori_loop(
            0, z.own, tables_part, (square, square, column, column)
        )
        reduce_across(layer, z.join_kind)
        if above is not None:
            small_across(above)

        rows_table = jnp.where(same_wide, rows_table, 0.0).reshape(z.high, z.tj, z.rb)
        rows_table = jnp.sum(rows_table, axis=1)
        rows_table = lax.dot_general(
            rows_table, pick_high, (((1,), (0,)), ((), ())), preferred_element_type=f32, precision=lax.Precision.HIGHEST
        )
        cols_table = jnp.sum(jnp.where(same_high, cols_table, 0.0).reshape(z.high, z.tj, z.rb), axis=0)
        cols_table = lax.dot_general(
            cols_table, pick_wide, (((1,), (0,)), ((), ())), preferred_element_type=f32, precision=lax.Precision.HIGHEST
        )
        r.mg[0 : z.high, 0:16] = rows_table
        r.mg[:, 16:32] = cols_table
        r.mg[0 : z.high, 32:33] = jnp.sum(rows_sum.reshape(z.high, z.tj, 1), axis=1)
        r.mg[:, 33:34] = jnp.sum(cols_sum.reshape(z.high, z.tj, 1), axis=0)

        exchange_wait(slot)
        stats = jnp.sum(r.stats[slot], axis=0)
        bias_total = wide_row([stats[t : t + 1] for t in range(z.ct)])
        gain_total = wide_row([stats[z.ct + t : z.ct + t + 1] for t in range(z.ct)])
        r.mv[layer, 3:4, :] = gain_total
        r.mv[layer, 4:5, :] = bias_total
        factor = inv_std * param(layer, 9)
        plain = bias_total * (1.0 / z.cells)
        cross = gain_total * (1.0 / z.cells) * inv_std

        def conv_gate(b, layer=layer, mean=mean, factor=factor, plain=plain, cross=cross):
            lines = pl.ds(b * z.high, z.high)
            value = r.gz[lines] - plain - (r.a[layer, lines] - mean) * cross
            r.ga[b, 1 : z.high + 1] = jnp.where(real_part, value * factor, 0.0)

        loop(z.own, conv_gate)

        def conv_back(t, layer=layer):
            b, part = lax.div(t, z.high // z.lines), lax.rem(t, z.high // z.lines)
            start = part * z.lines
            lines = pl.ds(b * z.high + start, z.lines)
            for tile in range(z.ct):
                lanes = slice(LANES * tile, LANES * (tile + 1))
                taps = [r.pf[layer, 8 - row : 9 - row, lanes] for row in range(9)]
                value = conv(r.ga[b, pl.ds(start, z.lines + 2), :, lanes], taps)
                r.gx[lines, :, lanes] = jnp.where(inside, value + r.gu[lines, :, lanes], 0.0)

        loop(z.own * (z.high // z.lines), conv_back)

        if layer == 0:
            slices_of(r.gx, 3)
            swap_start(3)
            own_tile(3)

        for tile in range(z.ct):
            lanes = slice(LANES * tile, LANES * (tile + 1))

            def kernel_part(t, carry, layer=layer, lanes=lanes):
                b, part = lax.div(t, z.high // z.lines), lax.rem(t, z.high // z.lines)
                start = part * z.lines
                lines = r.x[layer, b, pl.ds(start, z.lines + 2), :, lanes]
                upstream = r.ga[b, pl.ds(start + 1, z.lines), :, lanes]
                shifted = (pltpu.roll(lines, 1, 1), lines, pltpu.roll(lines, z.tj - 1, 1))
                return tuple(
                    carry[3 * down + side]
                    + jnp.sum(jnp.sum(shifted[side][down : down + z.lines] * upstream, axis=0), axis=0, keepdims=True)
                    for down in range(3)
                    for side in range(3)
                )

            totals = lax.fori_loop(
                0,
                z.own * (z.high // z.lines),
                kernel_part,
                tuple(jnp.zeros((1, LANES), f32) for _ in range(9)),
            )
            for row in range(9):
                r.sg[row : row + 1, lanes] = totals[row]

        tiles = [r.sg[:, LANES * tile : LANES * (tile + 1)] for tile in range(z.ct)]
        for part in range(nk):
            r.sgm[layer, part, 0:16, :] = cut(tiles, part * z.cl, z.cl)
            for tile in range(z.ftiles):
                start = part * z.fl + LANES * tile
                width = min(LANES, z.fl - LANES * tile)
                hidden = [
                    r.bg[:, LANES * t : min(LANES * (t + 1), nk * z.fl)] for t in range(-(-nk * z.fl // LANES))
                ]
                r.sgm[layer, part, 13 + tile : 14 + tile, :] = cut(hidden, start, width)[0:1]
            r.sgm[layer, part, 16:32, :] = r.mg[...]
        r.sgk[layer, k] = r.sgm[layer, k]
        for step in range(1, nk):
            other = lax.rem(k + step, nk)
            send(("s1", layer), r.sgm.at[layer, other], r.sgk.at[layer, k], at(i, other))

    for layer in range(1, layers):
        spread_across(layer, "m")
        spread_across(layer, "j")
    reduce_along(0, "m")
    reduce_along(0, "j")
    small_across(0)
    for layer in range(1, layers):
        spread_pair(layer, "m")
        spread_pair(layer, "j")
    swap_wait(2)
    r.out_y[...] = r.land[2]
    spread_across(0, "m")
    spread_across(0, "j")
    for layer in range(1, layers):
        small_ready(layer)
        spread_ready(layer, "m")
        spread_ready(layer, "j")
    swap_wait(3)
    r.out_g[...] = r.land[3]
    small_ready(0)
    spread_pair(0, "m")
    spread_pair(0, "j")
    spread_ready(0, "m")
    spread_ready(0, "j")

    for number, ref in sends:
        pltpu.make_async_remote_copy(
            src_ref=ref,
            dst_ref=ref,
            send_sem=ssem.at[number],
            recv_sem=rsem.at[number],
            device_id=at(partner, k),
            device_id_type=MESH,
        ).wait_send()


EVENTS = 80


def finish(z, *refs):
    count = 3 + len(z.parts)
    sources, refs = refs[:count], refs[count:]
    sem, copies, refs = refs[-1], refs[-1 - count : -1], refs[: -1 - count]
    loads = [pltpu.make_async_copy(src, dst, sem.at[n]) for n, (src, dst) in enumerate(zip(sources, copies, strict=True))]
    for load in loads:
        load.start()
    land_y, land_g, small = copies[:3]
    fins = dict(zip(z.parts, copies[3:], strict=True))
    mean_in, var_in = refs[:2]
    (output, images_grad, conv_grad, bn_gain, bn_bias, rows_grad, rows_bias, cols_grad, cols_bias, join) = refs[2:12]
    (join_bias, norm_gain, norm_bias, rising, bias_in, falling, bias_out, mean_out, var_out, tmp) = refs[12:]
    for number, land, out in ((0, land_y, output), (1, land_g, images_grad)):
        loads[number].wait()
        for k in range(z.nk):

            def group(first, tile, lines, tiles, land=land, k=k):
                source = [land[k, tile + t].astype(f32) for t in range(tiles)]
                for j in range(lines):
                    m = first + j
                    n = k * z.own + lax.div(m, z.high)
                    tmp[lax.rem(m, z.high), pl.ds(n, z.wide, stride=z.group), :] = cut(source, j * z.cl, z.cl)[: z.wide]

            line_groups(z, group)

        def line(h, carry, out=out):
            out[h] = tmp[h, :, 0 : z.cl].reshape(z.wide, z.group, z.cl).astype(out.dtype)
            return carry

        lax.fori_loop(0, z.high, line, 0)
    for load in loads[2:]:
        load.wait()
    for layer in range(z.layers):
        here = slice(layer, layer + 1)

        def row(number, layer=layer):
            return small[layer, number : number + 1, 0 : z.cl]

        for tap in range(9):
            conv_grad[tap // 3, tap % 3, here, :] = row(tap)
        join_bias[here, :] = row(9)
        norm_gain[here, :] = row(10)
        norm_bias[here, :] = row(11)
        bias_out[here, :] = row(12)
        for tile in range(z.ftiles):
            stop = min(z.fl, LANES * (tile + 1))
            bias_in[here, LANES * tile : stop] = small[layer, 13 + tile : 14 + tile, 0 : stop - LANES * tile]
        rows_grad[:, layer, :] = small[layer, 16 : 16 + z.high, 0 : z.high]
        cols_grad[:, layer, :] = small[layer, 16 : 16 + z.wide, 16 : 16 + z.wide]
        turned = small[layer, 16:32, :].T
        rows_bias[here, :] = turned[32:33, 0 : z.high]
        cols_bias[here, :] = turned[33:34, 0 : z.wide]
        mean_out[here, :] = 0.9 * mean_in[here, :] + 0.1 * row(32)
        var_out[here, :] = 0.9 * var_in[here, :] + (0.1 * z.cells / (z.cells - 1.0)) * row(33)
        bn_gain[here, :] = row(35)
        bn_bias[here, :] = row(36)
        fin = fins["m"]
        rising[layer] = fin[layer, 0 : z.fl, 0 : z.channels].astype(f32).T
        falling[layer] = fin[layer, z.fl : 2 * z.fl, 0 : z.channels].astype(f32)
        fin = fins[z.join_kind]
        for branch in range(3):
            start = z.join_row + branch * z.clp
            join[layer, branch] = fin[layer, start : start + z.cl, 0 : z.channels].astype(f32)


EVENTS = 80


def on_device(ni, nk, *args):
    first, second = (1, 2, 0, 3), (1, 0, 2)
    args = list(args)
    for number, order in ((0, first), (1, first), (18, first), (4, second), (6, second)):
        args[number] = args[number].transpose(order)
    images, conv_kernel, weight_in = args[0], args[1], args[12]
    running_mean, running_var, cotangent = args[16:19]
    z = Sizes(ni, nk, images, conv_kernel, weight_in)
    inputs = (*args[:16], cotangent)
    land = jax.ShapeDtypeStruct((nk, z.packed, z.tj, LANES), bf16)
    out_shape = (
        land,
        land,
        jax.ShapeDtypeStruct((z.layers, SMALL_ROWS, LANES), f32),
        *(jax.ShapeDtypeStruct((z.layers, ni * part, z.cp), bf16) for part in z.parts.values()),
    )
    vmem = pl.BlockSpec(memory_space=pltpu.VMEM)
    shapes, groups = scratch_list(z)
    scratch = [pltpu.VMEM(shape, kind) for table in (shapes, *groups) for shape, kind in table.values()]
    scratch += [pltpu.SemaphoreType.DMA((EVENTS,)), pltpu.SemaphoreType.DMA((EVENTS,))]
    moved = pl.pallas_call(
        functools.partial(whole, z),
        out_shape=out_shape,
        in_specs=[vmem] * len(inputs),
        out_specs=(vmem,) * len(out_shape),
        scratch_shapes=scratch,
        compiler_params=pltpu.CompilerParams(
            collective_id=0, has_side_effects=True, vmem_limit_bytes=62 * 2**20
        ),
    )(*inputs)
    lead = z.layers
    tokens = (z.high, z.wide, z.group, z.cl)
    sizes = [
        (tokens, bf16),
        (tokens, f32),
        ((3, 3, lead, z.cl), f32),
        ((lead, z.cl), f32),
        ((lead, z.cl), f32),
        ((z.high, lead, z.high), f32),
        ((lead, z.high), f32),
        ((z.wide, lead, z.wide), f32),
        ((lead, z.wide), f32),
        ((lead, 3, z.cl, z.channels), f32),
        ((lead, z.cl), f32),
        ((lead, z.cl), f32),
        ((lead, z.cl), f32),
        ((lead, z.channels, z.fl), f32),
        ((lead, z.fl), f32),
        ((lead, z.fl, z.channels), f32),
        ((lead, z.cl), f32),
        ((lead, z.cl), f32),
        ((lead, z.cl), f32),
    ]
    results = pl.pallas_call(
        functools.partial(finish, z),
        out_shape=tuple(jax.ShapeDtypeStruct(*size) for size in sizes),
        in_specs=[pl.BlockSpec(memory_space=pl.ANY)] * len(moved) + [vmem] * 2,
        out_specs=(vmem,) * len(sizes),
        scratch_shapes=[
            pltpu.VMEM((z.high, z.wide * z.group, LANES), f32),
            *(pltpu.VMEM(item.shape, item.dtype) for item in moved),
            pltpu.SemaphoreType.DMA((len(moved),)),
        ],
        compiler_params=pltpu.CompilerParams(vmem_limit_bytes=62 * 2**20),
    )(*moved, running_mean, running_var)
    results = list(results)
    for number, order in ((0, (2, 0, 1, 3)), (1, (2, 0, 1, 3)), (2, (2, 0, 1, 3)), (5, second), (7, second)):
        results[number] = results[number].transpose(order)
    return tuple(results)


def solution(mesh):
    return jax.shard_map(
        functools.partial(on_device, mesh.shape["img"], mesh.shape["ch"]),
        mesh=mesh,
        in_specs=(
            P("img", None, None, "ch"),
            P(None, None, None, "ch"),
            P(None, "ch"),
            P(None, "ch"),
            P(),
            P(),
            P(),
            P(),
            P(None, None, "ch", None),
            P(None, "ch"),
            P(None, "ch"),
            P(None, "ch"),
            P(None, None, "ch"),
            P(None, "ch"),
            P(None, "ch", None),
            P(None, "ch"),
            P(None, "ch"),
            P(None, "ch"),
            P("img", None, None, "ch"),
        ),
        out_specs=(
            P("img", None, None, "ch"),
            P("img", None, None, "ch"),
            P(None, None, None, "ch"),
            P(None, "ch"),
            P(None, "ch"),
            P(),
            P(),
            P(),
            P(),
            P(None, None, "ch", None),
            P(None, "ch"),
            P(None, "ch"),
            P(None, "ch"),
            P(None, None, "ch"),
            P(None, "ch"),
            P(None, "ch", None),
            P(None, "ch"),
            P(None, "ch"),
            P(None, "ch"),
        ),
        check_vma=False,
    )
```

```python
import functools
from types import SimpleNamespace

import jax
import jax.numpy as jnp
from jax import lax
from jax.experimental import pallas as pl
from jax.experimental.pallas import tpu as pltpu
from jax.sharding import PartitionSpec as P

f32 = jnp.float32
bf16 = jnp.bfloat16
MESH = pl.DeviceIdType.MESH
epsilon = 1e-05
LANES = 128
ROOT = 0.7978845608028654
CUBE = 0.044715


def up(number, step):
    return -(-number // step) * step


def dot_nn(left, right):
    return lax.dot_general(left, right, (((1,), (0,)), ((), ())), preferred_element_type=f32)


def dot_nt(left, right):
    return lax.dot_general(left, right, (((1,), (1,)), ((), ())), preferred_element_type=f32)


def dot_tn(left, right):
    return lax.dot_general(left, right, (((0,), (0,)), ((), ())), preferred_element_type=f32)


def gelu_both(value):
    square = value * value
    bend = jnp.tanh(value * (ROOT + (ROOT * CUBE) * square))
    half = 0.5 + 0.5 * bend
    slope = half + (0.5 * value) * (1.0 - bend * bend) * (ROOT + (3.0 * ROOT * CUBE) * square)
    return value * half, slope


def lane_index(shape):
    return lax.broadcasted_iota(jnp.int32, shape, len(shape) - 1)


def assemble(pieces, tiles):
    placed = [None] * tiles
    axis = pieces[0][0].ndim - 1
    lane = lane_index(pieces[0][0].shape)

    def add(place, value):
        placed[place] = value if placed[place] is None else placed[place] + value

    for tile, offset, width in pieces:
        first, shift = divmod(offset, LANES)
        if shift == 0:
            add(first, tile)
            continue
        turned = pltpu.roll(tile, shift, axis)
        if shift + width <= LANES:
            add(first, turned)
        else:
            add(first, jnp.where(lane >= shift, turned, 0.0))
            add(first + 1, jnp.where(lane < shift, turned, 0.0))
    return [jnp.zeros(pieces[0][0].shape, f32) if tile is None else tile for tile in placed]


def cut(tiles, offset, width):
    axis = tiles[0].ndim - 1
    lane = lane_index(tiles[0].shape)
    first, shift = divmod(offset, LANES)
    if shift == 0:
        value = tiles[first]
    else:
        value = pltpu.roll(tiles[first], LANES - shift, axis)
        if shift + width > LANES:
            value = jnp.where(lane < LANES - shift, value, pltpu.roll(tiles[first + 1], LANES - shift, axis))
    return value if width == LANES else jnp.where(lane < width, value, 0.0)


def line_groups(z, body):
    def run(g, carry):
        body(g * z.gl, g * z.gt, z.gl, z.gt)
        return carry

    if z.full:
        lax.fori_loop(0, z.full, run, 0)
    if z.rest:
        body(z.full * z.gl, z.full * z.gt, z.rest, z.rest_t)


def pack(z, stage, target, line):
    def group(first, tile, lines, tiles):
        values = assemble([(line(first + j), j * z.cl, z.cl) for j in range(lines)], tiles)
        for t in range(tiles):
            stage[target, tile + t] = values[t].astype(bf16)

    line_groups(z, group)


def unpack(z, land, store):
    def group(first, tile, lines, tiles):
        sources = [[land[k, tile + t].astype(f32) for t in range(tiles)] for k in range(z.nk)]
        for j in range(lines):
            store(
                first + j,
                assemble([(cut(source, j * z.cl, z.cl), k * z.cl, z.cl) for k, source in enumerate(sources)], z.ct),
            )

    line_groups(z, group)


class Sizes:
    def __init__(self, ni, nk, images, conv_kernel, weight_in):
        self.ni, self.nk, self.nd = ni, nk, ni * nk
        self.chips = ni // 2
        self.high, self.wide, self.group, self.cl = images.shape
        self.layers = conv_kernel.shape[2]
        self.own = self.group // nk
        self.channels = weight_in.shape[1]
        self.fl = weight_in.shape[2]
        self.tj = up(self.wide, 16)
        self.cp = up(self.channels, LANES)
        self.ct = self.cp // LANES
        self.bh = self.own * self.high
        self.rows = self.bh * self.tj
        self.rb = self.high * self.tj
        self.cells = ni * self.group * self.high * self.wide
        self.clp = up(self.cl, 16)
        def part_rows(rows):
            return up(-(-rows // ni), 16)

        join_rows, mlp_rows = 3 * self.clp, 2 * self.fl
        apart, together = part_rows(join_rows) + part_rows(mlp_rows), part_rows(join_rows + mlp_rows)
        if 4 * apart <= 5 * together:
            self.parts = {"m": part_rows(mlp_rows), "j": part_rows(join_rows)}
            self.join_kind, self.join_row = "j", 0
        else:
            self.parts = {"m": together}
            self.join_kind, self.join_row = "m", mlp_rows
        self.kg = next((n for n in range(1, nk + 1) if nk % n == 0 and n * self.fl % LANES == 0), nk)
        self.nkg = nk // self.kg
        self.ft = self.kg * self.fl
        self.ftiles = -(-self.fl // LANES)
        self.step = next(n for n in (4, 2, 1) if self.bh % n == 0)
        self.lines = next(n for n in (7, 4, 2, 1) if self.high % n == 0)
        self.stat = up(2 * self.ct, 8)
        self.gl = next(n for n in range(1, LANES + 1) if n * self.cl % LANES == 0)
        self.gt = self.gl * self.cl // LANES
        self.full, self.rest = divmod(self.bh, self.gl)
        self.rest_t = -(-self.rest * self.cl // LANES)
        self.packed = self.full * self.gt + self.rest_t


PARAM_ROWS = 16
SMALL_ROWS = 40


def scratch_list(z):
    tile = (z.packed, z.tj, LANES)
    layer, rows, cp = z.layers, z.rows, z.cp
    shapes = dict(
        tmp=((z.high, z.wide * z.group, LANES), f32),
        fy=((z.high, z.wide, z.group, z.cl), bf16),
        fg=((z.high, z.wide, z.group, z.cl), f32),
        xl=((z.group, z.high + 2, z.tj, LANES), f32),
        al=((z.group, z.high, z.tj, LANES), f32),
        stage=((4, z.nk) + tile, bf16),
        land=((4, z.nk) + tile, bf16),
        par=((layer, PARAM_ROWS + 8, LANES), f32),
        pars=((z.nk, layer, PARAM_ROWS + 8, LANES), f32),
        pf=((layer, PARAM_ROWS, cp), f32),
        bi=((layer, z.nkg, 8, z.ft), f32),
        msg=((2 * layer, z.stat, LANES), f32),
        stats=((2 * layer, z.nd, z.stat, LANES), f32),
        jf=((layer, 3, cp, cp), bf16),
        mix=((layer, 4, z.rb, z.rb), bf16),
        mixb=((layer, 2, z.rb, 8), f32),
        mixs=((4, 16, 16), f32),
        x=((layer, z.own, z.high + 2, z.tj, cp), f32),
        a=((layer, z.bh, z.tj, cp), f32),
        sz=((layer, z.bh, z.tj, cp), f32),
        mv=((layer, 8, cp), f32),
        u=((z.bh, z.tj, cp), f32),
        cat=((layer, 3, z.own, z.rb, cp), bf16),
        w=((z.bh, z.tj, cp), f32),
        what=((layer, z.bh, z.tj, cp), f32),
        inv=((layer, z.bh, z.tj, LANES), f32),
        yb=((layer, z.bh, z.tj, cp), bf16),
        hs=((layer, z.nkg, z.own, z.rb, z.ft), f32),
        gb=((layer, z.nkg, z.own, z.rb, z.ft), bf16),
        gh=((z.own, z.rb, z.ft), bf16),
        o=((z.bh, z.tj, cp), f32),
        y=((z.bh, z.tj, cp), f32),
        gx=((z.bh, z.tj, cp), f32),
        gob=((z.bh, z.tj, cp), bf16),
        gw=((z.bh, z.tj, cp), f32),
        gsb=((z.bh, z.tj, cp), bf16),
        gpq=((2, z.own, z.rb, cp), bf16),
        gu=((z.bh, z.tj, cp), f32),
        gz=((z.bh, z.tj, cp), f32),
        ga=((z.own, z.high + 2, z.tj, cp), f32),
        sg=((PARAM_ROWS, cp), f32),
        bg=((8, z.nkg * z.ft), f32),
        mg=((16, LANES), f32),
        sgm=((layer, z.nk, 32, LANES), f32),
        sgk=((layer, z.nk, 32, LANES), f32),
        sgz=((layer, 32, LANES), f32),
        sgi=((layer, z.ni, 32, LANES), f32),
    )
    groups = []
    for part in z.parts.values():
        whole_rows = z.ni * part
        groups.append(
            dict(
                wt=((layer, z.nk, whole_rows, cp), bf16),
                gr=((layer, z.nk, whole_rows, cp), bf16),
                r1=((layer, z.chips, z.nk, part, cp), bf16),
                r2=((layer, z.chips - 1, z.nk, part, cp), bf16),
                r3=((layer, z.nk - 1, part, cp), bf16),
                fin=((layer, whole_rows, cp), bf16),
            )
        )
    return shapes, groups


def whole(z, *refs):
    inputs, refs = refs[:17], refs[17:]
    outputs, refs = refs[: 3 + len(z.parts)], refs[3 + len(z.parts) :]
    shapes, groups = scratch_list(z)
    r = SimpleNamespace(**dict(zip(shapes, refs[: len(shapes)], strict=True)))
    (r.images, r.conv_kernel, r.bn_gain, r.bn_bias, r.mix_rows, r.mix_rows_bias, r.mix_cols, r.mix_cols_bias) = inputs[:8]
    (r.join_weight, r.join_bias, r.norm_gain, r.norm_bias, r.weight_in, r.bias_in, r.weight_out, r.bias_out) = inputs[8:16]
    r.cotangent = inputs[16]
    r.out_y, r.out_g, r.out_s = outputs[:3]
    r.outs = dict(zip(z.parts, outputs[3:], strict=True))
    refs = refs[len(shapes) :]
    table = SimpleNamespace(**{name: {} for name in groups[0]})
    for kind, group in zip(z.parts, groups, strict=True):
        for name, ref in zip(group, refs[: len(group)], strict=True):
            getattr(table, name)[kind] = ref
        refs = refs[len(group) :]
    r.wt, r.gr, r.r1, r.r2, r.r3, r.fin = table.wt, table.gr, table.r1, table.r2, table.r3, table.fin
    ssem, rsem, osem = refs
    ni, nk, nd, layers = z.ni, z.nk, z.nd, z.layers
    i = lax.axis_index("img")
    k = lax.axis_index("ch")
    core = lax.rem(i, 2)
    chip = lax.div(i, 2)
    partner = i + 1 - 2 * core
    events = {}
    sends = []
    stores = []

    def at(image_index, channel_index):
        return {"img": image_index, "ch": channel_index}

    def event(name):
        return events.setdefault(name, len(events))

    def send(name, src, dst, device):
        number = event(name)
        pltpu.make_async_remote_copy(
            src_ref=src,
            dst_ref=dst,
            send_sem=ssem.at[number],
            recv_sem=rsem.at[number],
            device_id=device,
            device_id_type=MESH,
        ).start()

    def arrived(name, ref):
        number = event(name)
        sends.append((number, ref))
        pltpu.make_async_remote_copy(
            src_ref=ref,
            dst_ref=ref,
            send_sem=ssem.at[number],
            recv_sem=rsem.at[number],
            device_id=at(partner, k),
            device_id_type=MESH,
        ).wait_recv()

    def store(src, dst):
        copy = pltpu.make_async_copy(src, dst, osem.at[len(stores)])
        stores.append(copy)
        copy.start()

    def loop(count, body, start=0):
        def run(index, carry):
            body(index)
            return carry

        lax.fori_loop(start, count, run, 0)

    barrier = pltpu.get_barrier_semaphore()

    def greet(j):
        pl.semaphore_signal(
            barrier,
            inc=1,
            device_id=at(lax.rem(i + lax.div(j, nk), ni), lax.rem(k + lax.rem(j, nk), nk)),
            device_id_type=MESH,
        )

    loop(nd, greet, 1)

    def exchange_start(slot):
        stats, msg = r.stats, r.msg
        mine = i * nk + k
        stats[slot, mine] = msg[slot]

        def one(j):
            send(
                ("st", slot),
                msg.at[slot],
                stats.at[slot, mine],
                at(lax.rem(i + lax.div(j, nk), ni), lax.rem(k + lax.rem(j, nk), nk)),
            )

        loop(nd, one, 1)

    def exchange_wait(slot):
        arrived(("st", slot), r.stats.at[slot, pl.ds(0, nd - 1)])

    def swap_start(slot):
        for step in range(1, nk):
            other = lax.rem(k + step, nk)
            send(("sw", slot), r.stage.at[slot, other], r.land.at[slot, k], at(i, other))

    def swap_wait(slot):
        arrived(("sw", slot), r.land.at[slot, pl.ds(0, nk - 1)])

    def own_tile(slot):
        r.land[slot, k] = r.stage[slot, k]

    def rps(kind):
        return z.parts[kind]

    def piece(number, size):
        return pl.ds(pl.multiple_of(number * size, 16), size)

    done = set()

    def once(work):
        def run(layer, kind):
            if kind in z.parts and (work, layer, kind) not in done:
                done.add((work, layer, kind))
                work(layer, kind)

        return run

    @once
    def weights_along(layer, kind):
        buffer = r.wt[kind]
        place = piece(i, rps(kind))
        for step in range(1, nk):
            ref = buffer.at[layer, k, place]
            send(("w1", layer, kind), ref, ref, at(i, lax.rem(k + step, nk)))

    @once
    def weights_across(layer, kind):
        buffer = r.wt[kind]
        size = rps(kind)
        arrived(("w1", layer, kind), buffer.at[layer, pl.ds(0, nk - 1), pl.ds(0, size)])
        for step in range(1, nk):
            ref = buffer.at[layer, lax.rem(k + step, nk), piece(i, size)]
            for turn in range(1, z.chips):
                send(("w2", layer, kind), ref, ref, at(2 * lax.rem(chip + turn, z.chips) + core, k))

    @once
    def weights_pair(layer, kind):
        buffer = r.wt[kind]
        size = rps(kind)
        arrived(("w2", layer, kind), buffer.at[layer, pl.ds(0, nk - 1), pl.ds(0, (z.chips - 1) * size)])
        for step in range(1, nk):
            for other in range(z.chips):
                ref = buffer.at[layer, lax.rem(k + step, nk), piece(2 * other + core, size)]
                send(("w3", layer, kind), ref, ref, at(partner, k))

    @once
    def weights_ready(layer, kind):
        size = rps(kind)
        arrived(("w3", layer, kind), r.wt[kind].at[layer, pl.ds(0, nk - 1), pl.ds(0, z.chips * size)])
        if kind == z.join_kind:
            for branch in range(3):
                row = z.join_row + branch * z.clp
                parts = [
                    r.wt[kind][layer, part, row : row + z.cl, :].astype(f32)
                    for part in range(nk)
                ]
                if z.cp > z.channels:
                    parts.append(jnp.zeros((z.cp - z.channels, z.cp), f32))
                r.jf[layer, branch] = jnp.concatenate(parts, axis=0).astype(bf16)

    @once
    def reduce_pair(layer, kind):
        size = rps(kind)
        for other in range(z.chips):
            send(
                ("r1", layer, kind),
                r.gr[kind].at[layer, :, piece(2 * other + 1 - core, size)],
                r.r1[kind].at[layer, other],
                at(partner, k),
            )

    @once
    def reduce_across(layer, kind):
        size = rps(kind)
        arrived(("r1", layer, kind), r.r1[kind].at[layer])
        for other in range(z.chips):
            place = piece(2 * other + core, size)

            def add(part, other=other, place=place):
                r.gr[kind][layer, part, place] = (
                    r.gr[kind][layer, part, place].astype(f32) + r.r1[kind][layer, other, part].astype(f32)
                ).astype(bf16)

            loop(nk, add)
        for turn in range(1, z.chips):
            other = lax.rem(chip + turn, z.chips)
            send(
                ("r2", layer, kind),
                r.gr[kind].at[layer, :, piece(2 * other + core, size)],
                r.r2[kind].at[layer, turn - 1],
                at(2 * other + core, k),
            )

    @once
    def reduce_along(layer, kind):
        arrived(("r2", layer, kind), r.r2[kind].at[layer])
        place = piece(i, rps(kind))

        def add(part):
            total = r.gr[kind][layer, part, place].astype(f32)
            for turn in range(z.chips - 1):
                total = total + r.r2[kind][layer, turn, part].astype(f32)
            r.gr[kind][layer, part, place] = total.astype(bf16)

        loop(nk, add)
        for step in range(1, nk):
            other = lax.rem(k + step, nk)
            send(
                ("r3", layer, kind),
                r.gr[kind].at[layer, other, place],
                r.r3[kind].at[layer, step - 1],
                at(i, other),
            )

    @once
    def spread_across(layer, kind):
        size = rps(kind)
        arrived(("r3", layer, kind), r.r3[kind].at[layer])
        place = piece(i, size)
        total = r.gr[kind][layer, k, place].astype(f32)
        for step in range(nk - 1):
            total = total + r.r3[kind][layer, step].astype(f32)
        r.fin[kind][layer, place] = total.astype(bf16)
        ref = r.fin[kind].at[layer, place]
        for turn in range(1, z.chips):
            send(("r4", layer, kind), ref, ref, at(2 * lax.rem(chip + turn, z.chips) + core, k))

    @once
    def spread_pair(layer, kind):
        size = rps(kind)
        arrived(("r4", layer, kind), r.fin[kind].at[layer, pl.ds(0, (z.chips - 1) * size)])
        for other in range(z.chips):
            ref = r.fin[kind].at[layer, piece(2 * other + core, size)]
            send(("r5", layer, kind), ref, ref, at(partner, k))

    @once
    def spread_ready(layer, kind):
        arrived(("r5", layer, kind), r.fin[kind].at[layer, pl.ds(0, z.chips * rps(kind))])
        store(r.fin[kind].at[layer], r.outs[kind].at[layer])

    def clear(refs):
        for ref in refs:
            if len(ref.shape) > 3:

                def clear_one(index, ref=ref):
                    ref[index] = jnp.zeros(ref.shape[1:], ref.dtype)

                loop(ref.shape[0], clear_one)
            else:
                ref[...] = jnp.zeros(ref.shape, ref.dtype)

    clear([r.tmp, r.xl, r.par])

    tile_row = lax.broadcasted_iota(jnp.int32, (z.tj, LANES), 0)
    inside = tile_row < z.wide

    def take(ref, slot):
        def line(h):
            r.tmp[h, :, 0 : z.cl] = ref[h].astype(f32).reshape(z.wide * z.group, z.cl)
            for n in range(z.group):
                r.xl[n, h + 1, 0 : z.wide, :] = r.tmp[h, pl.ds(n, z.wide, stride=z.group), :]

        loop(z.high, line)

        def target(d):
            pack(z, r.stage.at[slot], d, lambda m: r.xl[d * z.own + lax.div(m, z.high), lax.rem(m, z.high) + 1])

        loop(nk, target)

    take(r.images, 0)

    small = [
        (9, r.bn_gain),
        (10, r.bn_bias),
        (11, r.join_bias),
        (12, r.norm_gain),
        (13, r.norm_bias),
        (14, r.bias_out),
    ]
    for row, ref in small:
        values = ref[...].astype(f32)
        for layer in range(layers):
            r.par[layer, row : row + 1, 0 : z.cl] = values[layer : layer + 1]
    values = r.bias_in[...].astype(f32)
    for layer in range(layers):
        for tap in range(3):
            for side in range(3):
                row = 3 * tap + side
                r.par[layer, row : row + 1, 0 : z.cl] = r.conv_kernel[tap, side].astype(f32)[layer : layer + 1]
        for tile in range(z.ftiles):
            stop = min(z.fl, LANES * (tile + 1))
            r.par[layer, PARAM_ROWS + tile : PARAM_ROWS + tile + 1, 0 : stop - LANES * tile] = values[
                layer : layer + 1, LANES * tile : stop
            ]

    def conv(lines, taps):
        count = lines.shape[0] - 2
        shifted = (pltpu.roll(lines, 1, 1), lines, pltpu.roll(lines, z.tj - 1, 1))
        total = None
        for down in range(3):
            for side in range(3):
                term = shifted[side][down : down + count] * taps[3 * down + side]
                total = term if total is None else total + term
        return total

    taps = [r.par[0, t : t + 1, :] for t in range(9)]

    def conv_local(n, carry):
        value = jnp.where(inside, conv(r.xl[n], taps), 0.0)
        r.al[n] = value
        return carry + jnp.sum(value, axis=0)

    local_cells = z.group * z.high * z.wide
    total = lax.fori_loop(0, z.group, conv_local, jnp.zeros((z.tj, LANES), f32))
    local_mean = jnp.sum(total, axis=0, keepdims=True) * (1.0 / local_cells)

    def square_local(n, carry):
        away = jnp.where(inside, r.al[n] - local_mean, 0.0)
        return carry + jnp.sum(away * away, axis=0)

    total = lax.fori_loop(0, z.group, square_local, jnp.zeros((z.tj, LANES), f32))
    local_var = jnp.sum(total, axis=0, keepdims=True) * (1.0 / local_cells)
    r.msg[0] = jnp.concatenate([local_mean, local_var, jnp.zeros((z.stat - 2, LANES), f32)], axis=0)

    blank = jnp.zeros((z.cl, z.cp - z.channels), f32)
    blank_hidden = jnp.zeros((z.fl, z.cp - z.channels), f32)
    for layer in range(layers):
        for kind in z.parts:
            r.wt[kind][layer, k] = jnp.zeros(r.wt[kind].shape[2:], bf16)
        for branch in range(3):
            value = r.join_weight[layer, branch].astype(f32)
            if z.cp > z.channels:
                value = jnp.concatenate([value, blank], axis=1)
            row = z.join_row + branch * z.clp
            r.wt[z.join_kind][layer, k, row : row + z.cl, :] = value.astype(bf16)
        for place, value in (
            (0, r.weight_in[layer].astype(f32).T),
            (z.fl, r.weight_out[layer].astype(f32)),
        ):
            if z.cp > z.channels:
                value = jnp.concatenate([value, blank_hidden], axis=1)
            r.wt["m"][layer, k, place : place + z.fl, :] = value.astype(bf16)

    pl.semaphore_wait(barrier, nd - 1)

    exchange_start(0)
    r.pars[k] = r.par[...]
    for step in range(1, nk):
        send("par", r.par, r.pars.at[k], at(i, lax.rem(k + step, nk)))
    weights_along(0, "j")
    weights_along(0, "m")
    swap_start(0)
    own_tile(0)

    clear([r.x, r.ga, r.pf, r.bi, r.mixs, r.mg, r.sg, r.bg, r.sgm, *r.gr.values()])

    select_row = lax.broadcasted_iota(jnp.int32, (z.rb, 16), 0)
    select_col = lax.broadcasted_iota(jnp.int32, (z.rb, 16), 1)
    pick_high = (lax.div(select_row, z.tj) == select_col).astype(f32)
    pick_wide = (lax.rem(select_row, z.tj) == select_col).astype(f32)
    low_high, low_wide = pick_high.astype(bf16), pick_wide.astype(bf16)
    full_row = lax.broadcasted_iota(jnp.int32, (z.rb, z.rb), 0)
    full_col = lax.broadcasted_iota(jnp.int32, (z.rb, z.rb), 1)
    same_wide = (lax.rem(full_row, z.tj) == lax.rem(full_col, z.tj)) & (lax.rem(full_row, z.tj) < z.wide)
    same_high = lax.div(full_row, z.tj) == lax.div(full_col, z.tj)
    for layer in range(layers):
        for which, (maps, shifts, pick, same, extent) in enumerate(
            (
                (r.mix_rows, r.mix_rows_bias, low_high, same_wide, z.high),
                (r.mix_cols, r.mix_cols_bias, low_wide, same_high, z.wide),
            )
        ):
            r.mixs[which, 0:extent, 0:extent] = maps[:, layer, :].astype(f32)
            table = r.mixs[which].astype(bf16)
            for turned, half in ((0, dot_nn(pick, table)), (1, dot_nt(pick, table))):
                spread = dot_nt(half.astype(bf16), pick)
                r.mix[layer, 2 * which + turned] = jnp.where(same, spread, 0.0).astype(bf16)
            r.mixs[2 + which, 0:1, 0:extent] = shifts[layer : layer + 1, :].astype(f32)
            r.mixb[layer, which] = dot_nt(pick, r.mixs[2 + which, 0:8, :].astype(bf16))

    weights_across(0, "j")
    weights_across(0, "m")

    exchange_wait(0)
    arrived("par", r.pars.at[pl.ds(0, nk - 1)])
    for layer in range(layers):
        tiles = assemble(
            [(r.pars[part, layer, 0:PARAM_ROWS, :], part * z.cl, z.cl) for part in range(nk)], z.ct
        )
        for tile in range(z.ct):
            r.pf[layer, :, LANES * tile : LANES * (tile + 1)] = tiles[tile]
        for block in range(z.nkg):
            pieces = []
            for part in range(z.kg):
                for tile in range(z.ftiles):
                    row = PARAM_ROWS + tile
                    value = r.pars[block * z.kg + part, layer, row : row + 1, :]
                    width = min(LANES, z.fl - LANES * tile)
                    pieces.append((jnp.broadcast_to(value, (8, LANES)), part * z.fl + LANES * tile, width))
            tiles = assemble(pieces, -(-z.ft // LANES))
            for tile, value in enumerate(tiles):
                stop = min(z.ft, LANES * (tile + 1))
                r.bi[layer, block, :, LANES * tile : stop] = value[:, 0 : stop - LANES * tile]

    def param(layer, row):
        return r.pf[layer, row : row + 1, :]

    def wide_row(tiles):
        return jnp.concatenate(tiles, axis=1)

    def combine(means, variances):
        count = means.shape[0]
        mean = jnp.sum(means, axis=0, keepdims=True) * (1.0 / count)
        away = means - mean
        var = jnp.sum(variances + away * away, axis=0, keepdims=True) * (1.0 / count)
        return mean[0], var[0]

    lane_full = lane_index((z.step, z.tj, z.cp))
    column_full = lax.broadcasted_iota(jnp.int32, (z.step, z.tj, z.cp), 1)
    real_lane = lane_full < z.channels
    real_column = column_full < z.wide
    blocks = z.bh // z.step

    def place_of(t):
        return lax.div(t, z.high), lax.rem(t, z.high)

    def store_x(m, tiles):
        for tile in range(z.ct):
            r.x[0, lax.div(m, z.high), lax.rem(m, z.high) + 1, :, LANES * tile : LANES * (tile + 1)] = tiles[tile]

    def store_gx(m, tiles):
        for tile in range(z.ct):
            r.gx[m, :, LANES * tile : LANES * (tile + 1)] = tiles[tile]

    def slices_of(ref, slot):
        for d in range(nk):

            def line(m, d=d):
                return cut([ref[m, :, LANES * t : LANES * (t + 1)] for t in range(z.ct)], d * z.cl, z.cl)

            pack(z, r.stage.at[slot], d, line)

    if layers > 1:
        weights_along(1, "j")
        weights_along(1, "m")
    swap_wait(0)
    unpack(z, r.land.at[0], store_x)

    own_cells = z.own * z.high * z.wide

    for layer in range(layers):

        def conv_part(t, carry, layer=layer):
            b, part = lax.div(t, z.high // z.lines), lax.rem(t, z.high // z.lines)
            start = part * z.lines
            sums = []
            for tile in range(z.ct):
                lanes = slice(LANES * tile, LANES * (tile + 1))
                taps = [r.pf[layer, row : row + 1, lanes] for row in range(9)]
                value = conv(r.x[layer, b, pl.ds(start, z.lines + 2), :, lanes], taps)
                value = jnp.where(inside, value, 0.0)
                r.a[layer, pl.ds(b * z.high + start, z.lines), :, lanes] = value
                sums.append(carry[tile] + jnp.sum(value, axis=0))
            return tuple(sums)

        sums = lax.fori_loop(
            0,
            z.own * (z.high // z.lines),
            conv_part,
            tuple(jnp.zeros((z.tj, LANES), f32) for _ in range(z.ct)),
        )
        if layer == 0:
            stats = r.stats[0].reshape(ni, nk, z.stat, LANES)
            whole_mean, whole_var = [], []
            for part in range(nk):
                mean, var = combine(stats[:, part, 0:1, :], stats[:, part, 1:2, :])
                whole_mean.append((jnp.broadcast_to(mean, (8, LANES)), part * z.cl, z.cl))
                whole_var.append((jnp.broadcast_to(var, (8, LANES)), part * z.cl, z.cl))
            mean = wide_row([tile[0:1] for tile in assemble(whole_mean, z.ct)])
            var = wide_row([tile[0:1] for tile in assemble(whole_var, z.ct)])
        else:
            own_mean = wide_row([jnp.sum(tile, axis=0, keepdims=True) for tile in sums]) * (1.0 / own_cells)

            def square_part(t, carry, layer=layer, own_mean=own_mean):
                value = r.a[layer, pl.ds(t * z.step, z.step)] - own_mean
                value = jnp.where(real_column, value, 0.0)
                return carry + jnp.sum(value * value, axis=0)

            squares = lax.fori_loop(0, blocks, square_part, jnp.zeros((z.tj, z.cp), f32))
            own_var = jnp.sum(squares, axis=0, keepdims=True) * (1.0 / own_cells)
            for tile in range(z.ct):
                lanes = slice(LANES * tile, LANES * (tile + 1))
                r.msg[layer, tile : tile + 1, :] = own_mean[:, lanes]
                r.msg[layer, z.ct + tile : z.ct + tile + 1, :] = own_var[:, lanes]
            exchange_start(layer)
            weights_across(layer, "j")
            weights_across(layer, "m")
            if layer == 1:
                take(r.cotangent, 1)
                swap_start(1)
                own_tile(1)
            exchange_wait(layer)
            stats = r.stats[layer]
            mean, var = combine(stats[:, 0 : z.ct, :], stats[:, z.ct : 2 * z.ct, :])
            mean = wide_row([mean[t : t + 1] for t in range(z.ct)])
            var = wide_row([var[t : t + 1] for t in range(z.ct)])
        inv_std = lax.rsqrt(var + epsilon)
        r.mv[layer, 0:1, :] = mean
        r.mv[layer, 1:2, :] = var
        r.mv[layer, 2:3, :] = inv_std
        scale = inv_std * param(layer, 9)
        shift = param(layer, 10)

        def norm_part(t, layer=layer, mean=mean, scale=scale, shift=shift):
            lines = pl.ds(t * z.step, z.step)
            active, slope = gelu_both((r.a[layer, lines] - mean) * scale + shift)
            r.sz[layer, lines] = slope
            b, start = place_of(t * z.step)
            value = jnp.where(real_column, active, 0.0)
            r.u[lines] = value

        loop(blocks, norm_part)

        def add_part(b, layer=layer):
            value = r.u[pl.ds(b * z.high, z.high)] + r.x[layer, b, 1 : z.high + 1]
            r.u[pl.ds(b * z.high, z.high)] = value
            r.cat[layer, 0, b] = value.reshape(z.rb, z.cp).astype(bf16)

        loop(z.own, add_part)
        weights_pair(layer, z.join_kind)

        def mix_part(b, layer=layer):
            low = r.cat[layer, 0, b]
            for which in range(2):
                value = dot_nn(r.mix[layer, 2 * which], low) + r.mixb[layer, which, :, 0:1]
                r.cat[layer, 1 + which, b] = value.astype(bf16)

        loop(z.own, mix_part)
        weights_ready(layer, z.join_kind)
        weights_pair(layer, "m")
        if 0 < layer < layers - 1:
            weights_along(layer + 1, "j")
            weights_along(layer + 1, "m")

        def join_part(b, layer=layer):
            value = dot_nn(r.cat[layer, 0, b], r.jf[layer, 0])
            value = value + dot_nn(r.cat[layer, 1, b], r.jf[layer, 1])
            value = value + dot_nn(r.cat[layer, 2, b], r.jf[layer, 2])
            r.w[pl.ds(b * z.high, z.high)] = value.reshape(z.high, z.tj, z.cp)

        loop(z.own, join_part)

        def token_part(t, layer=layer):
            lines = pl.ds(t * z.step, z.step)
            value = r.w[lines] + r.u[lines] + param(layer, 11)
            r.w[lines] = value
            mean = jnp.sum(value, axis=2, keepdims=True) * (1.0 / z.channels)
            away = jnp.where(real_lane, value - mean, 0.0)
            var = jnp.sum(away * away, axis=2, keepdims=True) * (1.0 / z.channels)
            inv = lax.rsqrt(var + epsilon)
            what = away * inv
            r.what[layer, lines] = what
            r.inv[layer, lines] = jnp.broadcast_to(inv, (z.step, z.tj, LANES))
            r.yb[layer, lines] = (what * param(layer, 12) + param(layer, 13)).astype(bf16)

        loop(blocks, token_part)
        weights_ready(layer, "m")
        if layer + 1 < layers:
            weights_across(layer + 1, "j")

        def mlp_part(b, layer=layer):
            lines = pl.ds(b * z.high, z.high)
            low = r.yb[layer, lines].reshape(z.rb, z.cp)
            total = None
            for block in range(z.nkg):
                parts = slice(block * z.kg, (block + 1) * z.kg)
                rising = r.wt["m"][layer, parts, 0 : z.fl, :].reshape(z.ft, z.cp)
                hidden = dot_nt(low, rising) + r.bi[layer, block, 0:1, :]
                active, slope = gelu_both(hidden)
                r.hs[layer, block, b] = slope
                active = active.astype(bf16)
                r.gb[layer, block, b] = active
                falling = r.wt["m"][layer, parts, z.fl : 2 * z.fl, :].reshape(z.ft, z.cp)
                term = dot_nn(active, falling)
                total = term if total is None else total + term
            value = total.reshape(z.high, z.tj, z.cp) + r.w[lines] + param(layer, 14)
            value = jnp.where(real_part, value, 0.0)
            if layer + 1 < layers:
                r.x[layer + 1, b, 1 : z.high + 1] = value
            else:
                r.y[lines] = value

        real_part = lax.broadcasted_iota(jnp.int32, (z.high, z.tj, z.cp), 1) < z.wide
        loop(z.own, mlp_part)

    if layers == 1:
        take(r.cotangent, 1)
        swap_start(1)
        own_tile(1)
    swap_wait(1)
    unpack(z, r.land.at[1], store_gx)

    def small_across(layer):
        arrived(("s1", layer), r.sgk.at[layer, pl.ds(0, nk - 1)])
        r.sgz[layer] = jnp.sum(r.sgk[layer], axis=0)
        r.sgi[layer, i] = r.sgz[layer]

        def one(j):
            send(("s2", layer), r.sgz.at[layer], r.sgi.at[layer, i], at(lax.rem(i + j, ni), k))

        loop(ni, one, 1)

    def small_ready(layer):
        arrived(("s2", layer), r.sgi.at[layer, pl.ds(0, ni - 1)])
        r.out_s[layer, 0:32, :] = jnp.sum(r.sgi[layer], axis=0)
        tiles = [r.mv[layer, :, LANES * tile : LANES * (tile + 1)] for tile in range(z.ct)]
        mine = jnp.zeros((8, LANES), f32)
        for part in range(nk):
            mine = mine + jnp.where(k == part, cut(tiles, part * z.cl, z.cl), 0.0)
        r.out_s[layer, 32:40, :] = mine

    for layer in reversed(range(layers)):
        above = layer + 1 if layer + 1 < layers else None

        def start_part(t, carry):
            lines = pl.ds(t * z.step, z.step)
            value = r.gx[lines]
            r.gob[lines] = value.astype(bf16)
            return carry + jnp.sum(value, axis=0)

        total = lax.fori_loop(0, blocks, start_part, jnp.zeros((z.tj, z.cp), f32))
        r.sg[12:13, :] = jnp.sum(total, axis=0, keepdims=True)
        low_out = r.gob[...].reshape(z.rows, z.cp)

        for block in range(z.nkg):
            parts = slice(block * z.kg, (block + 1) * z.kg)
            falling = r.wt["m"][layer, parts, z.fl : 2 * z.fl, :].reshape(z.ft, z.cp)
            rising = r.wt["m"][layer, parts, 0 : z.fl, :].reshape(z.ft, z.cp)

            value = dot_nt(low_out, falling) * r.hs[layer, block].reshape(z.rows, z.ft)
            r.bg[0:1, block * z.ft : (block + 1) * z.ft] = jnp.sum(value, axis=0, keepdims=True)
            low_hidden = value.astype(bf16)
            term = dot_nn(low_hidden, rising).reshape(z.bh, z.tj, z.cp)
            r.o[...] = term if block == 0 else r.o[...] + term
            low_in = r.yb[layer].reshape(z.rows, z.cp)
            value = dot_tn(low_hidden, low_in).astype(bf16).reshape(z.kg, z.fl, z.cp)
            r.gr["m"][layer, parts, 0 : z.fl, :] = value
            low_active = r.gb[layer, block].reshape(z.rows, z.ft)
            value = dot_tn(low_active, low_out).astype(bf16).reshape(z.kg, z.fl, z.cp)
            r.gr["m"][layer, parts, z.fl : 2 * z.fl, :] = value
        if z.join_kind != "m":
            reduce_pair(layer, "m")

        def token_back(t, carry, layer=layer):
            lines = pl.ds(t * z.step, z.step)
            gain_sum, bias_sum, join_sum = carry
            gy, what = r.o[lines], r.what[layer, lines]
            inv = r.inv[layer, lines][:, :, 0:1]
            scaled = gy * param(layer, 12)
            plain = jnp.sum(scaled, axis=2, keepdims=True) * (1.0 / z.channels)
            cross = jnp.sum(scaled * what, axis=2, keepdims=True) * (1.0 / z.channels)
            value = r.gx[lines] + inv * (jnp.where(real_lane, scaled - plain, 0.0) - what * cross)
            r.gw[lines] = value
            r.gsb[lines] = value.astype(bf16)
            return (
                gain_sum + jnp.sum(gy * what, axis=0),
                bias_sum + jnp.sum(gy, axis=0),
                join_sum + jnp.sum(value, axis=0),
            )

        zero = jnp.zeros((z.tj, z.cp), f32)
        gain_sum, bias_sum, join_sum = lax.fori_loop(0, blocks, token_back, (zero, zero, zero))
        r.sg[9:10, :] = jnp.sum(join_sum, axis=0, keepdims=True)
        r.sg[10:11, :] = jnp.sum(gain_sum, axis=0, keepdims=True)
        r.sg[11:12, :] = jnp.sum(bias_sum, axis=0, keepdims=True)

        def mix_back(b, layer=layer):
            lines = pl.ds(b * z.high, z.high)
            low = r.gsb[lines].reshape(z.rb, z.cp)
            total = r.gw[lines].reshape(z.rb, z.cp) + dot_nt(low, r.jf[layer, 0])
            for which in range(2):
                back = dot_nt(low, r.jf[layer, 1 + which]).astype(bf16)
                r.gpq[which, b] = back
                total = total + dot_nn(r.mix[layer, 2 * which + 1], back)
            r.gu[lines] = total.reshape(z.high, z.tj, z.cp)

        loop(z.own, mix_back)

        inv_std = r.mv[layer, 2:3, :]
        mean = r.mv[layer, 0:1, :]

        def gate_back(t, carry, layer=layer, mean=mean, inv_std=inv_std):
            lines = pl.ds(t * z.step, z.step)
            value = r.gu[lines] * r.sz[layer, lines]
            r.gz[lines] = value
            centred = (r.a[layer, lines] - mean) * inv_std
            return carry[0] + jnp.sum(value, axis=0), carry[1] + jnp.sum(value * centred, axis=0)

        first, second = lax.fori_loop(0, blocks, gate_back, (zero, zero))
        first = jnp.sum(first, axis=0, keepdims=True)
        second = jnp.sum(second, axis=0, keepdims=True)
        slot = layers + layer
        for tile in range(z.ct):
            lanes = slice(LANES * tile, LANES * (tile + 1))
            r.msg[slot, tile : tile + 1, :] = first[:, lanes]
            r.msg[slot, z.ct + tile : z.ct + tile + 1, :] = second[:, lanes]
        exchange_start(slot)
        if above is not None:
            reduce_along(above, "m")
            reduce_along(above, "j")
        if z.join_kind != "m":
            reduce_across(layer, "m")
        low_join = r.gsb[...].reshape(z.rows, z.cp)
        for branch in range(3):
            value = dot_tn(r.cat[layer, branch].reshape(z.rows, z.cp), low_join)
            for part in range(nk):
                row = z.join_row + branch * z.clp
                r.gr[z.join_kind][layer, part, row : row + z.cl, :] = value[
                    part * z.cl : (part + 1) * z.cl
                ].astype(bf16)
        reduce_pair(layer, z.join_kind)
        if above is None:
            slices_of(r.y, 2)
            swap_start(2)
            own_tile(2)

        def tables_part(b, carry, layer=layer):
            low = r.cat[layer, 0, b]
            backs = [r.gpq[which, b] for which in range(2)]
            return (
                *(carry[which] + dot_nt(backs[which], low) for which in range(2)),
                *(
                    carry[2 + which] + jnp.sum(backs[which].astype(f32), axis=1, keepdims=True)
                    for which in range(2)
                ),
            )

        square, column = jnp.zeros((z.rb, z.rb), f32), jnp.zeros((z.rb, 1), f32)
        rows_table, cols_table, rows_sum, cols_sum = lax.fori_loop(
            0, z.own, tables_part, (square, square, column, column)
        )
        reduce_across(layer, z.join_kind)
        if above is not None:
            small_across(above)

        rows_table = jnp.where(same_wide, rows_table, 0.0).reshape(z.high, z.tj, z.rb)
        rows_table = jnp.sum(rows_table, axis=1)
        rows_table = lax.dot_general(
            rows_table, pick_high, (((1,), (0,)), ((), ())), preferred_element_type=f32, precision=lax.Precision.HIGHEST
        )
        cols_table = jnp.sum(jnp.where(same_high, cols_table, 0.0).reshape(z.high, z.tj, z.rb), axis=0)
        cols_table = lax.dot_general(
            cols_table, pick_wide, (((1,), (0,)), ((), ())), preferred_element_type=f32, precision=lax.Precision.HIGHEST
        )
        r.mg[0 : z.high, 0:16] = rows_table
        r.mg[:, 16:32] = cols_table
        r.mg[0 : z.high, 32:33] = jnp.sum(rows_sum.reshape(z.high, z.tj, 1), axis=1)
        r.mg[:, 33:34] = jnp.sum(cols_sum.reshape(z.high, z.tj, 1), axis=0)

        exchange_wait(slot)
        stats = jnp.sum(r.stats[slot], axis=0)
        bias_total = wide_row([stats[t : t + 1] for t in range(z.ct)])
        gain_total = wide_row([stats[z.ct + t : z.ct + t + 1] for t in range(z.ct)])
        r.mv[layer, 3:4, :] = gain_total
        r.mv[layer, 4:5, :] = bias_total
        factor = inv_std * param(layer, 9)
        plain = bias_total * (1.0 / z.cells)
        cross = gain_total * (1.0 / z.cells) * inv_std

        def conv_gate(b, layer=layer, mean=mean, factor=factor, plain=plain, cross=cross):
            lines = pl.ds(b * z.high, z.high)
            value = r.gz[lines] - plain - (r.a[layer, lines] - mean) * cross
            r.ga[b, 1 : z.high + 1] = jnp.where(real_part, value * factor, 0.0)

        loop(z.own, conv_gate)

        def conv_back(t, layer=layer):
            b, part = lax.div(t, z.high // z.lines), lax.rem(t, z.high // z.lines)
            start = part * z.lines
            lines = pl.ds(b * z.high + start, z.lines)
            for tile in range(z.ct):
                lanes = slice(LANES * tile, LANES * (tile + 1))
                taps = [r.pf[layer, 8 - row : 9 - row, lanes] for row in range(9)]
                value = conv(r.ga[b, pl.ds(start, z.lines + 2), :, lanes], taps)
                r.gx[lines, :, lanes] = jnp.where(inside, value + r.gu[lines, :, lanes], 0.0)

        loop(z.own * (z.high // z.lines), conv_back)

        if layer == 0:
            slices_of(r.gx, 3)
            swap_start(3)
            own_tile(3)

        for tile in range(z.ct):
            lanes = slice(LANES * tile, LANES * (tile + 1))

            def kernel_part(t, carry, layer=layer, lanes=lanes):
                b, part = lax.div(t, z.high // z.lines), lax.rem(t, z.high // z.lines)
                start = part * z.lines
                lines = r.x[layer, b, pl.ds(start, z.lines + 2), :, lanes]
                upstream = r.ga[b, pl.ds(start + 1, z.lines), :, lanes]
                shifted = (pltpu.roll(lines, 1, 1), lines, pltpu.roll(lines, z.tj - 1, 1))
                return tuple(
                    carry[3 * down + side]
                    + jnp.sum(jnp.sum(shifted[side][down : down + z.lines] * upstream, axis=0), axis=0, keepdims=True)
                    for down in range(3)
                    for side in range(3)
                )

            totals = lax.fori_loop(
                0,
                z.own * (z.high // z.lines),
                kernel_part,
                tuple(jnp.zeros((1, LANES), f32) for _ in range(9)),
            )
            for row in range(9):
                r.sg[row : row + 1, lanes] = totals[row]

        tiles = [r.sg[:, LANES * tile : LANES * (tile + 1)] for tile in range(z.ct)]
        for part in range(nk):
            r.sgm[layer, part, 0:16, :] = cut(tiles, part * z.cl, z.cl)
            for tile in range(z.ftiles):
                start = part * z.fl + LANES * tile
                width = min(LANES, z.fl - LANES * tile)
                hidden = [
                    r.bg[:, LANES * t : min(LANES * (t + 1), nk * z.fl)] for t in range(-(-nk * z.fl // LANES))
                ]
                r.sgm[layer, part, 13 + tile : 14 + tile, :] = cut(hidden, start, width)[0:1]
            r.sgm[layer, part, 16:32, :] = r.mg[...]
        r.sgk[layer, k] = r.sgm[layer, k]
        for step in range(1, nk):
            other = lax.rem(k + step, nk)
            send(("s1", layer), r.sgm.at[layer, other], r.sgk.at[layer, k], at(i, other))

    swap_wait(2)
    deliver(z, r.land.at[2], r.tmp, r.fy)
    store(r.fy, r.out_y)
    for layer in range(1, layers):
        spread_across(layer, "m")
        spread_across(layer, "j")
    reduce_along(0, "m")
    reduce_along(0, "j")
    small_across(0)
    for layer in range(1, layers):
        spread_pair(layer, "m")
        spread_pair(layer, "j")
    swap_wait(3)
    deliver(z, r.land.at[3], r.tmp, r.fg)
    store(r.fg, r.out_g)
    spread_across(0, "m")
    spread_across(0, "j")
    for layer in range(1, layers):
        small_ready(layer)
        spread_ready(layer, "m")
        spread_ready(layer, "j")
    small_ready(0)
    spread_pair(0, "m")
    spread_pair(0, "j")
    spread_ready(0, "m")
    spread_ready(0, "j")

    for copy in stores:
        copy.wait()
    for number, ref in sends:
        pltpu.make_async_remote_copy(
            src_ref=ref,
            dst_ref=ref,
            send_sem=ssem.at[number],
            recv_sem=rsem.at[number],
            device_id=at(partner, k),
            device_id_type=MESH,
        ).wait_send()


EVENTS = 80


def deliver(z, land, tmp, out):
    for k in range(z.nk):

        def group(first, tile, lines, tiles, k=k):
            source = [land[k, tile + t].astype(f32) for t in range(tiles)]
            for j in range(lines):
                m = first + j
                n = k * z.own + lax.div(m, z.high)
                tmp[lax.rem(m, z.high), pl.ds(n, z.wide, stride=z.group), :] = cut(source, j * z.cl, z.cl)[: z.wide]

        line_groups(z, group)

    def line(h, carry):
        out[h] = tmp[h, :, 0 : z.cl].reshape(z.wide, z.group, z.cl).astype(out.dtype)
        return carry

    lax.fori_loop(0, z.high, line, 0)


def finish(z, *refs):
    count = 3 + len(z.parts)
    sources, refs = refs[:count], refs[count:]
    sem, copies, refs = refs[-1], refs[1 - count : -1], refs[: 1 - count]
    copies = (refs[2], refs[3], *copies)
    loads = [pltpu.make_async_copy(src, dst, sem.at[n]) for n, (src, dst) in enumerate(zip(sources, copies, strict=True))]
    for load in loads:
        load.start()
    small = copies[2]
    fins = dict(zip(z.parts, copies[3:], strict=True))
    mean_in, var_in = refs[:2]
    (conv_grad, bn_gain, bn_bias, rows_grad, rows_bias, cols_grad, cols_bias, join) = refs[4:12]
    (join_bias, norm_gain, norm_bias, rising, bias_in, falling, bias_out, mean_out, var_out) = refs[12:]
    for load in loads[2:]:
        load.wait()
    for layer in range(z.layers):
        here = slice(layer, layer + 1)

        def row(number, layer=layer):
            return small[layer, number : number + 1, 0 : z.cl]

        for tap in range(9):
            conv_grad[tap // 3, tap % 3, here, :] = row(tap)
        join_bias[here, :] = row(9)
        norm_gain[here, :] = row(10)
        norm_bias[here, :] = row(11)
        bias_out[here, :] = row(12)
        for tile in range(z.ftiles):
            stop = min(z.fl, LANES * (tile + 1))
            bias_in[here, LANES * tile : stop] = small[layer, 13 + tile : 14 + tile, 0 : stop - LANES * tile]
        rows_grad[:, layer, :] = small[layer, 16 : 16 + z.high, 0 : z.high]
        cols_grad[:, layer, :] = small[layer, 16 : 16 + z.wide, 16 : 16 + z.wide]
        turned = small[layer, 16:32, :].T
        rows_bias[here, :] = turned[32:33, 0 : z.high]
        cols_bias[here, :] = turned[33:34, 0 : z.wide]
        mean_out[here, :] = 0.9 * mean_in[here, :] + 0.1 * row(32)
        var_out[here, :] = 0.9 * var_in[here, :] + (0.1 * z.cells / (z.cells - 1.0)) * row(33)
        bn_gain[here, :] = row(35)
        bn_bias[here, :] = row(36)
        fin = fins["m"]
        rising[layer] = fin[layer, 0 : z.fl, 0 : z.channels].astype(f32).T
        falling[layer] = fin[layer, z.fl : 2 * z.fl, 0 : z.channels].astype(f32)
        fin = fins[z.join_kind]
        for branch in range(3):
            start = z.join_row + branch * z.clp
            join[layer, branch] = fin[layer, start : start + z.cl, 0 : z.channels].astype(f32)
    for load in loads[:2]:
        load.wait()


EVENTS = 80


def on_device(ni, nk, *args):
    first, second = (1, 2, 0, 3), (1, 0, 2)
    args = list(args)
    for number, order in ((0, first), (1, first), (18, first), (4, second), (6, second)):
        args[number] = args[number].transpose(order)
    images, conv_kernel, weight_in = args[0], args[1], args[12]
    running_mean, running_var, cotangent = args[16:19]
    z = Sizes(ni, nk, images, conv_kernel, weight_in)
    inputs = (*args[:16], cotangent)
    tokens = (z.high, z.wide, z.group, z.cl)
    out_shape = (
        jax.ShapeDtypeStruct(tokens, bf16),
        jax.ShapeDtypeStruct(tokens, f32),
        jax.ShapeDtypeStruct((z.layers, SMALL_ROWS, LANES), f32),
        *(jax.ShapeDtypeStruct((z.layers, ni * part, z.cp), bf16) for part in z.parts.values()),
    )
    vmem, anywhere = pl.BlockSpec(memory_space=pltpu.VMEM), pl.BlockSpec(memory_space=pl.ANY)
    shapes, groups = scratch_list(z)
    scratch = [pltpu.VMEM(shape, kind) for table in (shapes, *groups) for shape, kind in table.values()]
    scratch += [pltpu.SemaphoreType.DMA((EVENTS,)), pltpu.SemaphoreType.DMA((EVENTS,)), pltpu.SemaphoreType.DMA((16,))]
    moved = pl.pallas_call(
        functools.partial(whole, z),
        out_shape=out_shape,
        in_specs=[vmem] * len(inputs),
        out_specs=tuple(vmem if number == 2 else anywhere for number in range(len(out_shape))),
        scratch_shapes=scratch,
        compiler_params=pltpu.CompilerParams(
            collective_id=0, has_side_effects=True, vmem_limit_bytes=62 * 2**20
        ),
    )(*inputs)
    lead = z.layers
    sizes = [
        (tokens, bf16),
        (tokens, f32),
        ((3, 3, lead, z.cl), f32),
        ((lead, z.cl), f32),
        ((lead, z.cl), f32),
        ((z.high, lead, z.high), f32),
        ((lead, z.high), f32),
        ((z.wide, lead, z.wide), f32),
        ((lead, z.wide), f32),
        ((lead, 3, z.cl, z.channels), f32),
        ((lead, z.cl), f32),
        ((lead, z.cl), f32),
        ((lead, z.cl), f32),
        ((lead, z.channels, z.fl), f32),
        ((lead, z.fl), f32),
        ((lead, z.fl, z.channels), f32),
        ((lead, z.cl), f32),
        ((lead, z.cl), f32),
        ((lead, z.cl), f32),
    ]
    results = pl.pallas_call(
        functools.partial(finish, z),
        out_shape=tuple(jax.ShapeDtypeStruct(*size) for size in sizes),
        in_specs=[anywhere] * len(moved) + [vmem] * 2,
        out_specs=(vmem,) * len(sizes),
        scratch_shapes=[
            *(pltpu.VMEM(item.shape, item.dtype) for item in moved[2:]),
            pltpu.SemaphoreType.DMA((len(moved),)),
        ],
        compiler_params=pltpu.CompilerParams(vmem_limit_bytes=62 * 2**20),
    )(*moved, running_mean, running_var)
    results = list(results)
    for number, order in ((0, (2, 0, 1, 3)), (1, (2, 0, 1, 3)), (2, (2, 0, 1, 3)), (5, second), (7, second)):
        results[number] = results[number].transpose(order)
    return tuple(results)


def solution(mesh):
    return jax.shard_map(
        functools.partial(on_device, mesh.shape["img"], mesh.shape["ch"]),
        mesh=mesh,
        in_specs=(
            P("img", None, None, "ch"),
            P(None, None, None, "ch"),
            P(None, "ch"),
            P(None, "ch"),
            P(),
            P(),
            P(),
            P(),
            P(None, None, "ch", None),
            P(None, "ch"),
            P(None, "ch"),
            P(None, "ch"),
            P(None, None, "ch"),
            P(None, "ch"),
            P(None, "ch", None),
            P(None, "ch"),
            P(None, "ch"),
            P(None, "ch"),
            P("img", None, None, "ch"),
        ),
        out_specs=(
            P("img", None, None, "ch"),
            P("img", None, None, "ch"),
            P(None, None, None, "ch"),
            P(None, "ch"),
            P(None, "ch"),
            P(),
            P(),
            P(),
            P(),
            P(None, None, "ch", None),
            P(None, "ch"),
            P(None, "ch"),
            P(None, "ch"),
            P(None, None, "ch"),
            P(None, "ch"),
            P(None, "ch", None),
            P(None, "ch"),
            P(None, "ch"),
            P(None, "ch"),
        ),
        check_vma=False,
    )
```

```python
import functools
from types import SimpleNamespace

import jax
import jax.numpy as jnp
from jax import lax
from jax.experimental import pallas as pl
from jax.experimental.pallas import tpu as pltpu
from jax.sharding import PartitionSpec as P

f32 = jnp.float32
bf16 = jnp.bfloat16
MESH = pl.DeviceIdType.MESH
epsilon = 1e-05
LANES = 128
ROOT = 0.7978845608028654
CUBE = 0.044715


def up(number, step):
    return -(-number // step) * step


def dot_nn(left, right):
    return lax.dot_general(left, right, (((1,), (0,)), ((), ())), preferred_element_type=f32)


def dot_nt(left, right):
    return lax.dot_general(left, right, (((1,), (1,)), ((), ())), preferred_element_type=f32)


def dot_tn(left, right):
    return lax.dot_general(left, right, (((0,), (0,)), ((), ())), preferred_element_type=f32)


def gelu_both(value):
    square = value * value
    bend = jnp.tanh(value * (ROOT + (ROOT * CUBE) * square))
    half = 0.5 + 0.5 * bend
    slope = half + (0.5 * value) * (1.0 - bend * bend) * (ROOT + (3.0 * ROOT * CUBE) * square)
    return value * half, slope


def lane_index(shape):
    return lax.broadcasted_iota(jnp.int32, shape, len(shape) - 1)


def assemble(pieces, tiles):
    placed = [None] * tiles
    axis = pieces[0][0].ndim - 1
    lane = lane_index(pieces[0][0].shape)

    def add(place, value):
        placed[place] = value if placed[place] is None else placed[place] + value

    for tile, offset, width in pieces:
        first, shift = divmod(offset, LANES)
        if shift == 0:
            add(first, tile)
            continue
        turned = pltpu.roll(tile, shift, axis)
        if shift + width <= LANES:
            add(first, turned)
        else:
            add(first, jnp.where(lane >= shift, turned, 0.0))
            add(first + 1, jnp.where(lane < shift, turned, 0.0))
    return [jnp.zeros(pieces[0][0].shape, f32) if tile is None else tile for tile in placed]


def cut(tiles, offset, width):
    axis = tiles[0].ndim - 1
    lane = lane_index(tiles[0].shape)
    first, shift = divmod(offset, LANES)
    if shift == 0:
        value = tiles[first]
    else:
        value = pltpu.roll(tiles[first], LANES - shift, axis)
        if shift + width > LANES:
            value = jnp.where(lane < LANES - shift, value, pltpu.roll(tiles[first + 1], LANES - shift, axis))
    return value if width == LANES else jnp.where(lane < width, value, 0.0)


def line_groups(z, body):
    def run(g, carry):
        body(g * z.gl, g * z.gt, z.gl, z.gt)
        return carry

    if z.full:
        lax.fori_loop(0, z.full, run, 0)
    if z.rest:
        body(z.full * z.gl, z.full * z.gt, z.rest, z.rest_t)


def pack(z, stage, target, line):
    def group(first, tile, lines, tiles):
        values = assemble([(line(first + j), j * z.cl, z.cl) for j in range(lines)], tiles)
        for t in range(tiles):
            stage[target, tile + t] = values[t].astype(bf16)

    line_groups(z, group)


def unpack(z, land, store):
    def group(first, tile, lines, tiles):
        sources = [[land[k, tile + t].astype(f32) for t in range(tiles)] for k in range(z.nk)]
        for j in range(lines):
            store(
                first + j,
                assemble([(cut(source, j * z.cl, z.cl), k * z.cl, z.cl) for k, source in enumerate(sources)], z.ct),
            )

    line_groups(z, group)


class Sizes:
    def __init__(self, ni, nk, images, conv_kernel, weight_in):
        self.ni, self.nk, self.nd = ni, nk, ni * nk
        self.chips = ni // 2
        self.high, self.wide, self.group, self.cl = images.shape
        self.layers = conv_kernel.shape[2]
        self.own = self.group // nk
        self.channels = weight_in.shape[1]
        self.fl = weight_in.shape[2]
        self.tj = up(self.wide, 16)
        self.cp = up(self.channels, LANES)
        self.ct = self.cp // LANES
        self.bh = self.own * self.high
        self.rows = self.bh * self.tj
        self.rb = self.high * self.tj
        self.cells = ni * self.group * self.high * self.wide
        self.clp = up(self.cl, 16)
        def part_rows(rows):
            return up(-(-rows // ni), 16)

        join_rows, mlp_rows = 3 * self.clp, 2 * self.fl
        apart, together = part_rows(join_rows) + part_rows(mlp_rows), part_rows(join_rows + mlp_rows)
        if 4 * apart <= 5 * together:
            self.parts = {"m": part_rows(mlp_rows), "j": part_rows(join_rows)}
            self.join_kind, self.join_row = "j", 0
        else:
            self.parts = {"m": together}
            self.join_kind, self.join_row = "m", mlp_rows
        self.kg = next((n for n in range(1, nk + 1) if nk % n == 0 and n * self.fl % LANES == 0), nk)
        self.nkg = nk // self.kg
        self.ft = self.kg * self.fl
        self.ftiles = -(-self.fl // LANES)
        self.step = next(n for n in (4, 2, 1) if self.bh % n == 0)
        self.lines = next(n for n in (7, 4, 2, 1) if self.high % n == 0)
        self.stat = up(2 * self.ct, 8)
        self.gl = next(n for n in range(1, LANES + 1) if n * self.cl % LANES == 0)
        self.gt = self.gl * self.cl // LANES
        self.full, self.rest = divmod(self.bh, self.gl)
        self.rest_t = -(-self.rest * self.cl // LANES)
        self.packed = self.full * self.gt + self.rest_t


PARAM_ROWS = 16
SMALL_ROWS = 40


def scratch_list(z):
    tile = (z.packed, z.tj, LANES)
    layer, rows, cp = z.layers, z.rows, z.cp
    shapes = dict(
        tmp=((z.high, z.tj * z.group, LANES), f32),
        fy=((z.high, z.wide, z.group, z.cl), bf16),
        fg=((z.high, z.wide, z.group, z.cl), f32),
        xl=((z.group, z.high + 2, z.tj, LANES), f32),
        al=((z.group, z.high, z.tj, LANES), f32),
        stage=((4, z.nk) + tile, bf16),
        land=((4, z.nk) + tile, bf16),
        par=((layer, PARAM_ROWS + 8, LANES), f32),
        pars=((z.nk, layer, PARAM_ROWS + 8, LANES), f32),
        pf=((layer, PARAM_ROWS, cp), f32),
        bi=((layer, z.nkg, 8, z.ft), f32),
        msg=((2 * layer, z.stat, LANES), f32),
        stats=((2 * layer, z.nd, z.stat, LANES), f32),
        jf=((layer, 3, cp, cp), bf16),
        mix=((layer, 4, z.rb, z.rb), bf16),
        mixb=((layer, 2, z.rb, 8), f32),
        mixs=((4, 16, 16), f32),
        x=((layer, z.own, z.high + 2, z.tj, cp), f32),
        a=((layer, z.bh, z.tj, cp), f32),
        sz=((layer, z.bh, z.tj, cp), f32),
        mv=((layer, 8, cp), f32),
        u=((z.bh, z.tj, cp), f32),
        cat=((layer, 3, z.own, z.rb, cp), bf16),
        w=((z.bh, z.tj, cp), f32),
        what=((layer, z.bh, z.tj, cp), f32),
        inv=((layer, z.bh, z.tj, LANES), f32),
        yb=((layer, z.bh, z.tj, cp), bf16),
        hs=((layer, z.nkg, z.own, z.rb, z.ft), f32),
        gb=((layer, z.nkg, z.own, z.rb, z.ft), bf16),
        gh=((z.own, z.rb, z.ft), bf16),
        o=((z.bh, z.tj, cp), f32),
        y=((z.bh, z.tj, cp), f32),
        gx=((z.bh, z.tj, cp), f32),
        gob=((z.bh, z.tj, cp), bf16),
        gw=((z.bh, z.tj, cp), f32),
        gsb=((z.bh, z.tj, cp), bf16),
        gpq=((2, z.own, z.rb, cp), bf16),
        gu=((z.bh, z.tj, cp), f32),
        gz=((z.bh, z.tj, cp), f32),
        ga=((z.own, z.high + 2, z.tj, cp), f32),
        sg=((PARAM_ROWS, cp), f32),
        bg=((8, z.nkg * z.ft), f32),
        mg=((16, LANES), f32),
        sgm=((layer, z.nk, 32, LANES), f32),
        sgk=((layer, z.nk, 32, LANES), f32),
        sgz=((layer, 32, LANES), f32),
        sgi=((layer, z.ni, 32, LANES), f32),
    )
    groups = []
    for part in z.parts.values():
        whole_rows = z.ni * part
        groups.append(
            dict(
                wt=((layer, z.nk, whole_rows, cp), bf16),
                gr=((layer, z.nk, whole_rows, cp), bf16),
                r1=((layer, z.chips, z.nk, part, cp), bf16),
                r2=((layer, z.chips - 1, z.nk, part, cp), bf16),
                r3=((layer, z.nk - 1, part, cp), bf16),
                fin=((layer, whole_rows, cp), bf16),
            )
        )
    return shapes, groups


def whole(z, *refs):
    inputs, refs = refs[:17], refs[17:]
    outputs, refs = refs[: 3 + len(z.parts)], refs[3 + len(z.parts) :]
    shapes, groups = scratch_list(z)
    r = SimpleNamespace(**dict(zip(shapes, refs[: len(shapes)], strict=True)))
    (r.images, r.conv_kernel, r.bn_gain, r.bn_bias, r.mix_rows, r.mix_rows_bias, r.mix_cols, r.mix_cols_bias) = inputs[:8]
    (r.join_weight, r.join_bias, r.norm_gain, r.norm_bias, r.weight_in, r.bias_in, r.weight_out, r.bias_out) = inputs[8:16]
    r.cotangent = inputs[16]
    r.out_y, r.out_g, r.out_s = outputs[:3]
    r.outs = dict(zip(z.parts, outputs[3:], strict=True))
    refs = refs[len(shapes) :]
    table = SimpleNamespace(**{name: {} for name in groups[0]})
    for kind, group in zip(z.parts, groups, strict=True):
        for name, ref in zip(group, refs[: len(group)], strict=True):
            getattr(table, name)[kind] = ref
        refs = refs[len(group) :]
    r.wt, r.gr, r.r1, r.r2, r.r3, r.fin = table.wt, table.gr, table.r1, table.r2, table.r3, table.fin
    ssem, rsem, osem = refs
    ni, nk, nd, layers = z.ni, z.nk, z.nd, z.layers
    i = lax.axis_index("img")
    k = lax.axis_index("ch")
    core = lax.rem(i, 2)
    chip = lax.div(i, 2)
    partner = i + 1 - 2 * core
    events = {}
    sends = []
    stores = []

    def at(image_index, channel_index):
        return {"img": image_index, "ch": channel_index}

    def event(name):
        return events.setdefault(name, len(events))

    def send(name, src, dst, device):
        number = event(name)
        pltpu.make_async_remote_copy(
            src_ref=src,
            dst_ref=dst,
            send_sem=ssem.at[number],
            recv_sem=rsem.at[number],
            device_id=device,
            device_id_type=MESH,
        ).start()

    def arrived(name, ref):
        number = event(name)
        sends.append((number, ref))
        pltpu.make_async_remote_copy(
            src_ref=ref,
            dst_ref=ref,
            send_sem=ssem.at[number],
            recv_sem=rsem.at[number],
            device_id=at(partner, k),
            device_id_type=MESH,
        ).wait_recv()

    def store(src, dst):
        copy = pltpu.make_async_copy(src, dst, osem.at[len(stores)])
        stores.append(copy)
        copy.start()

    def loop(count, body, start=0):
        def run(index, carry):
            body(index)
            return carry

        lax.fori_loop(start, count, run, 0)

    barrier = pltpu.get_barrier_semaphore()

    def greet(j):
        pl.semaphore_signal(
            barrier,
            inc=1,
            device_id=at(lax.rem(i + lax.div(j, nk), ni), lax.rem(k + lax.rem(j, nk), nk)),
            device_id_type=MESH,
        )

    loop(nd, greet, 1)

    def exchange_start(slot):
        stats, msg = r.stats, r.msg
        mine = i * nk + k
        stats[slot, mine] = msg[slot]

        def one(j):
            send(
                ("st", slot),
                msg.at[slot],
                stats.at[slot, mine],
                at(lax.rem(i + lax.div(j, nk), ni), lax.rem(k + lax.rem(j, nk), nk)),
            )

        loop(nd, one, 1)

    def exchange_wait(slot):
        arrived(("st", slot), r.stats.at[slot, pl.ds(0, nd - 1)])

    def swap_start(slot):
        for step in range(1, nk):
            other = lax.rem(k + step, nk)
            send(("sw", slot), r.stage.at[slot, other], r.land.at[slot, k], at(i, other))

    def swap_wait(slot):
        arrived(("sw", slot), r.land.at[slot, pl.ds(0, nk - 1)])

    def own_tile(slot):
        r.land[slot, k] = r.stage[slot, k]

    def rps(kind):
        return z.parts[kind]

    def piece(number, size):
        return pl.ds(pl.multiple_of(number * size, 16), size)

    done = set()

    def once(work):
        def run(layer, kind):
            if kind in z.parts and (work, layer, kind) not in done:
                done.add((work, layer, kind))
                work(layer, kind)

        return run

    @once
    def weights_along(layer, kind):
        buffer = r.wt[kind]
        place = piece(i, rps(kind))
        for step in range(1, nk):
            ref = buffer.at[layer, k, place]
            send(("w1", layer, kind), ref, ref, at(i, lax.rem(k + step, nk)))

    @once
    def weights_across(layer, kind):
        buffer = r.wt[kind]
        size = rps(kind)
        arrived(("w1", layer, kind), buffer.at[layer, pl.ds(0, nk - 1), pl.ds(0, size)])
        for step in range(1, nk):
            ref = buffer.at[layer, lax.rem(k + step, nk), piece(i, size)]
            for turn in range(1, z.chips):
                send(("w2", layer, kind), ref, ref, at(2 * lax.rem(chip + turn, z.chips) + core, k))

    @once
    def weights_pair(layer, kind):
        buffer = r.wt[kind]
        size = rps(kind)
        arrived(("w2", layer, kind), buffer.at[layer, pl.ds(0, nk - 1), pl.ds(0, (z.chips - 1) * size)])
        for step in range(1, nk):
            for other in range(z.chips):
                ref = buffer.at[layer, lax.rem(k + step, nk), piece(2 * other + core, size)]
                send(("w3", layer, kind), ref, ref, at(partner, k))

    @once
    def weights_ready(layer, kind):
        size = rps(kind)
        arrived(("w3", layer, kind), r.wt[kind].at[layer, pl.ds(0, nk - 1), pl.ds(0, z.chips * size)])
        if kind == z.join_kind:
            for branch in range(3):
                row = z.join_row + branch * z.clp
                parts = [
                    r.wt[kind][layer, part, row : row + z.cl, :].astype(f32)
                    for part in range(nk)
                ]
                if z.cp > z.channels:
                    parts.append(jnp.zeros((z.cp - z.channels, z.cp), f32))
                r.jf[layer, branch] = jnp.concatenate(parts, axis=0).astype(bf16)

    @once
    def reduce_pair(layer, kind):
        size = rps(kind)
        for other in range(z.chips):
            send(
                ("r1", layer, kind),
                r.gr[kind].at[layer, :, piece(2 * other + 1 - core, size)],
                r.r1[kind].at[layer, other],
                at(partner, k),
            )

    @once
    def reduce_across(layer, kind):
        size = rps(kind)
        arrived(("r1", layer, kind), r.r1[kind].at[layer])
        for other in range(z.chips):
            place = piece(2 * other + core, size)

            def add(part, other=other, place=place):
                r.gr[kind][layer, part, place] = (
                    r.gr[kind][layer, part, place].astype(f32) + r.r1[kind][layer, other, part].astype(f32)
                ).astype(bf16)

            loop(nk, add)
        for turn in range(1, z.chips):
            other = lax.rem(chip + turn, z.chips)
            send(
                ("r2", layer, kind),
                r.gr[kind].at[layer, :, piece(2 * other + core, size)],
                r.r2[kind].at[layer, turn - 1],
                at(2 * other + core, k),
            )

    @once
    def reduce_along(layer, kind):
        arrived(("r2", layer, kind), r.r2[kind].at[layer])
        place = piece(i, rps(kind))

        def add(part):
            total = r.gr[kind][layer, part, place].astype(f32)
            for turn in range(z.chips - 1):
                total = total + r.r2[kind][layer, turn, part].astype(f32)
            r.gr[kind][layer, part, place] = total.astype(bf16)

        loop(nk, add)
        for step in range(1, nk):
            other = lax.rem(k + step, nk)
            send(
                ("r3", layer, kind),
                r.gr[kind].at[layer, other, place],
                r.r3[kind].at[layer, step - 1],
                at(i, other),
            )

    @once
    def spread_across(layer, kind):
        size = rps(kind)
        arrived(("r3", layer, kind), r.r3[kind].at[layer])
        place = piece(i, size)
        total = r.gr[kind][layer, k, place].astype(f32)
        for step in range(nk - 1):
            total = total + r.r3[kind][layer, step].astype(f32)
        r.fin[kind][layer, place] = total.astype(bf16)
        ref = r.fin[kind].at[layer, place]
        for turn in range(1, z.chips):
            send(("r4", layer, kind), ref, ref, at(2 * lax.rem(chip + turn, z.chips) + core, k))

    @once
    def spread_pair(layer, kind):
        size = rps(kind)
        arrived(("r4", layer, kind), r.fin[kind].at[layer, pl.ds(0, (z.chips - 1) * size)])
        for other in range(z.chips):
            ref = r.fin[kind].at[layer, piece(2 * other + core, size)]
            send(("r5", layer, kind), ref, ref, at(partner, k))

    @once
    def spread_ready(layer, kind):
        arrived(("r5", layer, kind), r.fin[kind].at[layer, pl.ds(0, z.chips * rps(kind))])
        store(r.fin[kind].at[layer], r.outs[kind].at[layer])

    def clear(refs):
        for ref in refs:
            if len(ref.shape) > 3:

                def clear_one(index, ref=ref):
                    ref[index] = jnp.zeros(ref.shape[1:], ref.dtype)

                loop(ref.shape[0], clear_one)
            else:
                ref[...] = jnp.zeros(ref.shape, ref.dtype)

    clear([r.tmp, r.xl, r.par])

    tile_row = lax.broadcasted_iota(jnp.int32, (z.tj, LANES), 0)
    inside = tile_row < z.wide

    def take(ref, slot):
        def line(h):
            r.tmp[h, 0 : z.wide * z.group, 0 : z.cl] = ref[h].astype(f32).reshape(z.wide * z.group, z.cl)
            for n in range(z.group):
                r.xl[n, h + 1, 0 : z.wide, :] = r.tmp[h, pl.ds(n, z.wide, stride=z.group), :]

        loop(z.high, line)

        def target(d):
            pack(z, r.stage.at[slot], d, lambda m: r.xl[d * z.own + lax.div(m, z.high), lax.rem(m, z.high) + 1])

        loop(nk, target)

    take(r.images, 0)

    small = [
        (9, r.bn_gain),
        (10, r.bn_bias),
        (11, r.join_bias),
        (12, r.norm_gain),
        (13, r.norm_bias),
        (14, r.bias_out),
    ]
    for row, ref in small:
        values = ref[...].astype(f32)
        for layer in range(layers):
            r.par[layer, row : row + 1, 0 : z.cl] = values[layer : layer + 1]
    values = r.bias_in[...].astype(f32)
    for layer in range(layers):
        for tap in range(3):
            for side in range(3):
                row = 3 * tap + side
                r.par[layer, row : row + 1, 0 : z.cl] = r.conv_kernel[tap, side].astype(f32)[layer : layer + 1]
        for tile in range(z.ftiles):
            stop = min(z.fl, LANES * (tile + 1))
            r.par[layer, PARAM_ROWS + tile : PARAM_ROWS + tile + 1, 0 : stop - LANES * tile] = values[
                layer : layer + 1, LANES * tile : stop
            ]

    def conv(lines, taps):
        count = lines.shape[0] - 2
        shifted = (pltpu.roll(lines, 1, 1), lines, pltpu.roll(lines, z.tj - 1, 1))
        total = None
        for down in range(3):
            for side in range(3):
                term = shifted[side][down : down + count] * taps[3 * down + side]
                total = term if total is None else total + term
        return total

    taps = [r.par[0, t : t + 1, :] for t in range(9)]

    def conv_local(n, carry):
        value = jnp.where(inside, conv(r.xl[n], taps), 0.0)
        r.al[n] = value
        return carry + jnp.sum(value, axis=0)

    local_cells = z.group * z.high * z.wide
    total = lax.fori_loop(0, z.group, conv_local, jnp.zeros((z.tj, LANES), f32))
    local_mean = jnp.sum(total, axis=0, keepdims=True) * (1.0 / local_cells)

    def square_local(n, carry):
        away = jnp.where(inside, r.al[n] - local_mean, 0.0)
        return carry + jnp.sum(away * away, axis=0)

    total = lax.fori_loop(0, z.group, square_local, jnp.zeros((z.tj, LANES), f32))
    local_var = jnp.sum(total, axis=0, keepdims=True) * (1.0 / local_cells)
    r.msg[0] = jnp.concatenate([local_mean, local_var, jnp.zeros((z.stat - 2, LANES), f32)], axis=0)

    blank = jnp.zeros((z.cl, z.cp - z.channels), f32)
    blank_hidden = jnp.zeros((z.fl, z.cp - z.channels), f32)
    for layer in range(layers):
        for kind in z.parts:
            r.wt[kind][layer, k] = jnp.zeros(r.wt[kind].shape[2:], bf16)
        for branch in range(3):
            value = r.join_weight[layer, branch].astype(f32)
            if z.cp > z.channels:
                value = jnp.concatenate([value, blank], axis=1)
            row = z.join_row + branch * z.clp
            r.wt[z.join_kind][layer, k, row : row + z.cl, :] = value.astype(bf16)
        for place, value in (
            (0, r.weight_in[layer].astype(f32).T),
            (z.fl, r.weight_out[layer].astype(f32)),
        ):
            if z.cp > z.channels:
                value = jnp.concatenate([value, blank_hidden], axis=1)
            r.wt["m"][layer, k, place : place + z.fl, :] = value.astype(bf16)

    pl.semaphore_wait(barrier, nd - 1)

    exchange_start(0)
    r.pars[k] = r.par[...]
    for step in range(1, nk):
        send("par", r.par, r.pars.at[k], at(i, lax.rem(k + step, nk)))
    weights_along(0, "j")
    weights_along(0, "m")
    swap_start(0)
    own_tile(0)

    clear([r.x, r.ga, r.pf, r.bi, r.mixs, r.mg, r.sg, r.bg, r.sgm, *r.gr.values()])

    select_row = lax.broadcasted_iota(jnp.int32, (z.rb, 16), 0)
    select_col = lax.broadcasted_iota(jnp.int32, (z.rb, 16), 1)
    pick_high = (lax.div(select_row, z.tj) == select_col).astype(f32)
    pick_wide = (lax.rem(select_row, z.tj) == select_col).astype(f32)
    low_high, low_wide = pick_high.astype(bf16), pick_wide.astype(bf16)
    full_row = lax.broadcasted_iota(jnp.int32, (z.rb, z.rb), 0)
    full_col = lax.broadcasted_iota(jnp.int32, (z.rb, z.rb), 1)
    same_wide = (lax.rem(full_row, z.tj) == lax.rem(full_col, z.tj)) & (lax.rem(full_row, z.tj) < z.wide)
    same_high = lax.div(full_row, z.tj) == lax.div(full_col, z.tj)
    for layer in range(layers):
        for which, (maps, shifts, pick, same, extent) in enumerate(
            (
                (r.mix_rows, r.mix_rows_bias, low_high, same_wide, z.high),
                (r.mix_cols, r.mix_cols_bias, low_wide, same_high, z.wide),
            )
        ):
            r.mixs[which, 0:extent, 0:extent] = maps[:, layer, :].astype(f32)
            table = r.mixs[which].astype(bf16)
            for turned, half in ((0, dot_nn(pick, table)), (1, dot_nt(pick, table))):
                spread = dot_nt(half.astype(bf16), pick)
                r.mix[layer, 2 * which + turned] = jnp.where(same, spread, 0.0).astype(bf16)
            r.mixs[2 + which, 0:1, 0:extent] = shifts[layer : layer + 1, :].astype(f32)
            r.mixb[layer, which] = dot_nt(pick, r.mixs[2 + which, 0:8, :].astype(bf16))

    weights_across(0, "j")
    weights_across(0, "m")

    exchange_wait(0)
    arrived("par", r.pars.at[pl.ds(0, nk - 1)])
    for layer in range(layers):
        tiles = assemble(
            [(r.pars[part, layer, 0:PARAM_ROWS, :], part * z.cl, z.cl) for part in range(nk)], z.ct
        )
        for tile in range(z.ct):
            r.pf[layer, :, LANES * tile : LANES * (tile + 1)] = tiles[tile]
        for block in range(z.nkg):
            pieces = []
            for part in range(z.kg):
                for tile in range(z.ftiles):
                    row = PARAM_ROWS + tile
                    value = r.pars[block * z.kg + part, layer, row : row + 1, :]
                    width = min(LANES, z.fl - LANES * tile)
                    pieces.append((jnp.broadcast_to(value, (8, LANES)), part * z.fl + LANES * tile, width))
            tiles = assemble(pieces, -(-z.ft // LANES))
            for tile, value in enumerate(tiles):
                stop = min(z.ft, LANES * (tile + 1))
                r.bi[layer, block, :, LANES * tile : stop] = value[:, 0 : stop - LANES * tile]

    def param(layer, row):
        return r.pf[layer, row : row + 1, :]

    def wide_row(tiles):
        return jnp.concatenate(tiles, axis=1)

    def combine(means, variances):
        count = means.shape[0]
        mean = jnp.sum(means, axis=0, keepdims=True) * (1.0 / count)
        away = means - mean
        var = jnp.sum(variances + away * away, axis=0, keepdims=True) * (1.0 / count)
        return mean[0], var[0]

    lane_full = lane_index((z.step, z.tj, z.cp))
    column_full = lax.broadcasted_iota(jnp.int32, (z.step, z.tj, z.cp), 1)
    real_lane = lane_full < z.channels
    real_column = column_full < z.wide
    blocks = z.bh // z.step

    def place_of(t):
        return lax.div(t, z.high), lax.rem(t, z.high)

    def store_x(m, tiles):
        for tile in range(z.ct):
            r.x[0, lax.div(m, z.high), lax.rem(m, z.high) + 1, :, LANES * tile : LANES * (tile + 1)] = tiles[tile]

    def store_gx(m, tiles):
        for tile in range(z.ct):
            r.gx[m, :, LANES * tile : LANES * (tile + 1)] = tiles[tile]

    def slices_of(ref, slot):
        for d in range(nk):

            def line(m, d=d):
                return cut([ref[m, :, LANES * t : LANES * (t + 1)] for t in range(z.ct)], d * z.cl, z.cl)

            pack(z, r.stage.at[slot], d, line)

    if layers > 1:
        weights_along(1, "j")
        weights_along(1, "m")
    swap_wait(0)
    unpack(z, r.land.at[0], store_x)

    own_cells = z.own * z.high * z.wide

    for layer in range(layers):

        def conv_part(t, carry, layer=layer):
            b, part = lax.div(t, z.high // z.lines), lax.rem(t, z.high // z.lines)
            start = part * z.lines
            sums = []
            for tile in range(z.ct):
                lanes = slice(LANES * tile, LANES * (tile + 1))
                taps = [r.pf[layer, row : row + 1, lanes] for row in range(9)]
                value = conv(r.x[layer, b, pl.ds(start, z.lines + 2), :, lanes], taps)
                value = jnp.where(inside, value, 0.0)
                r.a[layer, pl.ds(b * z.high + start, z.lines), :, lanes] = value
                sums.append(carry[tile] + jnp.sum(value, axis=0))
            return tuple(sums)

        sums = lax.fori_loop(
            0,
            z.own * (z.high // z.lines),
            conv_part,
            tuple(jnp.zeros((z.tj, LANES), f32) for _ in range(z.ct)),
        )
        if layer == 0:
            stats = r.stats[0].reshape(ni, nk, z.stat, LANES)
            whole_mean, whole_var = [], []
            for part in range(nk):
                mean, var = combine(stats[:, part, 0:1, :], stats[:, part, 1:2, :])
                whole_mean.append((jnp.broadcast_to(mean, (8, LANES)), part * z.cl, z.cl))
                whole_var.append((jnp.broadcast_to(var, (8, LANES)), part * z.cl, z.cl))
            mean = wide_row([tile[0:1] for tile in assemble(whole_mean, z.ct)])
            var = wide_row([tile[0:1] for tile in assemble(whole_var, z.ct)])
        else:
            own_mean = wide_row([jnp.sum(tile, axis=0, keepdims=True) for tile in sums]) * (1.0 / own_cells)

            def square_part(t, carry, layer=layer, own_mean=own_mean):
                value = r.a[layer, pl.ds(t * z.step, z.step)] - own_mean
                value = jnp.where(real_column, value, 0.0)
                return carry + jnp.sum(value * value, axis=0)

            squares = lax.fori_loop(0, blocks, square_part, jnp.zeros((z.tj, z.cp), f32))
            own_var = jnp.sum(squares, axis=0, keepdims=True) * (1.0 / own_cells)
            for tile in range(z.ct):
                lanes = slice(LANES * tile, LANES * (tile + 1))
                r.msg[layer, tile : tile + 1, :] = own_mean[:, lanes]
                r.msg[layer, z.ct + tile : z.ct + tile + 1, :] = own_var[:, lanes]
            exchange_start(layer)
            weights_across(layer, "j")
            weights_across(layer, "m")
            if layer == 1:
                take(r.cotangent, 1)
                swap_start(1)
                own_tile(1)
            exchange_wait(layer)
            stats = r.stats[layer]
            mean, var = combine(stats[:, 0 : z.ct, :], stats[:, z.ct : 2 * z.ct, :])
            mean = wide_row([mean[t : t + 1] for t in range(z.ct)])
            var = wide_row([var[t : t + 1] for t in range(z.ct)])
        inv_std = lax.rsqrt(var + epsilon)
        r.mv[layer, 0:1, :] = mean
        r.mv[layer, 1:2, :] = var
        r.mv[layer, 2:3, :] = inv_std
        scale = inv_std * param(layer, 9)
        shift = param(layer, 10)

        def norm_part(t, layer=layer, mean=mean, scale=scale, shift=shift):
            lines = pl.ds(t * z.step, z.step)
            active, slope = gelu_both((r.a[layer, lines] - mean) * scale + shift)
            r.sz[layer, lines] = slope
            b, start = place_of(t * z.step)
            value = jnp.where(real_column, active, 0.0)
            r.u[lines] = value

        loop(blocks, norm_part)

        def add_part(b, layer=layer):
            value = r.u[pl.ds(b * z.high, z.high)] + r.x[layer, b, 1 : z.high + 1]
            r.u[pl.ds(b * z.high, z.high)] = value
            r.cat[layer, 0, b] = value.reshape(z.rb, z.cp).astype(bf16)

        loop(z.own, add_part)
        weights_pair(layer, z.join_kind)

        def mix_part(b, layer=layer):
            low = r.cat[layer, 0, b]
            for which in range(2):
                value = dot_nn(r.mix[layer, 2 * which], low) + r.mixb[layer, which, :, 0:1]
                r.cat[layer, 1 + which, b] = value.astype(bf16)

        loop(z.own, mix_part)
        weights_ready(layer, z.join_kind)
        weights_pair(layer, "m")
        if 0 < layer < layers - 1:
            weights_along(layer + 1, "j")
            weights_along(layer + 1, "m")

        def join_part(b, layer=layer):
            value = dot_nn(r.cat[layer, 0, b], r.jf[layer, 0])
            value = value + dot_nn(r.cat[layer, 1, b], r.jf[layer, 1])
            value = value + dot_nn(r.cat[layer, 2, b], r.jf[layer, 2])
            r.w[pl.ds(b * z.high, z.high)] = value.reshape(z.high, z.tj, z.cp)

        loop(z.own, join_part)

        def token_part(t, layer=layer):
            lines = pl.ds(t * z.step, z.step)
            value = r.w[lines] + r.u[lines] + param(layer, 11)
            r.w[lines] = value
            mean = jnp.sum(value, axis=2, keepdims=True) * (1.0 / z.channels)
            away = jnp.where(real_lane, value - mean, 0.0)
            var = jnp.sum(away * away, axis=2, keepdims=True) * (1.0 / z.channels)
            inv = lax.rsqrt(var + epsilon)
            what = away * inv
            r.what[layer, lines] = what
            r.inv[layer, lines] = jnp.broadcast_to(inv, (z.step, z.tj, LANES))
            r.yb[layer, lines] = (what * param(layer, 12) + param(layer, 13)).astype(bf16)

        loop(blocks, token_part)
        weights_ready(layer, "m")
        if layer + 1 < layers:
            weights_across(layer + 1, "j")

        def mlp_part(b, layer=layer):
            lines = pl.ds(b * z.high, z.high)
            low = r.yb[layer, lines].reshape(z.rb, z.cp)
            total = None
            for block in range(z.nkg):
                parts = slice(block * z.kg, (block + 1) * z.kg)
                rising = r.wt["m"][layer, parts, 0 : z.fl, :].reshape(z.ft, z.cp)
                hidden = dot_nt(low, rising) + r.bi[layer, block, 0:1, :]
                active, slope = gelu_both(hidden)
                r.hs[layer, block, b] = slope
                active = active.astype(bf16)
                r.gb[layer, block, b] = active
                falling = r.wt["m"][layer, parts, z.fl : 2 * z.fl, :].reshape(z.ft, z.cp)
                term = dot_nn(active, falling)
                total = term if total is None else total + term
            value = total.reshape(z.high, z.tj, z.cp) + r.w[lines] + param(layer, 14)
            value = jnp.where(real_part, value, 0.0)
            if layer + 1 < layers:
                r.x[layer + 1, b, 1 : z.high + 1] = value
            else:
                r.y[lines] = value

        real_part = lax.broadcasted_iota(jnp.int32, (z.high, z.tj, z.cp), 1) < z.wide
        loop(z.own, mlp_part)

    if layers == 1:
        take(r.cotangent, 1)
        swap_start(1)
        own_tile(1)
    swap_wait(1)
    unpack(z, r.land.at[1], store_gx)

    def small_across(layer):
        arrived(("s1", layer), r.sgk.at[layer, pl.ds(0, nk - 1)])
        r.sgz[layer] = jnp.sum(r.sgk[layer], axis=0)
        r.sgi[layer, i] = r.sgz[layer]

        def one(j):
            send(("s2", layer), r.sgz.at[layer], r.sgi.at[layer, i], at(lax.rem(i + j, ni), k))

        loop(ni, one, 1)

    def small_ready(layer):
        arrived(("s2", layer), r.sgi.at[layer, pl.ds(0, ni - 1)])
        r.out_s[layer, 0:32, :] = jnp.sum(r.sgi[layer], axis=0)
        tiles = [r.mv[layer, :, LANES * tile : LANES * (tile + 1)] for tile in range(z.ct)]
        mine = jnp.zeros((8, LANES), f32)
        for part in range(nk):
            mine = mine + jnp.where(k == part, cut(tiles, part * z.cl, z.cl), 0.0)
        r.out_s[layer, 32:40, :] = mine

    for layer in reversed(range(layers)):
        above = layer + 1 if layer + 1 < layers else None

        def start_part(t, carry):
            lines = pl.ds(t * z.step, z.step)
            value = r.gx[lines]
            r.gob[lines] = value.astype(bf16)
            return carry + jnp.sum(value, axis=0)

        total = lax.fori_loop(0, blocks, start_part, jnp.zeros((z.tj, z.cp), f32))
        r.sg[12:13, :] = jnp.sum(total, axis=0, keepdims=True)
        low_out = r.gob[...].reshape(z.rows, z.cp)

        for block in range(z.nkg):
            parts = slice(block * z.kg, (block + 1) * z.kg)
            falling = r.wt["m"][layer, parts, z.fl : 2 * z.fl, :].reshape(z.ft, z.cp)
            rising = r.wt["m"][layer, parts, 0 : z.fl, :].reshape(z.ft, z.cp)

            value = dot_nt(low_out, falling) * r.hs[layer, block].reshape(z.rows, z.ft)
            r.bg[0:1, block * z.ft : (block + 1) * z.ft] = jnp.sum(value, axis=0, keepdims=True)
            low_hidden = value.astype(bf16)
            term = dot_nn(low_hidden, rising).reshape(z.bh, z.tj, z.cp)
            r.o[...] = term if block == 0 else r.o[...] + term
            low_in = r.yb[layer].reshape(z.rows, z.cp)
            value = dot_tn(low_hidden, low_in).astype(bf16).reshape(z.kg, z.fl, z.cp)
            r.gr["m"][layer, parts, 0 : z.fl, :] = value
            low_active = r.gb[layer, block].reshape(z.rows, z.ft)
            value = dot_tn(low_active, low_out).astype(bf16).reshape(z.kg, z.fl, z.cp)
            r.gr["m"][layer, parts, z.fl : 2 * z.fl, :] = value
        if z.join_kind != "m":
            reduce_pair(layer, "m")

        def token_back(t, carry, layer=layer):
            lines = pl.ds(t * z.step, z.step)
            gain_sum, bias_sum, join_sum = carry
            gy, what = r.o[lines], r.what[layer, lines]
            inv = r.inv[layer, lines][:, :, 0:1]
            scaled = gy * param(layer, 12)
            plain = jnp.sum(scaled, axis=2, keepdims=True) * (1.0 / z.channels)
            cross = jnp.sum(scaled * what, axis=2, keepdims=True) * (1.0 / z.channels)
            value = r.gx[lines] + inv * (jnp.where(real_lane, scaled - plain, 0.0) - what * cross)
            r.gw[lines] = value
            r.gsb[lines] = value.astype(bf16)
            return (
                gain_sum + jnp.sum(gy * what, axis=0),
                bias_sum + jnp.sum(gy, axis=0),
                join_sum + jnp.sum(value, axis=0),
            )

        zero = jnp.zeros((z.tj, z.cp), f32)
        gain_sum, bias_sum, join_sum = lax.fori_loop(0, blocks, token_back, (zero, zero, zero))
        r.sg[9:10, :] = jnp.sum(join_sum, axis=0, keepdims=True)
        r.sg[10:11, :] = jnp.sum(gain_sum, axis=0, keepdims=True)
        r.sg[11:12, :] = jnp.sum(bias_sum, axis=0, keepdims=True)

        def mix_back(b, layer=layer):
            lines = pl.ds(b * z.high, z.high)
            low = r.gsb[lines].reshape(z.rb, z.cp)
            total = r.gw[lines].reshape(z.rb, z.cp) + dot_nt(low, r.jf[layer, 0])
            for which in range(2):
                back = dot_nt(low, r.jf[layer, 1 + which]).astype(bf16)
                r.gpq[which, b] = back
                total = total + dot_nn(r.mix[layer, 2 * which + 1], back)
            r.gu[lines] = total.reshape(z.high, z.tj, z.cp)

        loop(z.own, mix_back)

        inv_std = r.mv[layer, 2:3, :]
        mean = r.mv[layer, 0:1, :]

        def gate_back(t, carry, layer=layer, mean=mean, inv_std=inv_std):
            lines = pl.ds(t * z.step, z.step)
            value = r.gu[lines] * r.sz[layer, lines]
            r.gz[lines] = value
            centred = (r.a[layer, lines] - mean) * inv_std
            return carry[0] + jnp.sum(value, axis=0), carry[1] + jnp.sum(value * centred, axis=0)

        first, second = lax.fori_loop(0, blocks, gate_back, (zero, zero))
        first = jnp.sum(first, axis=0, keepdims=True)
        second = jnp.sum(second, axis=0, keepdims=True)
        slot = layers + layer
        for tile in range(z.ct):
            lanes = slice(LANES * tile, LANES * (tile + 1))
            r.msg[slot, tile : tile + 1, :] = first[:, lanes]
            r.msg[slot, z.ct + tile : z.ct + tile + 1, :] = second[:, lanes]
        exchange_start(slot)
        if above is not None:
            reduce_along(above, "m")
            reduce_along(above, "j")
        if z.join_kind != "m":
            reduce_across(layer, "m")
        low_join = r.gsb[...].reshape(z.rows, z.cp)
        for branch in range(3):
            value = dot_tn(r.cat[layer, branch].reshape(z.rows, z.cp), low_join)
            for part in range(nk):
                row = z.join_row + branch * z.clp
                r.gr[z.join_kind][layer, part, row : row + z.cl, :] = value[
                    part * z.cl : (part + 1) * z.cl
                ].astype(bf16)
        reduce_pair(layer, z.join_kind)
        if above is None:
            slices_of(r.y, 2)
            swap_start(2)
            own_tile(2)

        def tables_part(b, carry, layer=layer):
            low = r.cat[layer, 0, b]
            backs = [r.gpq[which, b] for which in range(2)]
            return (
                *(carry[which] + dot_nt(backs[which], low) for which in range(2)),
                *(
                    carry[2 + which] + jnp.sum(backs[which].astype(f32), axis=1, keepdims=True)
                    for which in range(2)
                ),
            )

        square, column = jnp.zeros((z.rb, z.rb), f32), jnp.zeros((z.rb, 1), f32)
        rows_table, cols_table, rows_sum, cols_sum = lax.fori_loop(
            0, z.own, tables_part, (square, square, column, column)
        )
        reduce_across(layer, z.join_kind)
        if above is not None:
            small_across(above)

        rows_table = jnp.where(same_wide, rows_table, 0.0).reshape(z.high, z.tj, z.rb)
        rows_table = jnp.sum(rows_table, axis=1)
        rows_table = lax.dot_general(
            rows_table, pick_high, (((1,), (0,)), ((), ())), preferred_element_type=f32, precision=lax.Precision.HIGHEST
        )
        cols_table = jnp.sum(jnp.where(same_high, cols_table, 0.0).reshape(z.high, z.tj, z.rb), axis=0)
        cols_table = lax.dot_general(
            cols_table, pick_wide, (((1,), (0,)), ((), ())), preferred_element_type=f32, precision=lax.Precision.HIGHEST
        )
        r.mg[0 : z.high, 0:16] = rows_table
        r.mg[:, 16:32] = cols_table
        r.mg[0 : z.high, 32:33] = jnp.sum(rows_sum.reshape(z.high, z.tj, 1), axis=1)
        r.mg[:, 33:34] = jnp.sum(cols_sum.reshape(z.high, z.tj, 1), axis=0)

        exchange_wait(slot)
        stats = jnp.sum(r.stats[slot], axis=0)
        bias_total = wide_row([stats[t : t + 1] for t in range(z.ct)])
        gain_total = wide_row([stats[z.ct + t : z.ct + t + 1] for t in range(z.ct)])
        r.mv[layer, 3:4, :] = gain_total
        r.mv[layer, 4:5, :] = bias_total
        factor = inv_std * param(layer, 9)
        plain = bias_total * (1.0 / z.cells)
        cross = gain_total * (1.0 / z.cells) * inv_std

        def conv_gate(b, layer=layer, mean=mean, factor=factor, plain=plain, cross=cross):
            lines = pl.ds(b * z.high, z.high)
            value = r.gz[lines] - plain - (r.a[layer, lines] - mean) * cross
            r.ga[b, 1 : z.high + 1] = jnp.where(real_part, value * factor, 0.0)

        loop(z.own, conv_gate)

        def conv_back(t, layer=layer):
            b, part = lax.div(t, z.high // z.lines), lax.rem(t, z.high // z.lines)
            start = part * z.lines
            lines = pl.ds(b * z.high + start, z.lines)
            for tile in range(z.ct):
                lanes = slice(LANES * tile, LANES * (tile + 1))
                taps = [r.pf[layer, 8 - row : 9 - row, lanes] for row in range(9)]
                value = conv(r.ga[b, pl.ds(start, z.lines + 2), :, lanes], taps)
                r.gx[lines, :, lanes] = jnp.where(inside, value + r.gu[lines, :, lanes], 0.0)

        loop(z.own * (z.high // z.lines), conv_back)

        if layer == 0:
            slices_of(r.gx, 3)
            swap_start(3)
            own_tile(3)

        for tile in range(z.ct):
            lanes = slice(LANES * tile, LANES * (tile + 1))

            def kernel_part(t, carry, layer=layer, lanes=lanes):
                b, part = lax.div(t, z.high // z.lines), lax.rem(t, z.high // z.lines)
                start = part * z.lines
                lines = r.x[layer, b, pl.ds(start, z.lines + 2), :, lanes]
                upstream = r.ga[b, pl.ds(start + 1, z.lines), :, lanes]
                shifted = (pltpu.roll(lines, 1, 1), lines, pltpu.roll(lines, z.tj - 1, 1))
                return tuple(
                    carry[3 * down + side]
                    + jnp.sum(jnp.sum(shifted[side][down : down + z.lines] * upstream, axis=0), axis=0, keepdims=True)
                    for down in range(3)
                    for side in range(3)
                )

            totals = lax.fori_loop(
                0,
                z.own * (z.high // z.lines),
                kernel_part,
                tuple(jnp.zeros((1, LANES), f32) for _ in range(9)),
            )
            for row in range(9):
                r.sg[row : row + 1, lanes] = totals[row]

        tiles = [r.sg[:, LANES * tile : LANES * (tile + 1)] for tile in range(z.ct)]
        for part in range(nk):
            r.sgm[layer, part, 0:16, :] = cut(tiles, part * z.cl, z.cl)
            for tile in range(z.ftiles):
                start = part * z.fl + LANES * tile
                width = min(LANES, z.fl - LANES * tile)
                hidden = [
                    r.bg[:, LANES * t : min(LANES * (t + 1), nk * z.fl)] for t in range(-(-nk * z.fl // LANES))
                ]
                r.sgm[layer, part, 13 + tile : 14 + tile, :] = cut(hidden, start, width)[0:1]
            r.sgm[layer, part, 16:32, :] = r.mg[...]
        r.sgk[layer, k] = r.sgm[layer, k]
        for step in range(1, nk):
            other = lax.rem(k + step, nk)
            send(("s1", layer), r.sgm.at[layer, other], r.sgk.at[layer, k], at(i, other))

    swap_wait(2)
    deliver(z, r.land.at[2], r.tmp, r.fy)
    store(r.fy, r.out_y)
    for layer in range(1, layers):
        spread_across(layer, "m")
        spread_across(layer, "j")
    reduce_along(0, "m")
    reduce_along(0, "j")
    small_across(0)
    for layer in range(1, layers):
        spread_pair(layer, "m")
        spread_pair(layer, "j")
    swap_wait(3)
    deliver(z, r.land.at[3], r.tmp, r.fg)
    store(r.fg, r.out_g)
    spread_across(0, "m")
    spread_across(0, "j")
    for layer in range(1, layers):
        small_ready(layer)
        spread_ready(layer, "m")
        spread_ready(layer, "j")
    small_ready(0)
    spread_pair(0, "m")
    spread_pair(0, "j")
    spread_ready(0, "m")
    spread_ready(0, "j")

    for copy in stores:
        copy.wait()
    for number, ref in sends:
        pltpu.make_async_remote_copy(
            src_ref=ref,
            dst_ref=ref,
            send_sem=ssem.at[number],
            recv_sem=rsem.at[number],
            device_id=at(partner, k),
            device_id_type=MESH,
        ).wait_send()


EVENTS = 80


def deliver(z, land, tmp, out):
    for k in range(z.nk):

        def group(first, tile, lines, tiles, k=k):
            source = [land[k, tile + t].astype(f32) for t in range(tiles)]
            for j in range(lines):
                m = first + j
                n = k * z.own + lax.div(m, z.high)
                tmp[lax.rem(m, z.high), pl.ds(n, z.wide, stride=z.group), :] = cut(source, j * z.cl, z.cl)[: z.wide]

        line_groups(z, group)

    def line(h, carry):
        out[h] = tmp[h, 0 : z.wide * z.group, 0 : z.cl].reshape(z.wide, z.group, z.cl).astype(out.dtype)
        return carry

    lax.fori_loop(0, z.high, line, 0)


def finish(z, *refs):
    count = 3 + len(z.parts)
    sources, refs = refs[:count], refs[count:]
    sem, copies, refs = refs[-1], refs[1 - count : -1], refs[: 1 - count]
    copies = (refs[2], refs[3], *copies)
    loads = [pltpu.make_async_copy(src, dst, sem.at[n]) for n, (src, dst) in enumerate(zip(sources, copies, strict=True))]
    for load in loads:
        load.start()
    small = copies[2]
    fins = dict(zip(z.parts, copies[3:], strict=True))
    mean_in, var_in = refs[:2]
    (conv_grad, bn_gain, bn_bias, rows_grad, rows_bias, cols_grad, cols_bias, join) = refs[4:12]
    (join_bias, norm_gain, norm_bias, rising, bias_in, falling, bias_out, mean_out, var_out) = refs[12:]
    for load in loads[2:]:
        load.wait()
    for layer in range(z.layers):
        here = slice(layer, layer + 1)

        def row(number, layer=layer):
            return small[layer, number : number + 1, 0 : z.cl]

        for tap in range(9):
            conv_grad[tap // 3, tap % 3, here, :] = row(tap)
        join_bias[here, :] = row(9)
        norm_gain[here, :] = row(10)
        norm_bias[here, :] = row(11)
        bias_out[here, :] = row(12)
        for tile in range(z.ftiles):
            stop = min(z.fl, LANES * (tile + 1))
            bias_in[here, LANES * tile : stop] = small[layer, 13 + tile : 14 + tile, 0 : stop - LANES * tile]
        rows_grad[:, layer, :] = small[layer, 16 : 16 + z.high, 0 : z.high]
        cols_grad[:, layer, :] = small[layer, 16 : 16 + z.wide, 16 : 16 + z.wide]
        turned = small[layer, 16:32, :].T
        rows_bias[here, :] = turned[32:33, 0 : z.high]
        cols_bias[here, :] = turned[33:34, 0 : z.wide]
        mean_out[here, :] = 0.9 * mean_in[here, :] + 0.1 * row(32)
        var_out[here, :] = 0.9 * var_in[here, :] + (0.1 * z.cells / (z.cells - 1.0)) * row(33)
        bn_gain[here, :] = row(35)
        bn_bias[here, :] = row(36)
        fin = fins["m"]
        rising[layer] = fin[layer, 0 : z.fl, 0 : z.channels].astype(f32).T
        falling[layer] = fin[layer, z.fl : 2 * z.fl, 0 : z.channels].astype(f32)
        fin = fins[z.join_kind]
        for branch in range(3):
            start = z.join_row + branch * z.clp
            join[layer, branch] = fin[layer, start : start + z.cl, 0 : z.channels].astype(f32)
    for load in loads[:2]:
        load.wait()


EVENTS = 80


def on_device(ni, nk, *args):
    first, second = (1, 2, 0, 3), (1, 0, 2)
    args = list(args)
    for number, order in ((0, first), (1, first), (18, first), (4, second), (6, second)):
        args[number] = args[number].transpose(order)
    images, conv_kernel, weight_in = args[0], args[1], args[12]
    running_mean, running_var, cotangent = args[16:19]
    z = Sizes(ni, nk, images, conv_kernel, weight_in)
    inputs = (*args[:16], cotangent)
    tokens = (z.high, z.wide, z.group, z.cl)
    out_shape = (
        jax.ShapeDtypeStruct(tokens, bf16),
        jax.ShapeDtypeStruct(tokens, f32),
        jax.ShapeDtypeStruct((z.layers, SMALL_ROWS, LANES), f32),
        *(jax.ShapeDtypeStruct((z.layers, ni * part, z.cp), bf16) for part in z.parts.values()),
    )
    vmem, anywhere = pl.BlockSpec(memory_space=pltpu.VMEM), pl.BlockSpec(memory_space=pl.ANY)
    shapes, groups = scratch_list(z)
    scratch = [pltpu.VMEM(shape, kind) for table in (shapes, *groups) for shape, kind in table.values()]
    scratch += [pltpu.SemaphoreType.DMA((EVENTS,)), pltpu.SemaphoreType.DMA((EVENTS,)), pltpu.SemaphoreType.DMA((16,))]
    moved = pl.pallas_call(
        functools.partial(whole, z),
        out_shape=out_shape,
        in_specs=[vmem] * len(inputs),
        out_specs=tuple(vmem if number == 2 else anywhere for number in range(len(out_shape))),
        scratch_shapes=scratch,
        compiler_params=pltpu.CompilerParams(
            collective_id=0, has_side_effects=True, vmem_limit_bytes=62 * 2**20
        ),
    )(*inputs)
    lead = z.layers
    sizes = [
        (tokens, bf16),
        (tokens, f32),
        ((3, 3, lead, z.cl), f32),
        ((lead, z.cl), f32),
        ((lead, z.cl), f32),
        ((z.high, lead, z.high), f32),
        ((lead, z.high), f32),
        ((z.wide, lead, z.wide), f32),
        ((lead, z.wide), f32),
        ((lead, 3, z.cl, z.channels), f32),
        ((lead, z.cl), f32),
        ((lead, z.cl), f32),
        ((lead, z.cl), f32),
        ((lead, z.channels, z.fl), f32),
        ((lead, z.fl), f32),
        ((lead, z.fl, z.channels), f32),
        ((lead, z.cl), f32),
        ((lead, z.cl), f32),
        ((lead, z.cl), f32),
    ]
    results = pl.pallas_call(
        functools.partial(finish, z),
        out_shape=tuple(jax.ShapeDtypeStruct(*size) for size in sizes),
        in_specs=[anywhere] * len(moved) + [vmem] * 2,
        out_specs=(vmem,) * len(sizes),
        scratch_shapes=[
            *(pltpu.VMEM(item.shape, item.dtype) for item in moved[2:]),
            pltpu.SemaphoreType.DMA((len(moved),)),
        ],
        compiler_params=pltpu.CompilerParams(vmem_limit_bytes=62 * 2**20),
    )(*moved, running_mean, running_var)
    results = list(results)
    for number, order in ((0, (2, 0, 1, 3)), (1, (2, 0, 1, 3)), (2, (2, 0, 1, 3)), (5, second), (7, second)):
        results[number] = results[number].transpose(order)
    return tuple(results)


def solution(mesh):
    return jax.shard_map(
        functools.partial(on_device, mesh.shape["img"], mesh.shape["ch"]),
        mesh=mesh,
        in_specs=(
            P("img", None, None, "ch"),
            P(None, None, None, "ch"),
            P(None, "ch"),
            P(None, "ch"),
            P(),
            P(),
            P(),
            P(),
            P(None, None, "ch", None),
            P(None, "ch"),
            P(None, "ch"),
            P(None, "ch"),
            P(None, None, "ch"),
            P(None, "ch"),
            P(None, "ch", None),
            P(None, "ch"),
            P(None, "ch"),
            P(None, "ch"),
            P("img", None, None, "ch"),
        ),
        out_specs=(
            P("img", None, None, "ch"),
            P("img", None, None, "ch"),
            P(None, None, None, "ch"),
            P(None, "ch"),
            P(None, "ch"),
            P(),
            P(),
            P(),
            P(),
            P(None, None, "ch", None),
            P(None, "ch"),
            P(None, "ch"),
            P(None, "ch"),
            P(None, None, "ch"),
            P(None, "ch"),
            P(None, "ch", None),
            P(None, "ch"),
            P(None, "ch"),
            P(None, "ch"),
        ),
        check_vma=False,
    )
```
